32 devices in a mesh: wide: 16 (over z, y, core), narrow: 2 (over x).
Axes of the slice: x: 2, y: 2, z: 4, core: 2. Of those that a mesh axis runs over, the one named last changes fastest.
Arguments:
- inputs: bfloat16 [2, 32, 768, 512], P(None, ('wide', 'narrow')), may hold values from -6 to 6
- memory: bfloat16 [2, 32, 96, 512], P(None, ('wide', 'narrow')), may hold values from -6 to 6
- tau_scale: float32 [2, 32], P(None, ('wide', 'narrow')), may hold values from 0.5 to 2
- delta_shift: float32 [2, 32, 96], P(None, ('wide', 'narrow')), may hold values from -32 to 32
- horizon: int32 [2, 32], P(None, ('wide', 'narrow')), may hold values from 96 to 720, as said below
- self_params: bfloat16 [1052672], P(('wide', 'narrow')), may hold values from -2 to 2
- cross_params: bfloat16 [1052672], P(('wide', 'narrow')), may hold values from -2 to 2
- dense_params: bfloat16 [2101248], P(('wide', 'narrow')), may hold values from -2 to 2
- cotangent: bfloat16 [2, 32, 768, 512], P(None, ('wide', 'narrow')), may hold values from -6 to 6
Outputs:
- output: bfloat16 [2, 32, 768, 512], P(None, ('wide', 'narrow'))
- grad_input: float32 [2, 32, 768, 512], P(None, ('wide', 'narrow'))
- grad_memory: float32 [2, 32, 96, 512], P(None, ('wide', 'narrow'))
- grad_self: float32 [1052672], P(('wide', 'narrow'))
- grad_cross: float32 [1052672], P(('wide', 'narrow'))
- grad_dense: float32 [2101248], P(('wide', 'narrow'))
The draws below stay inside these ranges and needn't reach their ends.
Inputs may be any that keep to these rules, and one draw needn't show every extreme that they name: `horizon`: each entry is one of 96, 192, 336 or 720; the first item of the first micro-batch has 720.
All inputs are finite; a program needn't handle non-finite values.
Results may differ from the reference program's by a relative error of at most 0.025.
The reference program's roundings to bfloat16 on the way count: a program that leaves them out, or rounds other values in their place, can miss the bound.
Values may be sent and summed in bfloat16 or wider, within the bound.
No kernel may reach another device: no remote copies, remote signals or barrier semaphores. Data moves between devices by JAX's collectives and lax.ppermute only.
A program may use at most 192 MiB of HBM per device.

```python
import math
import jax
import jax.numpy as jnp
from jax import lax

D = 512
FF = 2048
HEADS = 8
HSTEP = 24
LABEL = 48
MEM = 96
SEQ = 768
MICRO = 2
ITEMS = 32
P_SELF = 1052672
P_CROSS = 1052672
P_DENSE = 2101248


def attention_draw(key, out_scale, length):
    first_key, second_key = jax.random.split(key)
    base = jax.random.truncated_normal(first_key, -4.0, 4.0, (length,), jnp.float32)
    unit = jax.random.uniform(second_key, (length,), jnp.float32, -1.0, 1.0)
    place = jnp.arange(length)
    square = D * D
    values = jnp.where(place < 3 * square, base * D ** (-0.5), base * 0.3)
    values = jnp.where((place >= 3 * square) & (place < 4 * square), base * (out_scale * D ** (-0.5)), values)
    gain_start = 4 * square + 3 * D
    values = jnp.where((place >= gain_start) & (place < gain_start + D), 1.0 + 0.15 * unit, values)
    return values.astype(jnp.bfloat16)


def draw_self_params(key, part):
    key = jax.random.fold_in(key, 11)
    return attention_draw(key, 4.0, P_SELF)


def draw_cross_params(key, part):
    key = jax.random.fold_in(key, 23)
    return attention_draw(key, 3.0, P_CROSS)


def draw_dense_params(key, part):
    key = jax.random.fold_in(key, 37)
    first_key, second_key = jax.random.split(key)
    base = jax.random.truncated_normal(first_key, -4.0, 4.0, (P_DENSE,), jnp.float32)
    unit = jax.random.uniform(second_key, (P_DENSE,), jnp.float32, -1.0, 1.0)
    place = jnp.arange(P_DENSE)
    matrix = D * FF
    values = jnp.where(place < matrix, base * D ** (-0.5), base * 0.3)
    values = jnp.where((place >= matrix) & (place < 2 * matrix), base * (1.5 * FF ** (-0.5)), values)
    gain_start = 2 * matrix + FF + D
    values = jnp.where((place >= gain_start) & (place < gain_start + D), 1.0 + 0.15 * unit, values)
    return values.astype(jnp.bfloat16)


def draw_horizon(key, part):
    key = jax.random.fold_in(key, 5)
    picks = jax.random.randint(key, (MICRO, ITEMS), 0, 4)
    table = jnp.array([4, 8, 14, 30], jnp.int32) * HSTEP
    chosen = table[picks]
    return chosen.at[0, 0].set(30 * HSTEP)


def block_scale(key, shape, cuts, least, high):
    loudness = 1.0
    for axis_at, parts in cuts:
        heights = jax.random.uniform(jax.random.fold_in(jax.random.fold_in(key, 6), axis_at), (parts,), jnp.float32, least / len(cuts), high / len(cuts))
        loudness = loudness * jnp.repeat(jnp.exp(heights), shape[axis_at] // parts).reshape((-1,) + (1,) * (len(shape) - 1 - axis_at))
    return loudness


def centred(rng, shape, scale, limit, cuts=(), kind=jnp.bfloat16):
    values = jax.random.normal(rng, shape, jnp.float32) * scale
    if len(cuts) > 0:
        values = block_scale(rng, shape, cuts, -0.22, 0.18) * values
    return jnp.clip(values, min=-limit, max=limit).astype(kind)


def setup_inputs(seed: int = 0) -> dict:
    key_list = jax.random.split(jax.random.key(seed), 10)
    return {
        "inputs": centred(key_list[0], (MICRO, ITEMS, SEQ, D), 1.0, 6.0, ((1, 32),)),
        "memory": centred(key_list[1], (MICRO, ITEMS, MEM, D), 1.0, 6.0, ((1, 32),)),
        "tau_scale": jnp.clip(jnp.exp(math.log(2.0) - 1.3862944 * jax.random.uniform(key_list[2], (MICRO, ITEMS), jnp.float32) ** block_scale(key_list[2], (MICRO, ITEMS), ((1, 32),), -0.2, 0.2)), 0.5, 2.0),
        "delta_shift": centred(key_list[3], (MICRO, ITEMS, MEM), 8.0, 32.0, ((1, 32),), jnp.float32),
        "horizon": draw_horizon(jax.random.fold_in(key_list[9], 71), 0),
        "self_params": draw_self_params(jax.random.fold_in(key_list[9], 71), 0),
        "cross_params": draw_cross_params(jax.random.fold_in(key_list[9], 71), 0),
        "dense_params": draw_dense_params(jax.random.fold_in(key_list[9], 71), 0),
        "cotangent": centred(key_list[8], (MICRO, ITEMS, SEQ, D), 1.0, 6.0, ((1, 32),)),
    }


@jax.custom_vjp
def low(v):
    return lax.optimization_barrier(v.astype(jnp.bfloat16)).astype(jnp.float32)

@jax.custom_vjp
def low_back(v):
    return v

def low_keep(v):
    return (low(v), None)

def low_pass(kept, grad):
    return (grad,)

def back_keep(v):
    return (v, None)

def back_low(kept, grad):
    return (low(grad),)
low.defvjp(low_keep, low_pass)
low_back.defvjp(back_keep, back_low)
eps_norm = 1e-05
negative = -1e+30
per_group = 4
highest = lax.Precision.HIGHEST

def split_attention(flat_params):
    square = D * D
    matrices = [flat_params[member * square:(member + 1) * square].reshape(D, D) for member in range(4)]
    offset = 4 * square
    vectors = [flat_params[offset + member * D:offset + (member + 1) * D] for member in range(5)]
    return matrices + vectors

def split_dense(flat_params):
    offset = D * FF
    weight_in = flat_params[:offset].reshape(D, FF)
    weight_out = flat_params[offset:2 * offset].reshape(FF, D)
    cursor = 2 * offset
    bias_in = flat_params[cursor:cursor + FF]
    cursor = cursor + FF
    vectors = [flat_params[cursor + member * D:cursor + (member + 1) * D] for member in range(3)]
    return [weight_in, weight_out, bias_in] + vectors

def project(source, weight):
    return jnp.einsum('gsd,df->gsf', source, weight, precision=highest)

def layer_norm(hidden, gain, shift):
    center = hidden - lax.optimization_barrier(jnp.mean(hidden, -1, keepdims=True))
    spread = lax.optimization_barrier(jnp.mean(center * center, -1, keepdims=True))
    return center * lax.rsqrt(spread + eps_norm) * gain + shift

def smooth_gate(values):
    return 0.5 * values * (1.0 + lax.erf(values * 0.7071067811865476))

def attend(query_rows, key_rows, value_rows, tau_item, key_shift, causal):
    group_count, query_count, width = query_rows.shape
    key_count = key_rows.shape[1]
    head_width = width // HEADS
    query_split = query_rows.reshape(group_count, query_count, HEADS, head_width)
    key_split = key_rows.reshape(group_count, key_count, HEADS, head_width)
    value_split = value_rows.reshape(group_count, key_count, HEADS, head_width)
    raw_scores = low_back(jnp.einsum('gshe,gmhe->ghsm', query_split, key_split, precision=highest))
    scores = raw_scores * tau_item[:, None, None, None]
    if key_shift is not None:
        scores = scores + key_shift[:, None, None, :]
    scores = scores / math.sqrt(head_width)
    if causal:
        row_place = lax.broadcasted_iota(jnp.int32, scores.shape, 2)
        col_place = lax.broadcasted_iota(jnp.int32, scores.shape, 3)
        scores = jnp.where(row_place >= col_place, scores, negative)
    row_max = lax.optimization_barrier(jnp.max(scores, -1, keepdims=True))
    exps = jnp.exp(scores - row_max)
    attention_weights = exps / lax.optimization_barrier(jnp.sum(exps, -1, keepdims=True))
    mixed = jnp.einsum('ghsm,gmhe->gshe', low(attention_weights), value_split, precision=highest)
    return low(low_back(mixed.reshape(group_count, query_count, width)))

def forward(self_flat, cross_flat, dense_flat, source, memory_rows, tau_item, shift_item, horizon_item):
    self_q, self_k, self_v, self_o, self_bq, self_bv, self_bo, gain_one, shift_one = split_attention(self_flat)
    cross_q, cross_k, cross_v, cross_o, cross_bq, cross_bv, cross_bo, gain_two, shift_two = split_attention(cross_flat)
    dense_in, dense_out, bias_in, bias_out, gain_three, shift_three = split_dense(dense_flat)
    query_one = low(low_back(project(source, self_q)) + self_bq)
    key_one = low(low_back(project(source, self_k)))
    value_one = low(low_back(project(source, self_v)) + self_bv)
    mixed_one = attend(query_one, key_one, value_one, tau_item, None, True)
    first = layer_norm(source + low_back(project(mixed_one, self_o)) + self_bo, gain_one, shift_one)
    query_two = low(low_back(project(low(first), cross_q)) + cross_bq)
    key_two = low(low_back(project(memory_rows, cross_k)))
    value_two = low(low_back(project(memory_rows, cross_v)) + cross_bv)
    mixed_two = attend(query_two, key_two, value_two, tau_item, shift_item, False)
    second = layer_norm(first + low_back(project(mixed_two, cross_o)) + cross_bo, gain_two, shift_two)
    pre_gate = low_back(project(low(second), dense_in)) + bias_in
    gated = low(smooth_gate(pre_gate))
    third = layer_norm(second + low_back(project(gated, dense_out)) + bias_out, gain_three, shift_three)
    valid_rows = (lax.broadcasted_iota(jnp.int32, third.shape[:2], 1) < LABEL + horizon_item[:, None]).astype(third.dtype)
    return third * valid_rows[..., None]

def reference(inputs, memory, tau_scale, delta_shift, horizon, self_params, cross_params, dense_params, cotangent):
    flat_params = (self_params.astype(jnp.float32), cross_params.astype(jnp.float32), dense_params.astype(jnp.float32))
    item_total = inputs.shape[0] * inputs.shape[1]

    def regroup(array):
        return array.reshape((item_total // per_group, per_group) + array.shape[2:])
    series = (regroup(inputs.astype(jnp.float32)), regroup(memory.astype(jnp.float32)), regroup(tau_scale), regroup(delta_shift), regroup(horizon), regroup(cotangent.astype(jnp.float32)))

    def group_step(running, piece):
        source, memory_rows, tau_item, shift_item, horizon_item, cotangent_rows = piece

        def layer(self_flat, cross_flat, dense_flat, rows_in, memory_in):
            return forward(self_flat, cross_flat, dense_flat, rows_in, memory_in, tau_item, shift_item, horizon_item)
        result, pullback = jax.vjp(layer, flat_params[0], flat_params[1], flat_params[2], source, memory_rows)
        gradients = pullback(cotangent_rows)
        running = (running[0] + gradients[0], running[1] + gradients[1], running[2] + gradients[2])
        return (running, (result.astype(jnp.bfloat16), gradients[3], gradients[4]))
    starting = tuple((jnp.zeros_like(flat) for flat in flat_params))
    totals, (output, grad_input, grad_memory) = lax.scan(group_step, starting, series)
    return (output.reshape(inputs.shape), grad_input.reshape(inputs.shape), grad_memory.reshape(memory.shape), totals[0], totals[1], totals[2])
```

```python
import functools
import math

import jax
import jax.numpy as jnp
from jax import lax
from jax.experimental import pallas as pl
from jax.experimental.pallas import tpu as pltpu
from jax.sharding import PartitionSpec as P

D = 512
FF = 2048
HEADS = 8
HW = D // HEADS
LABEL = 48
LANES = 128
CH = 256
EPS = 1e-05
NEG = -1e30
LOG2E = 1.4426950408889634
f32, bf16 = jnp.float32, jnp.bfloat16
VMEM_LIMIT = 60 * 2**20


def dot(a, b):
    return jnp.dot(a, b, preferred_element_type=f32)


def dot_nt(a, b):
    return lax.dot_general(a, b, (((1,), (1,)), ((), ())), preferred_element_type=f32)


def norm_stats(h):
    center = h - jnp.mean(h, -1, keepdims=True)
    rstd = lax.rsqrt(jnp.mean(center * center, -1, keepdims=True) + EPS)
    return center * rstd, rstd


def norm_back(dz, n, rstd, gain):
    dn = dz * gain
    return rstd * (dn - jnp.mean(dn, -1, keepdims=True) - n * jnp.mean(dn * n, -1, keepdims=True))


def col_sum(v):
    return jnp.sum(v, 0, keepdims=True)


def load_flat(order, near_ref, far_ref, flat, real):
    half = near_ref.shape[0]

    @pl.loop(0, half)
    def _(k):
        flat[pl.ds(order[k] * real, real), :] = near_ref[k, :real, :].astype(f32)
        flat[pl.ds(order[half + k] * real, real), :] = far_ref[k, :real, :].astype(f32)


def store_flat(order, near_ref, far_ref, flat, real):
    half, rows = near_ref.shape[:2]

    @pl.loop(0, half)
    def _(k):
        near_ref[k] = flat[pl.ds(order[k] * real, rows), :].astype(bf16)
        far_ref[k] = flat[pl.ds(order[half + k] * real, rows), :].astype(bf16)


def take_matrix(flat, start, height, width, put):
    per = width // LANES
    for j in range(per):
        put(j, flat[pl.ds(start + j, height, stride=per), :])


def take_vector(flat, start, width):
    return jnp.concatenate([flat[start + j : start + j + 1, :] for j in range(width // LANES)], 1)


def put_matrix(flat, start, height, width, get):
    per = width // LANES
    for j in range(per):
        flat[pl.ds(start + j, height, stride=per), :] = get(j)


def put_vector(flat, start, row):
    for j in range(row.shape[1] // LANES):
        flat[start + j : start + j + 1, :] = row[:, j * LANES : (j + 1) * LANES]


MAT_ROWS = D * D // LANES


def load_attention(order, near_ref, far_ref, flat, real, w_ref, vec_ref):
    load_flat(order, near_ref, far_ref, flat, real)
    for m in range(4):

        def put(j, block, m=m):
            w_ref[:, m * D + j * LANES : m * D + (j + 1) * LANES] = block.astype(bf16)

        take_matrix(flat, m * MAT_ROWS, D, D, put)
    for i in range(5):
        vec_ref[i : i + 1, :] = take_vector(flat, 4 * MAT_ROWS + i * (D // LANES), D)


def store_attention(order, near_ref, far_ref, flat, real, acc, vec_ref):
    for m in range(4):
        put_matrix(
            flat, m * MAT_ROWS, D, D, lambda j, m=m: acc[:, m * D + j * LANES : m * D + (j + 1) * LANES]
        )
    flat[4 * MAT_ROWS :, :] = jnp.zeros((flat.shape[0] - 4 * MAT_ROWS, LANES), f32)
    for i in range(5):
        put_vector(flat, 4 * MAT_ROWS + i * (D // LANES), vec_ref[i : i + 1, :])
    store_flat(order, near_ref, far_ref, flat, real)


def head_rhs(rows_t, head):
    block = rows_t[head * HW : (head + 1) * HW, :]
    zero = jnp.zeros_like(block)
    return jnp.concatenate([block, zero] if head % 2 == 0 else [zero, block], 0)


def pair_masks(shape, dtype):
    lane = lax.broadcasted_iota(jnp.int32, shape, 1)
    low = lane < HW
    return low.astype(f32).astype(dtype), jnp.logical_not(low).astype(f32).astype(dtype)


def causal_cut(scores, fill):
    keys = scores.shape[0]
    tail = scores[keys - CH :, :]
    key_at = lax.broadcasted_iota(jnp.int32, tail.shape, 0)
    query_at = lax.broadcasted_iota(jnp.int32, tail.shape, 1)
    tail = jnp.where(key_at <= query_at, tail, fill)
    if keys == CH:
        return tail
    return jnp.concatenate([scores[: keys - CH, :], tail], 0)


def self_forward_kernel(
    nch, order, tau, x_ref, pn_ref, pf_ref, q_o, qt_o, k_o, kt_o, v_o, at_o, h_o, lse_o, w_o, vec_o,
    flat, w, vec, ksc, vtsc, at, qt, *, real, chunks,
):
    item, chunk = pl.program_id(0), pl.program_id(1)

    @pl.when((item == 0) & (chunk == 0))
    def _():
        load_attention(order, pn_ref, pf_ref, flat, real, w, vec)
        w_o[...] = w[...]
        vec_o[...] = vec[...]

    @pl.when(chunk < nch[item])
    def _():
        scale = tau[item] * (LOG2E / math.sqrt(HW))
        x = x_ref[0]
        qkv = dot(x, w[:, : 3 * D])
        q = (qkv[:, :D] + vec[0:1, :]).astype(bf16)
        k = qkv[:, D : 2 * D].astype(bf16)
        v = (qkv[:, 2 * D :] + vec[1:2, :]).astype(bf16)
        q_o[0] = q
        k_o[0] = k
        v_o[0] = v
        qt[...] = q.T
        qt_o[0] = qt[...]
        kt_o[0] = k.T
        ksc[pl.ds(pl.multiple_of(chunk * CH, CH), CH), :] = k
        vtsc[:, pl.ds(pl.multiple_of(chunk * CH, CH), CH)] = v.T
        for at_chunk in range(chunks):

            @pl.when(chunk == at_chunk)
            def _(keys=(at_chunk + 1) * CH):
                for head in range(HEADS):
                    pair = head // 2
                    raw = dot(ksc[:keys, pair * LANES : (pair + 1) * LANES], head_rhs(qt, head))
                    s = causal_cut(raw * scale, NEG)
                    top = jnp.max(s, 0, keepdims=True)
                    e = jnp.exp2(s - top)
                    total = jnp.sum(e, 0, keepdims=True)
                    mixed = dot(vtsc[head * HW : (head + 1) * HW, :keys], e.astype(bf16))
                    at[head * HW : (head + 1) * HW, :] = (mixed * (1.0 / total)).astype(bf16)
                    lse_o[0, head : head + 1, :] = top + jnp.log2(total)

        at_o[0] = at[...]
        a = at[...].T
        h_o[0] = x.astype(f32) + dot(a, w[:, 3 * D :]) + vec[2:3, :]


def self_forward(nch, order, tau, x, params, real):
    items, steps, _ = x.shape
    chunks = steps // CH
    half, rows, _ = params[0].shape

    def row_block(i, c, nch_ref, _):
        return (i, jnp.minimum(c, nch_ref[i] - 1), 0)

    def col_block(i, c, nch_ref, _):
        return (i, 0, jnp.minimum(c, nch_ref[i] - 1))

    rowspec = pl.BlockSpec((1, CH, D), row_block)
    colspec = pl.BlockSpec((1, D, CH), col_block)
    whole2 = lambda i, c, *_: (0, 0)
    shards = pl.BlockSpec((half, rows, LANES), lambda i, c, *_: (0, 0, 0), pipeline_mode=pl.Buffered(1))
    shape = jax.ShapeDtypeStruct
    return pl.pallas_call(
        functools.partial(self_forward_kernel, real=real, chunks=chunks),
        grid_spec=pltpu.PrefetchScalarGridSpec(
            num_scalar_prefetch=2,
            grid=(items, chunks),
            in_specs=[
                pl.BlockSpec(memory_space=pltpu.SMEM),
                rowspec,
                shards, shards,
            ],
            out_specs=[
                rowspec, colspec, rowspec, colspec, rowspec, colspec, rowspec,
                pl.BlockSpec((1, HEADS, CH), col_block),
                pl.BlockSpec((D, 4 * D), whole2, pipeline_mode=pl.Buffered(1)),
                pl.BlockSpec((8, D), whole2, pipeline_mode=pl.Buffered(1)),
            ],
            scratch_shapes=[
                pltpu.VMEM((2 * half * real + 16, LANES), f32),
                pltpu.VMEM((D, 4 * D), bf16),
                pltpu.VMEM((8, D), f32),
                pltpu.VMEM((steps, D), bf16),
                pltpu.VMEM((D, steps), bf16),
                pltpu.VMEM((D, CH), bf16),
                pltpu.VMEM((D, CH), bf16),
            ],
        ),
        out_shape=[
            shape((items, steps, D), bf16), shape((items, D, steps), bf16),
            shape((items, steps, D), bf16), shape((items, D, steps), bf16),
            shape((items, steps, D), bf16), shape((items, D, steps), bf16),
            shape((items, steps, D), f32), shape((items, HEADS, steps), f32),
            shape((D, 4 * D), bf16), shape((8, D), f32),
        ],
        compiler_params=pltpu.CompilerParams(vmem_limit_bytes=VMEM_LIMIT),
        cost_estimate=pl.CostEstimate(flops=int(8e9), bytes_accessed=int(2e7), transcendentals=0),
        name="self_forward",
    )(nch, order, tau, x, *params)


def cross_forward_kernel(
    nch, order, tau, h_ref, m_ref, shift_ref, pn_ref, pf_ref, vec1_ref, q_o, qt_o, k_o, kt_o, v_o, at_o, h_o, lse_o, w_o, vec_o,
    flat, w, vec, vtsc, at, qt, *, real, mem,
):
    item, chunk = pl.program_id(0), pl.program_id(1)

    @pl.when((item == 0) & (chunk == 0))
    def _():
        load_attention(order, pn_ref, pf_ref, flat, real, w, vec)
        w_o[...] = w[...]
        vec_o[...] = vec[...]

    @pl.when(chunk == 0)
    def _():
        kv = dot(m_ref[0], w[:, D : 3 * D])
        k = kv[:, :D].astype(bf16)
        v = (kv[:, D:] + vec[1:2, :]).astype(bf16)
        k_o[0] = k
        kt_o[0] = k.T
        v_o[0] = v
        vtsc[...] = v.T

    @pl.when(chunk < nch[item])
    def _():
        scale = tau[item] * (LOG2E / math.sqrt(HW))
        shift = shift_ref[0] * (LOG2E / math.sqrt(HW))
        n1, _ = norm_stats(h_ref[0])
        x1 = n1 * vec1_ref[3:4, :] + vec1_ref[4:5, :]
        q = (dot(x1.astype(bf16), w[:, :D]) + vec[0:1, :]).astype(bf16)
        q_o[0] = q
        qt[...] = q.T
        qt_o[0] = qt[...]
        for head in range(HEADS):
            pair = head // 2
            raw = dot(k_o[0, :, pair * LANES : (pair + 1) * LANES], head_rhs(qt, head))
            s = raw * scale + shift
            top = jnp.max(s, 0, keepdims=True)
            e = jnp.exp2(s - top)
            total = jnp.sum(e, 0, keepdims=True)
            mixed = dot(vtsc[head * HW : (head + 1) * HW, :], e.astype(bf16))
            at[head * HW : (head + 1) * HW, :] = (mixed * (1.0 / total)).astype(bf16)
            lse_o[0, head : head + 1, :] = top + jnp.log2(total)
        at_o[0] = at[...]
        a = at[...].T
        h_o[0] = x1 + dot(a, w[:, 3 * D :]) + vec[2:3, :]


def cross_forward(nch, order, tau, h1, memory, shift, params, vec1, real):
    items, steps, _ = h1.shape
    mem = memory.shape[1]
    chunks = steps // CH
    half, rows, _ = params[0].shape

    def row_block(i, c, nch_ref, _):
        return (i, jnp.minimum(c, nch_ref[i] - 1), 0)

    def col_block(i, c, nch_ref, _):
        return (i, 0, jnp.minimum(c, nch_ref[i] - 1))

    per_item = lambda i, c, *_: (i, 0, 0)
    rowspec = pl.BlockSpec((1, CH, D), row_block)
    colspec = pl.BlockSpec((1, D, CH), col_block)
    memspec = pl.BlockSpec((1, mem, D), per_item)
    whole2 = lambda i, c, *_: (0, 0)
    shards = pl.BlockSpec((half, rows, LANES), lambda i, c, *_: (0, 0, 0), pipeline_mode=pl.Buffered(1))
    shape = jax.ShapeDtypeStruct
    return pl.pallas_call(
        functools.partial(cross_forward_kernel, real=real, mem=mem),
        grid_spec=pltpu.PrefetchScalarGridSpec(
            num_scalar_prefetch=2,
            grid=(items, chunks),
            in_specs=[
                pl.BlockSpec(memory_space=pltpu.SMEM),
                rowspec,
                memspec,
                pl.BlockSpec((1, mem, 1), per_item),
                shards, shards,
                pl.BlockSpec((8, D), whole2, pipeline_mode=pl.Buffered(1)),
            ],
            out_specs=[
                rowspec, colspec, memspec,
                pl.BlockSpec((1, D, mem), per_item),
                memspec, colspec, rowspec,
                pl.BlockSpec((1, HEADS, CH), col_block),
                pl.BlockSpec((D, 4 * D), whole2, pipeline_mode=pl.Buffered(1)),
                pl.BlockSpec((8, D), whole2, pipeline_mode=pl.Buffered(1)),
            ],
            scratch_shapes=[
                pltpu.VMEM((2 * half * real + 16, LANES), f32),
                pltpu.VMEM((D, 4 * D), bf16),
                pltpu.VMEM((8, D), f32),
                pltpu.VMEM((D, mem), bf16),
                pltpu.VMEM((D, CH), bf16),
                pltpu.VMEM((D, CH), bf16),
            ],
        ),
        out_shape=[
            shape((items, steps, D), bf16), shape((items, D, steps), bf16),
            shape((items, mem, D), bf16), shape((items, D, mem), bf16),
            shape((items, mem, D), bf16), shape((items, D, steps), bf16),
            shape((items, steps, D), f32), shape((items, HEADS, steps), f32),
            shape((D, 4 * D), bf16), shape((8, D), f32),
        ],
        compiler_params=pltpu.CompilerParams(vmem_limit_bytes=VMEM_LIMIT),
        cost_estimate=pl.CostEstimate(flops=int(4e9), bytes_accessed=int(2e7), transcendentals=0),
        name="cross_forward",
    )(nch, order, tau, h1, memory, shift, *params, vec1)


def dense_kernel(
    nch, order, horizon, h_ref, ct_ref, pn_ref, pf_ref, vec2_ref, y_o, dh2_o, gn_o, gf_o, small_o,
    flat, w_in, w_out, bias_in, vec, acc_in, acc_out, acc_bias, acc_vec, f_sc, gp_sc, *, real,
):
    item, chunk = pl.program_id(0), pl.program_id(1)
    first = (item == 0) & (chunk == 0)
    last = (item == pl.num_programs(0) - 1) & (chunk == pl.num_programs(1) - 1)
    mat = D * FF // LANES

    @pl.when(first)
    def _():
        load_flat(order, pn_ref, pf_ref, flat, real)

        def put_in(j, block):
            w_in[:, j * LANES : (j + 1) * LANES] = block.astype(bf16)

        def put_out(j, block):
            w_out[:, j * LANES : (j + 1) * LANES] = block.astype(bf16)

        take_matrix(flat, 0, D, FF, put_in)
        take_matrix(flat, mat, FF, D, put_out)
        bias_in[...] = take_vector(flat, 2 * mat, FF)
        for i in range(3):
            vec[i : i + 1, :] = take_vector(flat, 2 * mat + FF // LANES + i * (D // LANES), D)
        acc_in[...] = jnp.zeros_like(acc_in)
        acc_out[...] = jnp.zeros_like(acc_out)
        acc_bias[...] = jnp.zeros_like(acc_bias)
        acc_vec[...] = jnp.zeros_like(acc_vec)
        small_o[...] = jnp.zeros_like(small_o)

    @pl.when(chunk < nch[item])
    def _():
        n2, r2 = norm_stats(h_ref[0])
        x2 = n2 * vec2_ref[3:4, :] + vec2_ref[4:5, :]
        x2b = x2.astype(bf16)
        u = dot(x2b, w_in[...]) + bias_in[...]
        cdf = 0.5 * (1.0 + lax.erf(u * 0.7071067811865476))
        f_sc[...] = (u * cdf).astype(bf16)
        gp_sc[...] = cdf + u * jnp.exp(u * u * -0.5) * (1.0 / math.sqrt(2.0 * math.pi))
        h3 = x2 + dot(f_sc[...], w_out[...]) + vec[0:1, :]
        n3, r3 = norm_stats(h3)
        at = lax.broadcasted_iota(jnp.int32, (CH, 1), 0) + chunk * CH
        valid = (at < LABEL + horizon[item]).astype(f32)
        y_o[0] = ((n3 * vec[1:2, :] + vec[2:3, :]) * valid).astype(bf16)
        dy = ct_ref[0].astype(f32) * valid
        acc_vec[1:2, :] += col_sum(dy * n3)
        acc_vec[2:3, :] += col_sum(dy)
        dh3 = norm_back(dy, n3, r3, vec[1:2, :])
        acc_vec[0:1, :] += col_sum(dh3)
        e3 = dh3.astype(bf16)
        acc_out[...] += dot(e3.T, f_sc[...])
        du = dot_nt(e3, w_out[...]) * gp_sc[...]
        acc_bias[...] += col_sum(du)
        eu = du.astype(bf16)
        acc_in[...] += dot(x2b.T, eu)
        dx2 = dh3 + dot_nt(eu, w_in[...])
        small_o[3:4, :] += col_sum(dx2 * n2)
        small_o[4:5, :] += col_sum(dx2)
        dh2 = norm_back(dx2, n2, r2, vec2_ref[3:4, :])
        small_o[2:3, :] += col_sum(dh2)
        dh2_o[0] = dh2

    @pl.when(chunk >= nch[item])
    def _():
        y_o[0] = jnp.zeros((CH, D), bf16)

    @pl.when(last)
    def _():
        put_matrix(flat, 0, D, FF, lambda j: acc_in[:, j * LANES : (j + 1) * LANES])
        for j in range(D // LANES):
            flat[pl.ds(mat + j, FF, stride=D // LANES), :] = acc_out[j * LANES : (j + 1) * LANES, :].T
        flat[2 * mat :, :] = jnp.zeros((flat.shape[0] - 2 * mat, LANES), f32)
        put_vector(flat, 2 * mat, acc_bias[...])
        for i in range(3):
            put_vector(flat, 2 * mat + FF // LANES + i * (D // LANES), acc_vec[i : i + 1, :])
        store_flat(order, gn_o, gf_o, flat, real)


def dense_both(nch, order, horizon, h2, ct, params, vec2, real):
    items, steps, _ = h2.shape
    chunks = steps // CH
    half, rows, _ = params[0].shape

    def row_block(i, c, nch_ref, _):
        return (i, jnp.minimum(c, nch_ref[i] - 1), 0)

    rowspec = pl.BlockSpec((1, CH, D), row_block)
    whole2 = lambda i, c, *_: (0, 0)
    shards = pl.BlockSpec((half, rows, LANES), lambda i, c, *_: (0, 0, 0), pipeline_mode=pl.Buffered(1))
    shape = jax.ShapeDtypeStruct
    return pl.pallas_call(
        functools.partial(dense_kernel, real=real),
        grid_spec=pltpu.PrefetchScalarGridSpec(
            num_scalar_prefetch=2,
            grid=(items, chunks),
            in_specs=[
                pl.BlockSpec(memory_space=pltpu.SMEM),
                rowspec, rowspec,
                shards, shards,
                pl.BlockSpec((8, D), whole2, pipeline_mode=pl.Buffered(1)),
            ],
            out_specs=[
                pl.BlockSpec((1, CH, D), lambda i, c, *_: (i, c, 0)),
                rowspec,
                shards, shards,
                pl.BlockSpec((8, D), whole2, pipeline_mode=pl.Buffered(1)),
            ],
            scratch_shapes=[
                pltpu.VMEM((2 * half * real + 16, LANES), f32),
                pltpu.VMEM((D, FF), bf16), pltpu.VMEM((FF, D), bf16),
                pltpu.VMEM((1, FF), f32), pltpu.VMEM((8, D), f32),
                pltpu.VMEM((D, FF), f32), pltpu.VMEM((D, FF), f32),
                pltpu.VMEM((1, FF), f32), pltpu.VMEM((8, D), f32),
                pltpu.VMEM((CH, FF), bf16), pltpu.VMEM((CH, FF), f32),
            ],
        ),
        out_shape=[
            shape((items, steps, D), bf16), shape((items, steps, D), f32),
            shape((half, rows, LANES), bf16), shape((half, rows, LANES), bf16), shape((8, D), f32),
        ],
        compiler_params=pltpu.CompilerParams(vmem_limit_bytes=VMEM_LIMIT),
        cost_estimate=pl.CostEstimate(flops=int(2e10), bytes_accessed=int(3e7), transcendentals=0),
        name="dense_both",
    )(nch, order, horizon, h2, ct, *params, vec2)


def attend_back(head, pair, keys_pair, values_pair, keys_t, qt, dat, q_pair, da_pair, lse, shift, scale, masks, causal):
    raw = dot(keys_pair, head_rhs(qt, head))
    s = raw * scale - lse
    if shift is not None:
        s = s + shift
    weights = jnp.exp2(s)
    if causal:
        weights = causal_cut(weights, 0.0)
    dp = dot(values_pair, head_rhs(dat, head))
    inner = jnp.sum(weights * dp, 0, keepdims=True)
    g = (weights * (dp - inner)).astype(bf16)
    mask = masks[head % 2]
    dv = dot(weights.astype(bf16), da_pair * mask)
    dk = dot(g, q_pair * mask)
    dqt = dot(keys_t, g)
    return dqt, dk, dv


def cross_backward_kernel(
    nch, order, tau, dh2_ref, h1_ref, m_ref, shift_ref, q_ref, qt_ref, k_ref, kt_ref, v_ref, at_ref, lse_ref,
    w, vec1_ref, small2_ref, dh1_o, gm_o, gn_o, gf_o, small_o,
    flat, acc, acc_vec, dksc, dvsc, dqt, *, real,
):
    item, chunk = pl.program_id(0), pl.program_id(1)
    first = (item == 0) & (chunk == 0)
    last = (item == pl.num_programs(0) - 1) & (chunk == pl.num_programs(1) - 1)

    @pl.when(first)
    def _():
        acc[...] = jnp.zeros_like(acc)
        acc_vec[...] = small2_ref[...]
        small_o[...] = jnp.zeros_like(small_o)

    @pl.when(chunk == 0)
    def _():
        dksc[...] = jnp.zeros_like(dksc)
        dvsc[...] = jnp.zeros_like(dvsc)

    @pl.when(chunk < nch[item])
    def _():
        factor = tau[item] * (1.0 / math.sqrt(HW))
        scale = tau[item] * (LOG2E / math.sqrt(HW))
        shift = shift_ref[0] * (LOG2E / math.sqrt(HW))
        dh2 = dh2_ref[0]
        e2 = dh2.astype(bf16)
        acc[:, 3 * D :] += dot(at_ref[0], e2)
        da = dot_nt(e2, w[:, 3 * D :]).astype(bf16)
        dat = da.T
        qt = qt_ref[0]
        masks = pair_masks((CH, LANES), bf16)
        for pair in range(HEADS // 2):
            lanes = slice(pair * LANES, (pair + 1) * LANES)
            dk_pair, dv_pair = 0.0, 0.0
            for head in (2 * pair, 2 * pair + 1):
                rows = slice(head * HW, (head + 1) * HW)
                part, dk, dv = attend_back(
                    head, pair, k_ref[0, :, lanes], v_ref[0, :, lanes], kt_ref[0, rows, :], qt, dat,
                    q_ref[0, :, lanes], da[:, lanes], lse_ref[0, head : head + 1, :], shift, scale, masks, False,
                )
                dqt[rows, :] = (part * factor).astype(bf16)
                dk_pair, dv_pair = dk_pair + dk, dv_pair + dv
            dksc[:, lanes] += dk_pair * factor
            dvsc[:, lanes] += dv_pair
        dq = dqt[...].T
        acc_vec[0:1, :] += col_sum(dq.astype(f32))
        n1, r1 = norm_stats(h1_ref[0])
        x1b = (n1 * vec1_ref[3:4, :] + vec1_ref[4:5, :]).astype(bf16)
        acc[:, :D] += dot(x1b.T, dq)
        dx1 = dh2 + dot_nt(dq, w[:, :D])
        small_o[3:4, :] += col_sum(dx1 * n1)
        small_o[4:5, :] += col_sum(dx1)
        dh1 = norm_back(dx1, n1, r1, vec1_ref[3:4, :])
        small_o[2:3, :] += col_sum(dh1)
        dh1_o[0] = dh1

    @pl.when(chunk == pl.num_programs(1) - 1)
    def _():
        dv = dvsc[...]
        acc_vec[1:2, :] += col_sum(dv)
        dkv = jnp.concatenate([dksc[...].astype(bf16), dv.astype(bf16)], 1)
        acc[:, D : 3 * D] += dot(m_ref[0].T, dkv)
        gm_o[0] = dot_nt(dkv, w[:, D : 3 * D])

    @pl.when(last)
    def _():
        store_attention(order, gn_o, gf_o, flat, real, acc, acc_vec)


def cross_backward(nch, order, tau, dh2, h1, memory, shift, saved, w, vec1, small2, half, rows, real):
    q, qt, k, kt, v, at, lse = saved
    items, steps, _ = h1.shape
    mem = memory.shape[1]
    chunks = steps // CH

    def row_block(i, c, nch_ref, _):
        return (i, jnp.minimum(c, nch_ref[i] - 1), 0)

    def col_block(i, c, nch_ref, _):
        return (i, 0, jnp.minimum(c, nch_ref[i] - 1))

    per_item = lambda i, c, *_: (i, 0, 0)
    rowspec = pl.BlockSpec((1, CH, D), row_block)
    colspec = pl.BlockSpec((1, D, CH), col_block)
    memspec = pl.BlockSpec((1, mem, D), per_item)
    whole2 = lambda i, c, *_: (0, 0)
    shards = pl.BlockSpec((half, rows, LANES), lambda i, c, *_: (0, 0, 0), pipeline_mode=pl.Buffered(1))
    once = pl.Buffered(1)
    shape = jax.ShapeDtypeStruct
    return pl.pallas_call(
        functools.partial(cross_backward_kernel, real=real),
        grid_spec=pltpu.PrefetchScalarGridSpec(
            num_scalar_prefetch=2,
            grid=(items, chunks),
            in_specs=[
                pl.BlockSpec(memory_space=pltpu.SMEM),
                rowspec, rowspec, memspec,
                pl.BlockSpec((1, mem, 1), per_item),
                rowspec, colspec, memspec,
                pl.BlockSpec((1, D, mem), per_item),
                memspec, colspec,
                pl.BlockSpec((1, HEADS, CH), col_block),
                pl.BlockSpec((D, 4 * D), whole2, pipeline_mode=once),
                pl.BlockSpec((8, D), whole2, pipeline_mode=once),
                pl.BlockSpec((8, D), whole2, pipeline_mode=once),
            ],
            out_specs=[
                rowspec, memspec,
                shards, shards,
                pl.BlockSpec((8, D), whole2, pipeline_mode=once),
            ],
            scratch_shapes=[
                pltpu.VMEM((2 * half * real + 16, LANES), f32),
                pltpu.VMEM((D, 4 * D), f32), pltpu.VMEM((8, D), f32),
                pltpu.VMEM((mem, D), f32), pltpu.VMEM((mem, D), f32),
                pltpu.VMEM((D, CH), bf16),
            ],
        ),
        out_shape=[
            shape((items, steps, D), f32), shape((items, mem, D), f32),
            shape((half, rows, LANES), bf16), shape((half, rows, LANES), bf16), shape((8, D), f32),
        ],
        compiler_params=pltpu.CompilerParams(vmem_limit_bytes=VMEM_LIMIT),
        cost_estimate=pl.CostEstimate(flops=int(8e9), bytes_accessed=int(2e7), transcendentals=0),
        name="cross_backward",
    )(nch, order, tau, dh2, h1, memory, shift, q, qt, k, kt, v, at, lse, w, vec1, small2)


def self_backward_kernel(
    nch, order, tau, dh1_ref, x_ref, q_ref, qt_ref, k_ref, kt_ref, v_ref, at_ref, lse_ref,
    w, small1_ref, gx_o, gn_o, gf_o,
    flat, acc, acc_vec, dksc, dvsc, dqt, *, real, chunks,
):
    item, step = pl.program_id(0), pl.program_id(1)
    chunk = chunks - 1 - step
    first = (item == 0) & (step == 0)
    last = (item == pl.num_programs(0) - 1) & (step == chunks - 1)

    @pl.when(first)
    def _():
        acc[...] = jnp.zeros_like(acc)
        acc_vec[...] = small1_ref[...]

    @pl.when(step == 0)
    def _():
        dksc[...] = jnp.zeros_like(dksc)
        dvsc[...] = jnp.zeros_like(dvsc)

    @pl.when(chunk < nch[item])
    def _():
        factor = tau[item] * (1.0 / math.sqrt(HW))
        scale = tau[item] * (LOG2E / math.sqrt(HW))
        dh1 = dh1_ref[0]
        e1 = dh1.astype(bf16)
        acc[:, 3 * D :] += dot(at_ref[0], e1)
        da = dot_nt(e1, w[:, 3 * D :]).astype(bf16)
        dat = da.T
        qt = qt_ref[0]
        masks = pair_masks((CH, LANES), bf16)
        for at_chunk in range(chunks):

            @pl.when(chunk == at_chunk)
            def _(keys=(at_chunk + 1) * CH):
                for pair in range(HEADS // 2):
                    lanes = slice(pair * LANES, (pair + 1) * LANES)
                    dk_pair, dv_pair = 0.0, 0.0
                    for head in (2 * pair, 2 * pair + 1):
                        rows = slice(head * HW, (head + 1) * HW)
                        part, dk, dv = attend_back(
                            head, pair, k_ref[0, :keys, lanes], v_ref[0, :keys, lanes], kt_ref[0, rows, :keys], qt, dat,
                            q_ref[0, :, lanes], da[:, lanes], lse_ref[0, head : head + 1, :], None, scale, masks, True,
                        )
                        dqt[rows, :] = (part * factor).astype(bf16)
                        dk_pair, dv_pair = dk_pair + dk, dv_pair + dv
                    dksc[:keys, lanes] += dk_pair * factor
                    dvsc[:keys, lanes] += dv_pair

        here = pl.ds(pl.multiple_of(chunk * CH, CH), CH)
        dq = dqt[...].T
        dv = dvsc[here, :]
        acc_vec[0:1, :] += col_sum(dq.astype(f32))
        acc_vec[1:2, :] += col_sum(dv)
        dqkv = jnp.concatenate([dq, dksc[here, :].astype(bf16), dv.astype(bf16)], 1)
        acc[:, : 3 * D] += dot(x_ref[0].T, dqkv)
        gx_o[0] = dh1 + dot_nt(dqkv, w[:, : 3 * D])

    @pl.when(chunk >= nch[item])
    def _():
        gx_o[0] = jnp.zeros((CH, D), f32)

    @pl.when(last)
    def _():
        store_attention(order, gn_o, gf_o, flat, real, acc, acc_vec)


def self_backward(nch, order, tau, dh1, x, saved, w, small1, half, rows, real):
    q, qt, k, kt, v, at, lse = saved
    items, steps, _ = x.shape
    chunks = steps // CH

    def row_block(i, c, nch_ref, _):
        return (i, jnp.minimum(chunks - 1 - c, nch_ref[i] - 1), 0)

    def col_block(i, c, nch_ref, _):
        return (i, 0, jnp.minimum(chunks - 1 - c, nch_ref[i] - 1))

    per_item = lambda i, c, *_: (i, 0, 0)
    rowspec = pl.BlockSpec((1, CH, D), row_block)
    colspec = pl.BlockSpec((1, D, CH), col_block)
    itemspec = pl.BlockSpec((1, steps, D), per_item)
    whole2 = lambda i, c, *_: (0, 0)
    shards = pl.BlockSpec((half, rows, LANES), lambda i, c, *_: (0, 0, 0), pipeline_mode=pl.Buffered(1))
    once = pl.Buffered(1)
    shape = jax.ShapeDtypeStruct
    return pl.pallas_call(
        functools.partial(self_backward_kernel, real=real, chunks=chunks),
        grid_spec=pltpu.PrefetchScalarGridSpec(
            num_scalar_prefetch=2,
            grid=(items, chunks),
            in_specs=[
                pl.BlockSpec(memory_space=pltpu.SMEM),
                rowspec, rowspec, rowspec, colspec, itemspec,
                pl.BlockSpec((1, D, steps), per_item),
                itemspec, colspec,
                pl.BlockSpec((1, HEADS, CH), col_block),
                pl.BlockSpec((D, 4 * D), whole2, pipeline_mode=once),
                pl.BlockSpec((8, D), whole2, pipeline_mode=once),
            ],
            out_specs=[
                pl.BlockSpec((1, CH, D), lambda i, c, *_: (i, chunks - 1 - c, 0)),
                shards, shards,
            ],
            scratch_shapes=[
                pltpu.VMEM((2 * half * real + 16, LANES), f32),
                pltpu.VMEM((D, 4 * D), f32), pltpu.VMEM((8, D), f32),
                pltpu.VMEM((steps, D), f32), pltpu.VMEM((steps, D), f32),
                pltpu.VMEM((D, CH), bf16),
            ],
        ),
        out_shape=[shape((items, steps, D), f32), shape((half, rows, LANES), bf16), shape((half, rows, LANES), bf16)],
        compiler_params=pltpu.CompilerParams(vmem_limit_bytes=VMEM_LIMIT),
        cost_estimate=pl.CostEstimate(flops=int(1.5e10), bytes_accessed=int(2e7), transcendentals=0),
        name="self_backward",
    )(nch, order, tau, dh1, x, q, qt, k, kt, v, at, lse, w, small1)


AXES = ("wide", "narrow")


def exchange(rows, offset, count):
    return lax.ppermute(rows, AXES, [(i, i ^ offset) for i in range(count)])


def offsets(narrow, count):
    core, plane = narrow, 4 * narrow
    along_z = list(range(plane, count, plane))
    within = [y * 2 * narrow + x for y in range(2) for x in range(narrow)][1:]
    return along_z, within, core


def slot_owners(narrow, count):
    along_z, within, core = offsets(narrow, count)
    near = [a ^ b for a in [0] + within for b in [0] + along_z]
    return near + [a ^ core for a in near]


def gather_shards(shard, narrow, count):
    along_z, within, core = offsets(narrow, count)
    line = jnp.stack([shard] + [exchange(shard, o, count) for o in along_z])
    near = jnp.concatenate([line] + [exchange(line, o, count) for o in within])
    return near, exchange(near, core, count)


def add_up(parts):
    return sum(part.astype(f32) for part in parts)


def scatter_shards(near, far, narrow, count):
    along_z, within, core = offsets(narrow, count)
    depth = 1 + len(along_z)
    mine = add_up([near, exchange(far, core, count)]).astype(bf16)
    got = [exchange(mine[(1 + i) * depth : (2 + i) * depth], o, count) for i, o in enumerate(within)]
    line = add_up([mine[:depth]] + got).astype(bf16)
    got = [exchange(line[1 + i], o, count) for i, o in enumerate(along_z)]
    return add_up([line[0]] + got)


def to_rows(shard):
    real = shard.shape[0] // LANES
    padded = (real + 15) // 16 * 16
    return jnp.pad(shard.reshape(real, LANES), ((0, padded - real), (0, 0)))


def from_rows(rows, length):
    return rows[: length // LANES].reshape(length)


def body(inputs, memory, tau_scale, delta_shift, horizon, self_params, cross_params, dense_params, cotangent):
    narrow = lax.axis_size("narrow")
    count = lax.axis_size(AXES)
    x, m, ct = inputs[:, 0], memory[:, 0], cotangent[:, 0]
    tau, shift, horizon = tau_scale[:, 0], delta_shift[:, 0, :, None], horizon[:, 0]
    order = lax.axis_index(AXES) ^ jnp.array(slot_owners(narrow, count), jnp.int32)
    steps = x.shape[1]
    nch = jnp.minimum((horizon + (LABEL + CH - 1)) // CH, steps // CH).astype(jnp.int32)
    real_a, real_d = self_params.shape[0] // LANES, dense_params.shape[0] // LANES
    p_self = gather_shards(to_rows(self_params), narrow, count)
    p_cross = gather_shards(to_rows(cross_params), narrow, count)
    p_dense = gather_shards(to_rows(dense_params), narrow, count)
    half, rows = p_self[0].shape[:2]
    q, qt, k, kt, v, at, h1, lse, w1, vec1 = self_forward(nch, order, tau, x, p_self, real_a)
    q2, qt2, k2, kt2, v2, at2, h2, lse2, w2, vec2 = cross_forward(nch, order, tau, h1, m, shift, p_cross, vec1, real_a)
    y, dh2, gn, gf, small2 = dense_both(nch, order, horizon, h2, ct, p_dense, vec2, real_d)
    g_dense = scatter_shards(gn, gf, narrow, count)
    dh1, gm, gn, gf, small1 = cross_backward(
        nch, order, tau, dh2, h1, m, shift, (q2, qt2, k2, kt2, v2, at2, lse2), w2, vec1, small2, half, rows, real_a
    )
    g_cross = scatter_shards(gn, gf, narrow, count)
    gx, gn, gf = self_backward(nch, order, tau, dh1, x, (q, qt, k, kt, v, at, lse), w1, small1, half, rows, real_a)
    g_self = scatter_shards(gn, gf, narrow, count)
    return (
        y[:, None], gx[:, None], gm[:, None],
        from_rows(g_self, self_params.shape[0]),
        from_rows(g_cross, cross_params.shape[0]),
        from_rows(g_dense, dense_params.shape[0]),
    )


def solution(mesh):
    items = P(None, AXES, None, None)
    placed = (items, items, P(None, AXES), P(None, AXES, None), P(None, AXES), P(AXES), P(AXES), P(AXES), items)
    return jax.shard_map(
        body, mesh=mesh, in_specs=placed, out_specs=(items, items, items, P(AXES), P(AXES), P(AXES)), check_vma=False
    )
```

```python
import functools
import math

import jax
import jax.numpy as jnp
from jax import lax
from jax.experimental import pallas as pl
from jax.experimental.pallas import tpu as pltpu
from jax.sharding import PartitionSpec as P

D = 512
FF = 2048
HEADS = 8
HW = D // HEADS
LABEL = 48
LANES = 128
CH = 256
EPS = 1e-05
NEG = -1e30
LOG2E = 1.4426950408889634
f32, bf16 = jnp.float32, jnp.bfloat16
VMEM_LIMIT = 60 * 2**20


def dot(a, b):
    return jnp.dot(a, b, preferred_element_type=f32)


def dot_nt(a, b):
    return lax.dot_general(a, b, (((1,), (1,)), ((), ())), preferred_element_type=f32)


def norm_stats(h):
    center = h - jnp.mean(h, -1, keepdims=True)
    rstd = lax.rsqrt(jnp.mean(center * center, -1, keepdims=True) + EPS)
    return center * rstd, rstd


def norm_back(dz, n, rstd, gain):
    dn = dz * gain
    return rstd * (dn - jnp.mean(dn, -1, keepdims=True) - n * jnp.mean(dn * n, -1, keepdims=True))


def col_sum(v):
    return jnp.sum(v, 0, keepdims=True)


def load_flat(order, near_ref, far_ref, flat, real):
    half = near_ref.shape[0]

    @pl.loop(0, half)
    def _(k):
        flat[pl.ds(order[k] * real, real), :] = near_ref[k, :real, :].astype(f32)
        flat[pl.ds(order[half + k] * real, real), :] = far_ref[k, :real, :].astype(f32)


def store_flat(order, near_ref, far_ref, flat, real):
    half, rows = near_ref.shape[:2]

    @pl.loop(0, half)
    def _(k):
        near_ref[k] = flat[pl.ds(order[k] * real, rows), :].astype(bf16)
        far_ref[k] = flat[pl.ds(order[half + k] * real, rows), :].astype(bf16)


def take_matrix(flat, start, height, width, put):
    per = width // LANES
    for j in range(per):
        put(j, flat[pl.ds(start + j, height, stride=per), :])


def take_vector(flat, start, width):
    return jnp.concatenate([flat[start + j : start + j + 1, :] for j in range(width // LANES)], 1)


def put_matrix(flat, start, height, width, get):
    per = width // LANES
    for j in range(per):
        flat[pl.ds(start + j, height, stride=per), :] = get(j)


def put_vector(flat, start, row):
    for j in range(row.shape[1] // LANES):
        flat[start + j : start + j + 1, :] = row[:, j * LANES : (j + 1) * LANES]


MAT_ROWS = D * D // LANES


def load_attention(order, near_ref, far_ref, flat, real, w_ref, vec_ref):
    load_flat(order, near_ref, far_ref, flat, real)
    for m in range(4):

        def put(j, block, m=m):
            w_ref[:, m * D + j * LANES : m * D + (j + 1) * LANES] = block.astype(bf16)

        take_matrix(flat, m * MAT_ROWS, D, D, put)
    for i in range(5):
        vec_ref[i : i + 1, :] = take_vector(flat, 4 * MAT_ROWS + i * (D // LANES), D)


def store_attention(order, near_ref, far_ref, flat, real, acc, vec_ref):
    for m in range(4):
        put_matrix(
            flat, m * MAT_ROWS, D, D, lambda j, m=m: acc[:, m * D + j * LANES : m * D + (j + 1) * LANES]
        )
    flat[4 * MAT_ROWS :, :] = jnp.zeros((flat.shape[0] - 4 * MAT_ROWS, LANES), f32)
    for i in range(5):
        put_vector(flat, 4 * MAT_ROWS + i * (D // LANES), vec_ref[i : i + 1, :])
    store_flat(order, near_ref, far_ref, flat, real)


def head_rhs(rows_t, head):
    block = rows_t[head * HW : (head + 1) * HW, :]
    zero = jnp.zeros_like(block)
    return jnp.concatenate([block, zero] if head % 2 == 0 else [zero, block], 0)


def shift_column(shift_ref):
    row = shift_ref[0] * (LOG2E / math.sqrt(HW))
    return jnp.broadcast_to(row, (8, row.shape[1])).T[:, :1]


def pair_masks(shape, dtype):
    lane = lax.broadcasted_iota(jnp.int32, shape, 1)
    low = lane < HW
    return low.astype(f32).astype(dtype), jnp.logical_not(low).astype(f32).astype(dtype)


def causal_cut(scores, fill):
    keys = scores.shape[0]
    tail = scores[keys - CH :, :]
    key_at = lax.broadcasted_iota(jnp.int32, tail.shape, 0)
    query_at = lax.broadcasted_iota(jnp.int32, tail.shape, 1)
    tail = jnp.where(key_at <= query_at, tail, fill)
    if keys == CH:
        return tail
    return jnp.concatenate([scores[: keys - CH, :], tail], 0)


def self_forward_kernel(
    nch, order, tau, x_ref, pn_ref, pf_ref, q_o, qt_o, k_o, kt_o, v_o, at_o, h_o, lse_o, w_o, vec_o,
    flat, w, vec, ksc, vtsc, at, qt, *, real, chunks,
):
    item, chunk = pl.program_id(0), pl.program_id(1)

    @pl.when((item == 0) & (chunk == 0))
    def _():
        load_attention(order, pn_ref, pf_ref, flat, real, w, vec)
        w_o[...] = w[...]
        vec_o[...] = vec[...]

    @pl.when(chunk < nch[item])
    def _():
        scale = tau[item] * (LOG2E / math.sqrt(HW))
        x = x_ref[0]
        qkv = dot(x, w[:, : 3 * D])
        q = (qkv[:, :D] + vec[0:1, :]).astype(bf16)
        k = qkv[:, D : 2 * D].astype(bf16)
        v = (qkv[:, 2 * D :] + vec[1:2, :]).astype(bf16)
        q_o[0] = q
        k_o[0] = k
        v_o[0] = v
        qt[...] = q.T
        qt_o[0] = qt[...]
        kt_o[0] = k.T
        ksc[pl.ds(pl.multiple_of(chunk * CH, CH), CH), :] = k
        vtsc[:, pl.ds(pl.multiple_of(chunk * CH, CH), CH)] = v.T
        for at_chunk in range(chunks):

            @pl.when(chunk == at_chunk)
            def _(keys=(at_chunk + 1) * CH):
                for head in range(HEADS):
                    pair = head // 2
                    raw = dot(ksc[:keys, pair * LANES : (pair + 1) * LANES], head_rhs(qt, head))
                    s = causal_cut(raw * scale, NEG)
                    top = jnp.max(s, 0, keepdims=True)
                    e = jnp.exp2(s - top)
                    total = jnp.sum(e, 0, keepdims=True)
                    mixed = dot(vtsc[head * HW : (head + 1) * HW, :keys], e.astype(bf16))
                    at[head * HW : (head + 1) * HW, :] = (mixed * (1.0 / total)).astype(bf16)
                    lse_o[0, head : head + 1, :] = top + jnp.log2(total)

        at_o[0] = at[...]
        a = at[...].T
        h_o[0] = x.astype(f32) + dot(a, w[:, 3 * D :]) + vec[2:3, :]


def self_forward(nch, order, tau, x, params, real):
    items, steps, _ = x.shape
    chunks = steps // CH
    half, rows, _ = params[0].shape

    def row_block(i, c, nch_ref, _):
        return (i, jnp.minimum(c, nch_ref[i] - 1), 0)

    def col_block(i, c, nch_ref, _):
        return (i, 0, jnp.minimum(c, nch_ref[i] - 1))

    rowspec = pl.BlockSpec((1, CH, D), row_block)
    colspec = pl.BlockSpec((1, D, CH), col_block)
    whole2 = lambda i, c, *_: (0, 0)
    shards = pl.BlockSpec((half, rows, LANES), lambda i, c, *_: (0, 0, 0), pipeline_mode=pl.Buffered(1))
    shape = jax.ShapeDtypeStruct
    return pl.pallas_call(
        functools.partial(self_forward_kernel, real=real, chunks=chunks),
        grid_spec=pltpu.PrefetchScalarGridSpec(
            num_scalar_prefetch=2,
            grid=(items, chunks),
            in_specs=[
                pl.BlockSpec(memory_space=pltpu.SMEM),
                rowspec,
                shards, shards,
            ],
            out_specs=[
                rowspec, colspec, rowspec, colspec, rowspec, colspec, rowspec,
                pl.BlockSpec((1, HEADS, CH), col_block),
                pl.BlockSpec((D, 4 * D), whole2, pipeline_mode=pl.Buffered(1)),
                pl.BlockSpec((8, D), whole2, pipeline_mode=pl.Buffered(1)),
            ],
            scratch_shapes=[
                pltpu.VMEM((2 * half * real + 16, LANES), f32),
                pltpu.VMEM((D, 4 * D), bf16),
                pltpu.VMEM((8, D), f32),
                pltpu.VMEM((steps, D), bf16),
                pltpu.VMEM((D, steps), bf16),
                pltpu.VMEM((D, CH), bf16),
                pltpu.VMEM((D, CH), bf16),
            ],
        ),
        out_shape=[
            shape((items, steps, D), bf16), shape((items, D, steps), bf16),
            shape((items, steps, D), bf16), shape((items, D, steps), bf16),
            shape((items, steps, D), bf16), shape((items, D, steps), bf16),
            shape((items, steps, D), f32), shape((items, HEADS, steps), f32),
            shape((D, 4 * D), bf16), shape((8, D), f32),
        ],
        compiler_params=pltpu.CompilerParams(vmem_limit_bytes=VMEM_LIMIT),
        cost_estimate=pl.CostEstimate(flops=int(8e9), bytes_accessed=int(2e7), transcendentals=0),
        name="self_forward",
    )(nch, order, tau, x, *params)


def cross_forward_kernel(
    nch, order, tau, h_ref, m_ref, shift_ref, pn_ref, pf_ref, vec1_ref, q_o, qt_o, k_o, kt_o, v_o, at_o, h_o, lse_o, w_o, vec_o,
    flat, w, vec, vtsc, at, qt, *, real, mem,
):
    item, chunk = pl.program_id(0), pl.program_id(1)

    @pl.when((item == 0) & (chunk == 0))
    def _():
        load_attention(order, pn_ref, pf_ref, flat, real, w, vec)
        w_o[...] = w[...]
        vec_o[...] = vec[...]

    @pl.when(chunk == 0)
    def _():
        kv = dot(m_ref[0], w[:, D : 3 * D])
        k = kv[:, :D].astype(bf16)
        v = (kv[:, D:] + vec[1:2, :]).astype(bf16)
        k_o[0] = k
        kt_o[0] = k.T
        v_o[0] = v
        vtsc[...] = v.T

    @pl.when(chunk < nch[item])
    def _():
        scale = tau[item] * (LOG2E / math.sqrt(HW))
        shift = shift_column(shift_ref)
        n1, _ = norm_stats(h_ref[0])
        x1 = n1 * vec1_ref[3:4, :] + vec1_ref[4:5, :]
        q = (dot(x1.astype(bf16), w[:, :D]) + vec[0:1, :]).astype(bf16)
        q_o[0] = q
        qt[...] = q.T
        qt_o[0] = qt[...]
        for head in range(HEADS):
            pair = head // 2
            raw = dot(k_o[0, :, pair * LANES : (pair + 1) * LANES], head_rhs(qt, head))
            s = raw * scale + shift
            top = jnp.max(s, 0, keepdims=True)
            e = jnp.exp2(s - top)
            total = jnp.sum(e, 0, keepdims=True)
            mixed = dot(vtsc[head * HW : (head + 1) * HW, :], e.astype(bf16))
            at[head * HW : (head + 1) * HW, :] = (mixed * (1.0 / total)).astype(bf16)
            lse_o[0, head : head + 1, :] = top + jnp.log2(total)
        at_o[0] = at[...]
        a = at[...].T
        h_o[0] = x1 + dot(a, w[:, 3 * D :]) + vec[2:3, :]


def cross_forward(nch, order, tau, h1, memory, shift, params, vec1, real):
    items, steps, _ = h1.shape
    mem = memory.shape[1]
    chunks = steps // CH
    half, rows, _ = params[0].shape

    def row_block(i, c, nch_ref, _):
        return (i, jnp.minimum(c, nch_ref[i] - 1), 0)

    def col_block(i, c, nch_ref, _):
        return (i, 0, jnp.minimum(c, nch_ref[i] - 1))

    per_item = lambda i, c, *_: (i, 0, 0)
    rowspec = pl.BlockSpec((1, CH, D), row_block)
    colspec = pl.BlockSpec((1, D, CH), col_block)
    memspec = pl.BlockSpec((1, mem, D), per_item)
    whole2 = lambda i, c, *_: (0, 0)
    shards = pl.BlockSpec((half, rows, LANES), lambda i, c, *_: (0, 0, 0), pipeline_mode=pl.Buffered(1))
    shape = jax.ShapeDtypeStruct
    return pl.pallas_call(
        functools.partial(cross_forward_kernel, real=real, mem=mem),
        grid_spec=pltpu.PrefetchScalarGridSpec(
            num_scalar_prefetch=2,
            grid=(items, chunks),
            in_specs=[
                pl.BlockSpec(memory_space=pltpu.SMEM),
                rowspec,
                memspec,
                pl.BlockSpec((1, 1, mem), per_item),
                shards, shards,
                pl.BlockSpec((8, D), whole2, pipeline_mode=pl.Buffered(1)),
            ],
            out_specs=[
                rowspec, colspec, memspec,
                pl.BlockSpec((1, D, mem), per_item),
                memspec, colspec, rowspec,
                pl.BlockSpec((1, HEADS, CH), col_block),
                pl.BlockSpec((D, 4 * D), whole2, pipeline_mode=pl.Buffered(1)),
                pl.BlockSpec((8, D), whole2, pipeline_mode=pl.Buffered(1)),
            ],
            scratch_shapes=[
                pltpu.VMEM((2 * half * real + 16, LANES), f32),
                pltpu.VMEM((D, 4 * D), bf16),
                pltpu.VMEM((8, D), f32),
                pltpu.VMEM((D, mem), bf16),
                pltpu.VMEM((D, CH), bf16),
                pltpu.VMEM((D, CH), bf16),
            ],
        ),
        out_shape=[
            shape((items, steps, D), bf16), shape((items, D, steps), bf16),
            shape((items, mem, D), bf16), shape((items, D, mem), bf16),
            shape((items, mem, D), bf16), shape((items, D, steps), bf16),
            shape((items, steps, D), f32), shape((items, HEADS, steps), f32),
            shape((D, 4 * D), bf16), shape((8, D), f32),
        ],
        compiler_params=pltpu.CompilerParams(vmem_limit_bytes=VMEM_LIMIT),
        cost_estimate=pl.CostEstimate(flops=int(4e9), bytes_accessed=int(2e7), transcendentals=0),
        name="cross_forward",
    )(nch, order, tau, h1, memory, shift, *params, vec1)


def dense_kernel(
    nch, order, horizon, h_ref, ct_ref, pn_ref, pf_ref, vec2_ref, y_o, dh2_o, gn_o, gf_o, small_o,
    flat, w_in, w_out, bias_in, vec, acc_in, acc_out, acc_bias, acc_vec, f_sc, gp_sc, *, real,
):
    item, chunk = pl.program_id(0), pl.program_id(1)
    first = (item == 0) & (chunk == 0)
    last = (item == pl.num_programs(0) - 1) & (chunk == pl.num_programs(1) - 1)
    mat = D * FF // LANES

    @pl.when(first)
    def _():
        load_flat(order, pn_ref, pf_ref, flat, real)

        def put_in(j, block):
            w_in[:, j * LANES : (j + 1) * LANES] = block.astype(bf16)

        def put_out(j, block):
            w_out[:, j * LANES : (j + 1) * LANES] = block.astype(bf16)

        take_matrix(flat, 0, D, FF, put_in)
        take_matrix(flat, mat, FF, D, put_out)
        bias_in[...] = take_vector(flat, 2 * mat, FF)
        for i in range(3):
            vec[i : i + 1, :] = take_vector(flat, 2 * mat + FF // LANES + i * (D // LANES), D)
        acc_in[...] = jnp.zeros_like(acc_in)
        acc_out[...] = jnp.zeros_like(acc_out)
        acc_bias[...] = jnp.zeros_like(acc_bias)
        acc_vec[...] = jnp.zeros_like(acc_vec)
        small_o[...] = jnp.zeros_like(small_o)

    @pl.when(chunk < nch[item])
    def _():
        n2, r2 = norm_stats(h_ref[0])
        x2 = n2 * vec2_ref[3:4, :] + vec2_ref[4:5, :]
        x2b = x2.astype(bf16)
        u = dot(x2b, w_in[...]) + bias_in[...]
        cdf = 0.5 * (1.0 + lax.erf(u * 0.7071067811865476))
        f_sc[...] = (u * cdf).astype(bf16)
        gp_sc[...] = cdf + u * jnp.exp(u * u * -0.5) * (1.0 / math.sqrt(2.0 * math.pi))
        h3 = x2 + dot(f_sc[...], w_out[...]) + vec[0:1, :]
        n3, r3 = norm_stats(h3)
        at = lax.broadcasted_iota(jnp.int32, (CH, 1), 0) + chunk * CH
        valid = (at < LABEL + horizon[item]).astype(f32)
        y_o[0] = ((n3 * vec[1:2, :] + vec[2:3, :]) * valid).astype(bf16)
        dy = ct_ref[0].astype(f32) * valid
        acc_vec[1:2, :] += col_sum(dy * n3)
        acc_vec[2:3, :] += col_sum(dy)
        dh3 = norm_back(dy, n3, r3, vec[1:2, :])
        acc_vec[0:1, :] += col_sum(dh3)
        e3 = dh3.astype(bf16)
        acc_out[...] += dot(e3.T, f_sc[...])
        du = dot_nt(e3, w_out[...]) * gp_sc[...]
        acc_bias[...] += col_sum(du)
        eu = du.astype(bf16)
        acc_in[...] += dot(x2b.T, eu)
        dx2 = dh3 + dot_nt(eu, w_in[...])
        small_o[3:4, :] += col_sum(dx2 * n2)
        small_o[4:5, :] += col_sum(dx2)
        dh2 = norm_back(dx2, n2, r2, vec2_ref[3:4, :])
        small_o[2:3, :] += col_sum(dh2)
        dh2_o[0] = dh2

    @pl.when(chunk >= nch[item])
    def _():
        y_o[0] = jnp.zeros((CH, D), bf16)

    @pl.when(last)
    def _():
        put_matrix(flat, 0, D, FF, lambda j: acc_in[:, j * LANES : (j + 1) * LANES])
        for j in range(D // LANES):
            flat[pl.ds(mat + j, FF, stride=D // LANES), :] = acc_out[j * LANES : (j + 1) * LANES, :].T
        flat[2 * mat :, :] = jnp.zeros((flat.shape[0] - 2 * mat, LANES), f32)
        put_vector(flat, 2 * mat, acc_bias[...])
        for i in range(3):
            put_vector(flat, 2 * mat + FF // LANES + i * (D // LANES), acc_vec[i : i + 1, :])
        store_flat(order, gn_o, gf_o, flat, real)


def dense_both(nch, order, horizon, h2, ct, params, vec2, real):
    items, steps, _ = h2.shape
    chunks = steps // CH
    half, rows, _ = params[0].shape

    def row_block(i, c, nch_ref, _):
        return (i, jnp.minimum(c, nch_ref[i] - 1), 0)

    rowspec = pl.BlockSpec((1, CH, D), row_block)
    whole2 = lambda i, c, *_: (0, 0)
    shards = pl.BlockSpec((half, rows, LANES), lambda i, c, *_: (0, 0, 0), pipeline_mode=pl.Buffered(1))
    shape = jax.ShapeDtypeStruct
    return pl.pallas_call(
        functools.partial(dense_kernel, real=real),
        grid_spec=pltpu.PrefetchScalarGridSpec(
            num_scalar_prefetch=2,
            grid=(items, chunks),
            in_specs=[
                pl.BlockSpec(memory_space=pltpu.SMEM),
                rowspec, rowspec,
                shards, shards,
                pl.BlockSpec((8, D), whole2, pipeline_mode=pl.Buffered(1)),
            ],
            out_specs=[
                pl.BlockSpec((1, CH, D), lambda i, c, *_: (i, c, 0)),
                rowspec,
                shards, shards,
                pl.BlockSpec((8, D), whole2, pipeline_mode=pl.Buffered(1)),
            ],
            scratch_shapes=[
                pltpu.VMEM((2 * half * real + 16, LANES), f32),
                pltpu.VMEM((D, FF), bf16), pltpu.VMEM((FF, D), bf16),
                pltpu.VMEM((1, FF), f32), pltpu.VMEM((8, D), f32),
                pltpu.VMEM((D, FF), f32), pltpu.VMEM((D, FF), f32),
                pltpu.VMEM((1, FF), f32), pltpu.VMEM((8, D), f32),
                pltpu.VMEM((CH, FF), bf16), pltpu.VMEM((CH, FF), f32),
            ],
        ),
        out_shape=[
            shape((items, steps, D), bf16), shape((items, steps, D), f32),
            shape((half, rows, LANES), bf16), shape((half, rows, LANES), bf16), shape((8, D), f32),
        ],
        compiler_params=pltpu.CompilerParams(vmem_limit_bytes=VMEM_LIMIT),
        cost_estimate=pl.CostEstimate(flops=int(2e10), bytes_accessed=int(3e7), transcendentals=0),
        name="dense_both",
    )(nch, order, horizon, h2, ct, *params, vec2)


def attend_back(head, pair, keys_pair, values_pair, keys_t, qt, dat, q_pair, da_pair, lse, shift, scale, masks, causal):
    raw = dot(keys_pair, head_rhs(qt, head))
    s = raw * scale - lse
    if shift is not None:
        s = s + shift
    weights = jnp.exp2(s)
    if causal:
        weights = causal_cut(weights, 0.0)
    dp = dot(values_pair, head_rhs(dat, head))
    inner = jnp.sum(weights * dp, 0, keepdims=True)
    g = (weights * (dp - inner)).astype(bf16)
    mask = masks[head % 2]
    dv = dot(weights.astype(bf16), da_pair * mask)
    dk = dot(g, q_pair * mask)
    dqt = dot(keys_t, g)
    return dqt, dk, dv


def cross_backward_kernel(
    nch, order, tau, dh2_ref, h1_ref, m_ref, shift_ref, q_ref, qt_ref, k_ref, kt_ref, v_ref, at_ref, lse_ref,
    w, vec1_ref, small2_ref, dh1_o, gm_o, gn_o, gf_o, small_o,
    flat, acc, acc_vec, dksc, dvsc, dqt, *, real,
):
    item, chunk = pl.program_id(0), pl.program_id(1)
    first = (item == 0) & (chunk == 0)
    last = (item == pl.num_programs(0) - 1) & (chunk == pl.num_programs(1) - 1)

    @pl.when(first)
    def _():
        acc[...] = jnp.zeros_like(acc)
        acc_vec[...] = small2_ref[...]
        small_o[...] = jnp.zeros_like(small_o)

    @pl.when(chunk == 0)
    def _():
        dksc[...] = jnp.zeros_like(dksc)
        dvsc[...] = jnp.zeros_like(dvsc)

    @pl.when(chunk < nch[item])
    def _():
        factor = tau[item] * (1.0 / math.sqrt(HW))
        scale = tau[item] * (LOG2E / math.sqrt(HW))
        shift = shift_column(shift_ref)
        dh2 = dh2_ref[0]
        e2 = dh2.astype(bf16)
        acc[:, 3 * D :] += dot(at_ref[0], e2)
        da = dot_nt(e2, w[:, 3 * D :]).astype(bf16)
        dat = da.T
        qt = qt_ref[0]
        masks = pair_masks((CH, LANES), bf16)
        for pair in range(HEADS // 2):
            lanes = slice(pair * LANES, (pair + 1) * LANES)
            dk_pair, dv_pair = 0.0, 0.0
            for head in (2 * pair, 2 * pair + 1):
                rows = slice(head * HW, (head + 1) * HW)
                part, dk, dv = attend_back(
                    head, pair, k_ref[0, :, lanes], v_ref[0, :, lanes], kt_ref[0, rows, :], qt, dat,
                    q_ref[0, :, lanes], da[:, lanes], lse_ref[0, head : head + 1, :], shift, scale, masks, False,
                )
                dqt[rows, :] = (part * factor).astype(bf16)
                dk_pair, dv_pair = dk_pair + dk, dv_pair + dv
            dksc[:, lanes] += dk_pair * factor
            dvsc[:, lanes] += dv_pair
        dq = dqt[...].T
        acc_vec[0:1, :] += col_sum(dq.astype(f32))
        n1, r1 = norm_stats(h1_ref[0])
        x1b = (n1 * vec1_ref[3:4, :] + vec1_ref[4:5, :]).astype(bf16)
        acc[:, :D] += dot(x1b.T, dq)
        dx1 = dh2 + dot_nt(dq, w[:, :D])
        small_o[3:4, :] += col_sum(dx1 * n1)
        small_o[4:5, :] += col_sum(dx1)
        dh1 = norm_back(dx1, n1, r1, vec1_ref[3:4, :])
        small_o[2:3, :] += col_sum(dh1)
        dh1_o[0] = dh1

    @pl.when(chunk == pl.num_programs(1) - 1)
    def _():
        dv = dvsc[...]
        acc_vec[1:2, :] += col_sum(dv)
        dkv = jnp.concatenate([dksc[...].astype(bf16), dv.astype(bf16)], 1)
        acc[:, D : 3 * D] += dot(m_ref[0].T, dkv)
        gm_o[0] = dot_nt(dkv, w[:, D : 3 * D])

    @pl.when(last)
    def _():
        store_attention(order, gn_o, gf_o, flat, real, acc, acc_vec)


def cross_backward(nch, order, tau, dh2, h1, memory, shift, saved, w, vec1, small2, half, rows, real):
    q, qt, k, kt, v, at, lse = saved
    items, steps, _ = h1.shape
    mem = memory.shape[1]
    chunks = steps // CH

    def row_block(i, c, nch_ref, _):
        return (i, jnp.minimum(c, nch_ref[i] - 1), 0)

    def col_block(i, c, nch_ref, _):
        return (i, 0, jnp.minimum(c, nch_ref[i] - 1))

    per_item = lambda i, c, *_: (i, 0, 0)
    rowspec = pl.BlockSpec((1, CH, D), row_block)
    colspec = pl.BlockSpec((1, D, CH), col_block)
    memspec = pl.BlockSpec((1, mem, D), per_item)
    whole2 = lambda i, c, *_: (0, 0)
    shards = pl.BlockSpec((half, rows, LANES), lambda i, c, *_: (0, 0, 0), pipeline_mode=pl.Buffered(1))
    once = pl.Buffered(1)
    shape = jax.ShapeDtypeStruct
    return pl.pallas_call(
        functools.partial(cross_backward_kernel, real=real),
        grid_spec=pltpu.PrefetchScalarGridSpec(
            num_scalar_prefetch=2,
            grid=(items, chunks),
            in_specs=[
                pl.BlockSpec(memory_space=pltpu.SMEM),
                rowspec, rowspec, memspec,
                pl.BlockSpec((1, 1, mem), per_item),
                rowspec, colspec, memspec,
                pl.BlockSpec((1, D, mem), per_item),
                memspec, colspec,
                pl.BlockSpec((1, HEADS, CH), col_block),
                pl.BlockSpec((D, 4 * D), whole2, pipeline_mode=once),
                pl.BlockSpec((8, D), whole2, pipeline_mode=once),
                pl.BlockSpec((8, D), whole2, pipeline_mode=once),
            ],
            out_specs=[
                rowspec, memspec,
                shards, shards,
                pl.BlockSpec((8, D), whole2, pipeline_mode=once),
            ],
            scratch_shapes=[
                pltpu.VMEM((2 * half * real + 16, LANES), f32),
                pltpu.VMEM((D, 4 * D), f32), pltpu.VMEM((8, D), f32),
                pltpu.VMEM((mem, D), f32), pltpu.VMEM((mem, D), f32),
                pltpu.VMEM((D, CH), bf16),
            ],
        ),
        out_shape=[
            shape((items, steps, D), f32), shape((items, mem, D), f32),
            shape((half, rows, LANES), bf16), shape((half, rows, LANES), bf16), shape((8, D), f32),
        ],
        compiler_params=pltpu.CompilerParams(vmem_limit_bytes=VMEM_LIMIT),
        cost_estimate=pl.CostEstimate(flops=int(8e9), bytes_accessed=int(2e7), transcendentals=0),
        name="cross_backward",
    )(nch, order, tau, dh2, h1, memory, shift, q, qt, k, kt, v, at, lse, w, vec1, small2)


def self_backward_kernel(
    nch, order, tau, dh1_ref, x_ref, q_ref, qt_ref, k_ref, kt_ref, v_ref, at_ref, lse_ref,
    w, small1_ref, gx_o, gn_o, gf_o,
    flat, acc, acc_vec, dksc, dvsc, dqt, *, real, chunks,
):
    item, step = pl.program_id(0), pl.program_id(1)
    chunk = chunks - 1 - step
    first = (item == 0) & (step == 0)
    last = (item == pl.num_programs(0) - 1) & (step == chunks - 1)

    @pl.when(first)
    def _():
        acc[...] = jnp.zeros_like(acc)
        acc_vec[...] = small1_ref[...]

    @pl.when(step == 0)
    def _():
        dksc[...] = jnp.zeros_like(dksc)
        dvsc[...] = jnp.zeros_like(dvsc)

    @pl.when(chunk < nch[item])
    def _():
        factor = tau[item] * (1.0 / math.sqrt(HW))
        scale = tau[item] * (LOG2E / math.sqrt(HW))
        dh1 = dh1_ref[0]
        e1 = dh1.astype(bf16)
        acc[:, 3 * D :] += dot(at_ref[0], e1)
        da = dot_nt(e1, w[:, 3 * D :]).astype(bf16)
        dat = da.T
        qt = qt_ref[0]
        masks = pair_masks((CH, LANES), bf16)
        for at_chunk in range(chunks):

            @pl.when(chunk == at_chunk)
            def _(keys=(at_chunk + 1) * CH):
                for pair in range(HEADS // 2):
                    lanes = slice(pair * LANES, (pair + 1) * LANES)
                    dk_pair, dv_pair = 0.0, 0.0
                    for head in (2 * pair, 2 * pair + 1):
                        rows = slice(head * HW, (head + 1) * HW)
                        part, dk, dv = attend_back(
                            head, pair, k_ref[0, :keys, lanes], v_ref[0, :keys, lanes], kt_ref[0, rows, :keys], qt, dat,
                            q_ref[0, :, lanes], da[:, lanes], lse_ref[0, head : head + 1, :], None, scale, masks, True,
                        )
                        dqt[rows, :] = (part * factor).astype(bf16)
                        dk_pair, dv_pair = dk_pair + dk, dv_pair + dv
                    dksc[:keys, lanes] += dk_pair * factor
                    dvsc[:keys, lanes] += dv_pair

        here = pl.ds(pl.multiple_of(chunk * CH, CH), CH)
        dq = dqt[...].T
        dv = dvsc[here, :]
        acc_vec[0:1, :] += col_sum(dq.astype(f32))
        acc_vec[1:2, :] += col_sum(dv)
        dqkv = jnp.concatenate([dq, dksc[here, :].astype(bf16), dv.astype(bf16)], 1)
        acc[:, : 3 * D] += dot(x_ref[0].T, dqkv)
        gx_o[0] = dh1 + dot_nt(dqkv, w[:, : 3 * D])

    @pl.when(chunk >= nch[item])
    def _():
        gx_o[0] = jnp.zeros((CH, D), f32)

    @pl.when(last)
    def _():
        store_attention(order, gn_o, gf_o, flat, real, acc, acc_vec)


def self_backward(nch, order, tau, dh1, x, saved, w, small1, half, rows, real):
    q, qt, k, kt, v, at, lse = saved
    items, steps, _ = x.shape
    chunks = steps // CH

    def row_block(i, c, nch_ref, _):
        return (i, jnp.minimum(chunks - 1 - c, nch_ref[i] - 1), 0)

    def col_block(i, c, nch_ref, _):
        return (i, 0, jnp.minimum(chunks - 1 - c, nch_ref[i] - 1))

    per_item = lambda i, c, *_: (i, 0, 0)
    rowspec = pl.BlockSpec((1, CH, D), row_block)
    colspec = pl.BlockSpec((1, D, CH), col_block)
    itemspec = pl.BlockSpec((1, steps, D), per_item)
    whole2 = lambda i, c, *_: (0, 0)
    shards = pl.BlockSpec((half, rows, LANES), lambda i, c, *_: (0, 0, 0), pipeline_mode=pl.Buffered(1))
    once = pl.Buffered(1)
    shape = jax.ShapeDtypeStruct
    return pl.pallas_call(
        functools.partial(self_backward_kernel, real=real, chunks=chunks),
        grid_spec=pltpu.PrefetchScalarGridSpec(
            num_scalar_prefetch=2,
            grid=(items, chunks),
            in_specs=[
                pl.BlockSpec(memory_space=pltpu.SMEM),
                rowspec, rowspec, rowspec, colspec, itemspec,
                pl.BlockSpec((1, D, steps), per_item),
                itemspec, colspec,
                pl.BlockSpec((1, HEADS, CH), col_block),
                pl.BlockSpec((D, 4 * D), whole2, pipeline_mode=once),
                pl.BlockSpec((8, D), whole2, pipeline_mode=once),
            ],
            out_specs=[
                pl.BlockSpec((1, CH, D), lambda i, c, *_: (i, chunks - 1 - c, 0)),
                shards, shards,
            ],
            scratch_shapes=[
                pltpu.VMEM((2 * half * real + 16, LANES), f32),
                pltpu.VMEM((D, 4 * D), f32), pltpu.VMEM((8, D), f32),
                pltpu.VMEM((steps, D), f32), pltpu.VMEM((steps, D), f32),
                pltpu.VMEM((D, CH), bf16),
            ],
        ),
        out_shape=[shape((items, steps, D), f32), shape((half, rows, LANES), bf16), shape((half, rows, LANES), bf16)],
        compiler_params=pltpu.CompilerParams(vmem_limit_bytes=VMEM_LIMIT),
        cost_estimate=pl.CostEstimate(flops=int(1.5e10), bytes_accessed=int(2e7), transcendentals=0),
        name="self_backward",
    )(nch, order, tau, dh1, x, q, qt, k, kt, v, at, lse, w, small1)


AXES = ("wide", "narrow")


def after(value, event):
    return lax.optimization_barrier((value, event))[0]


def offsets(narrow, count):
    core, plane = narrow, 4 * narrow
    along_z = list(range(plane, count, plane))
    within = [y * 2 * narrow + x for y in range(2) for x in range(narrow)][1:]
    return along_z, within, core


def slot_owners(narrow, count):
    along_z, within, core = offsets(narrow, count)
    near = [a ^ b for a in [0] + within for b in [0] + along_z]
    return near + [a ^ core for a in near]


def to_rows(shard):
    real = shard.shape[0] // LANES
    padded = (real + 15) // 16 * 16
    return jnp.pad(shard.reshape(real, LANES), ((0, padded - real), (0, 0)))


def from_rows(rows, length):
    return rows[0, : length // LANES].reshape(length)


def add_up(parts):
    return sum(part.astype(f32) for part in parts)


def body(inputs, memory, tau_scale, delta_shift, horizon, self_params, cross_params, dense_params, cotangent):
    narrow = lax.axis_size("narrow")
    count = lax.axis_size(AXES)
    along_z, within, core = offsets(narrow, count)
    depth = 1 + len(along_z)

    def swap(rows, offset):
        return lax.ppermute(rows, AXES, [(i, i ^ offset) for i in range(count)])

    def line_round(piece):
        return [piece[None]] + [swap(piece[None], o) for o in along_z]

    def plane_round(line):
        return [line] + [swap(line, o) for o in within]

    def plane_scatter(mine):
        return [mine[:depth]] + [swap(mine[depth * i : depth * (i + 1)], o) for i, o in enumerate(within, 1)]

    def line_scatter(line):
        return [line[:1]] + [swap(line[i : i + 1], o) for i, o in enumerate(along_z, 1)]

    x, m, ct = inputs[:, 0], memory[:, 0], cotangent[:, 0]
    tau, shift, horizon = tau_scale[:, 0], delta_shift, horizon[:, 0]
    order = lax.axis_index(AXES) ^ jnp.array(slot_owners(narrow, count), jnp.int32)
    steps = x.shape[1]
    nch = jnp.minimum((horizon + (LABEL + CH - 1)) // CH, steps // CH).astype(jnp.int32)
    real_a, real_d = self_params.shape[0] // LANES, dense_params.shape[0] // LANES
    piece_self = to_rows(self_params)
    piece_rest = jnp.concatenate([to_rows(cross_params), to_rows(dense_params)])
    cut = piece_self.shape[0]

    line_self = jnp.concatenate(line_round(piece_self))
    line_rest = line_round(after(piece_rest, line_self))
    near_self = jnp.concatenate(after(plane_round(line_self), line_rest))
    p_self = near_self, swap(near_self, core)
    plane_rest = plane_round(jnp.concatenate(after(line_rest, p_self)))
    q, qt, k, kt, v, at, h1, lse, w1, vec1 = self_forward(nch, order, tau, x, p_self, real_a)
    plane_rest = after(plane_rest, vec1)
    near_cross = jnp.concatenate([p[:, :cut] for p in plane_rest])
    near_dense = jnp.concatenate([p[:, cut:] for p in plane_rest])
    p_cross = near_cross, swap(near_cross, core)
    far_dense = swap(after(near_dense, p_cross), core)
    q2, qt2, k2, kt2, v2, at2, h2, lse2, w2, vec2 = cross_forward(nch, order, tau, h1, m, shift, p_cross, vec1, real_a)
    p_dense = after((near_dense, far_dense), vec2)
    y, dh2, gn_dense, gf_dense, small2 = dense_both(nch, order, horizon, h2, ct, p_dense, vec2, real_d)
    other_dense = swap(gf_dense, core)
    half, rows, _ = near_self.shape
    dh1, gm, gn_cross, gf_cross, small1 = cross_backward(
        nch, order, tau, after(dh2, gf_dense), h1, m, shift, (q2, qt2, k2, kt2, v2, at2, lse2), w2, vec1, small2, half, rows, real_a
    )
    other_cross = swap(gf_cross, core)
    mine_rest = jnp.concatenate(
        [add_up([gn_cross, other_cross]).astype(bf16), add_up([gn_dense, after(other_dense, small1)]).astype(bf16)], 1
    )
    plane_rest = plane_scatter(mine_rest)
    gx, gn_self, gf_self = self_backward(
        nch, order, tau, after(dh1, mine_rest), x, (q, qt, k, kt, v, at, lse), w1, small1, half, rows, real_a
    )
    plane_rest, gf_self = after((plane_rest, gf_self), gn_self)
    other_self = swap(gf_self, core)
    line_rest = line_scatter(add_up(plane_rest).astype(bf16))
    plane_self = plane_scatter(add_up([gn_self, other_self]).astype(bf16))
    line_self = line_scatter(add_up(plane_self).astype(bf16))
    rest = add_up(after(line_rest, line_self))
    return (
        y[:, None], gx[:, None], gm[:, None],
        from_rows(add_up(line_self), self_params.shape[0]),
        from_rows(rest[:, :cut], cross_params.shape[0]),
        from_rows(rest[:, cut:], dense_params.shape[0]),
    )


def solution(mesh):
    items = P(None, AXES, None, None)
    placed = (items, items, P(None, AXES), P(None, AXES, None), P(None, AXES), P(AXES), P(AXES), P(AXES), items)
    return jax.shard_map(
        body, mesh=mesh, in_specs=placed, out_specs=(items, items, items, P(AXES), P(AXES), P(AXES)), check_vma=False
    )
```

```python
import functools
import math

import jax
import jax.numpy as jnp
from jax import lax
from jax.experimental import pallas as pl
from jax.experimental.pallas import tpu as pltpu
from jax.sharding import PartitionSpec as P

D = 512
FF = 2048
HEADS = 8
HW = D // HEADS
LABEL = 48
LANES = 128
CH_BITS = 8
CH = 1 << CH_BITS
PIECES = 32
HALF = PIECES // 2
CORE = 2
SQ = 4 * D // PIECES
FR = 2 * FF // PIECES
IN = D // (PIECES // 2)
TILES = FF // D
VEC = 16
SHARD_ROWS = 257
SHARD_PAD = (SHARD_ROWS + 15) // 16 * 16
EPS = 1e-05
NEG = -1e30
LOG2E = 1.4426950408889634
LIMITS = (48, 0, 48, 40, 44)
ROOT = 1.0 / math.sqrt(HW)
f32, bf16 = jnp.float32, jnp.bfloat16
MIB = 2**20


def dot(a, b):
    return jnp.dot(a, b, preferred_element_type=f32)


def dot_nt(a, b):
    return lax.dot_general(a, b, (((1,), (1,)), ((), ())), preferred_element_type=f32)


def norm_stats(h):
    center = h - jnp.mean(h, -1, keepdims=True)
    rstd = lax.rsqrt(jnp.mean(center * center, -1, keepdims=True) + EPS)
    return center * rstd, rstd


def norm_back(dz, n, rstd, gain):
    dn = dz * gain
    return rstd * (dn - jnp.mean(dn, -1, keepdims=True) - n * jnp.mean(dn * n, -1, keepdims=True))


def col_sum(v):
    return jnp.sum(v, 0, keepdims=True)


def slot_offset(slot):
    return ((slot & 3) << 3) | (((slot >> 3) & 1) << 2) | ((slot >> 2) & 1)


def each_piece(me, near, far):
    for slot in range(HALF):
        who = me[0] ^ slot_offset(slot)
        yield slot, who, near, slot
        yield HALF + slot, who ^ CORE, far, slot


def slot_of(me, who):
    away = me[0] ^ who
    return (((away >> 2) & 1) * 2 + (away & 1)) * 4 + (away >> 3), (away & CORE) != 0


def either(is_far, near_copy, far_copy):
    pl.when(jnp.logical_not(is_far))(near_copy.start)
    pl.when(is_far)(far_copy.start)


def load_shards(me, near, far, first, flat, w, vec):
    for _, who, ref, slot in each_piece(me, near, far):
        flat[pl.ds(who * SHARD_ROWS, SHARD_ROWS), :] = ref[slot, first : first + SHARD_ROWS, :].astype(f32)
    per = D // LANES
    for j in range(per):
        w[:, j * LANES : (j + 1) * LANES] = flat[pl.ds(j, 4 * D, stride=per), :].astype(bf16)
    vec[...] = jnp.zeros_like(vec)
    for i in range(5):
        for j in range(per):
            at = 4 * D * per + i * per + j
            vec[i : i + 1, j * LANES : (j + 1) * LANES] = flat[at : at + 1, :]


def store_shards(me, near, far, flat, acc, vec):
    per = D // LANES
    for m in range(4):
        for j in range(per):
            flat[pl.ds(m * D * per + j, D, stride=per), :] = acc[m, :, j * LANES : (j + 1) * LANES]
    start = 4 * D * per
    flat[start:, :] = jnp.zeros((flat.shape[0] - start, LANES), f32)
    for i in range(5):
        for j in range(per):
            flat[start + i * per + j : start + i * per + j + 1, :] = vec[i : i + 1, j * LANES : (j + 1) * LANES]
    rows = near.shape[1]

    @pl.loop(0, HALF)
    def _(slot):
        who = me[0] ^ slot_offset(slot)
        near[slot] = flat[pl.ds(who * SHARD_ROWS, rows), :].astype(bf16)
        far[slot] = flat[pl.ds((who ^ CORE) * SHARD_ROWS, rows), :].astype(bf16)


def head_rows(head):
    return slice(head * HW, (head + 1) * HW)


def pair_lanes(head):
    return slice(head // 2 * LANES, (head // 2 + 1) * LANES)


def head_rhs(block, head):
    zero = jnp.zeros_like(block)
    return jnp.concatenate([block, zero] if head % 2 == 0 else [zero, block], 0)


def one_head(rows, head):
    lane = lax.broadcasted_iota(jnp.int32, rows.shape, 1)
    return jnp.where((lane < HW) == (head % 2 == 0), rows, jnp.zeros_like(rows))


def causal_cut(scores, fill):
    keys = scores.shape[0]
    tail = scores[keys - CH :, :]
    key_at = lax.broadcasted_iota(jnp.int32, tail.shape, 0)
    query_at = lax.broadcasted_iota(jnp.int32, tail.shape, 1)
    tail = jnp.where(key_at <= query_at, tail, fill)
    return tail if keys == CH else jnp.concatenate([scores[: keys - CH, :], tail], 0)


def shift_column(shift_ref):
    row = shift_ref[0] * (LOG2E * ROOT)
    return jnp.broadcast_to(row, (8, row.shape[1])).T[:, :1]


def attend(s, values_t):
    top = jnp.max(s, 0, keepdims=True)
    e = jnp.exp2(s - top)
    total = jnp.sum(e, 0, keepdims=True)
    mixed = dot(values_t, e.astype(bf16))
    return (mixed * (1.0 / total)).astype(bf16), top + jnp.log2(total)


def head_inner(da_t, a_t):
    return jnp.sum(da_t.astype(f32) * a_t.astype(f32), 0, keepdims=True)


def chunk_count(horizon, item, chunks):
    return jnp.minimum(lax.shift_right_logical(horizon[item] + (LABEL + CH - 1), CH_BITS), chunks)


def by_rows(horizon, item, chunks, rows_of):
    count = chunk_count(horizon, item, chunks)
    for n in range(1, chunks + 1):
        pl.when(count == n)(functools.partial(rows_of, n * CH))


class Outbox:
    def __init__(self, pairs, sems):
        self.pairs, self.sems = pairs, sems

    def copy(self, name, item):
        index = list(self.pairs).index(name)
        src, dst = self.pairs[name]
        return pltpu.make_async_copy(src.at[item], dst.at[item], self.sems.at[item, index])

    def send(self, name, item):
        self.copy(name, item).start()

    def close(self, items):
        for item in range(items):
            for name in self.pairs:
                self.copy(name, item).wait()


def vmem(*shape, dtype=f32):
    return pltpu.VMEM(shape, dtype)


def call(kernel, name, items, prefetch, ins, outs, scratch, limit, flops):
    return pl.pallas_call(
        kernel,
        grid_spec=pltpu.PrefetchScalarGridSpec(
            num_scalar_prefetch=len(prefetch),
            grid=(items,),
            in_specs=[spec for _, spec in ins],
            out_specs=[spec for _, spec in outs],
            scratch_shapes=scratch,
        ),
        out_shape=[shape for shape, _ in outs],
        compiler_params=pltpu.CompilerParams(vmem_limit_bytes=limit * MIB),
        cost_estimate=pl.CostEstimate(flops=int(flops), bytes_accessed=int(2e7), transcendentals=0),
        name=name,
    )(*prefetch, *[array for array, _ in ins])


def any_spec():
    return pl.BlockSpec(memory_space=pl.ANY)


def item_spec(*shape):
    return pl.BlockSpec((1, *shape), lambda i, *_: (i, *[0] * len(shape)))


def whole_spec(*shape):
    return pl.BlockSpec(shape, lambda i, *_: (0,) * len(shape), pipeline_mode=pl.Buffered(1))


def kept(*shape, dtype=bf16):
    return pltpu.HBM(shape, dtype)


shape_of = jax.ShapeDtypeStruct


def attention_forward_kernel(
    horizon, me, tau, x_ref, m_ref, shift_ref, pn_ref, pf_ref,
    q_o, k_o, v_o, at_o, h1_o, w1_o, q2_o, at2_o, h2_o, w2_o, k2_o, v2_o, lse_o, lse2_o, vec1_o, vec2_o,
    flat, w, w2, vt, qt, vt2, q, k, v, at, h1, q2, at2, h2, sems, w_sems, *, chunks,
):
    item = pl.program_id(0)
    box = Outbox(
        {
            "q": (q, q_o), "k": (k, k_o), "v": (v, v_o), "at": (at, at_o), "h1": (h1, h1_o),
            "q2": (q2, q2_o), "at2": (at2, at2_o), "h2": (h2, h2_o),
        },
        sems,
    )
    w_copies = [pltpu.make_async_copy(a, b, w_sems.at[i]) for i, (a, b) in enumerate(((w, w1_o), (w2, w2_o)))]

    @pl.when(item == 0)
    def _():
        load_shards(me, pn_ref, pf_ref, 0, flat, w, vec1_o)
        w_copies[0].start()
        load_shards(me, pn_ref, pf_ref, SHARD_PAD, flat, w2, vec2_o)
        w_copies[1].start()

    k2_o[0] = dot(m_ref[0], w2[D : 2 * D]).astype(bf16)
    v2_o[0] = (dot(m_ref[0], w2[2 * D : 3 * D]) + vec2_o[1:2, :]).astype(bf16)
    vt2[...] = v2_o[0].T

    def rows_of(n):
        scale = tau[item] * (LOG2E * ROOT)
        x = x_ref[0, :n]
        q[item, :n] = (dot(x, w[:D]) + vec1_o[0:1, :]).astype(bf16)
        box.send("q", item)
        k[item, :n] = dot(x, w[D : 2 * D]).astype(bf16)
        box.send("k", item)
        v[item, :n] = (dot(x, w[2 * D : 3 * D]) + vec1_o[1:2, :]).astype(bf16)
        box.send("v", item)
        qt[:, :n] = q[item, :n].T
        vt[:, :n] = v[item, :n].T
        for start in range(0, n, CH):
            keys, here = start + CH, slice(start, start + CH)
            for head in range(HEADS):
                rows = head_rows(head)
                s = causal_cut(dot(k[item, :keys, pair_lanes(head)], head_rhs(qt[rows, here], head)) * scale, NEG)
                at[item, rows, here], lse_o[0, head : head + 1, here] = attend(s, vt[rows, :keys])
        box.send("at", item)
        hidden = x.astype(f32) + dot(at[item, :, :n].T, w[3 * D :]) + vec1_o[2:3, :]
        h1[item, :n] = hidden
        box.send("h1", item)

        shift = shift_column(shift_ref)
        n1, _ = norm_stats(hidden)
        x1 = n1 * vec1_o[3:4, :] + vec1_o[4:5, :]
        h2[item, :n] = x1
        q2[item, :n] = (dot(x1.astype(bf16), w2[:D]) + vec2_o[0:1, :]).astype(bf16)
        box.send("q2", item)
        qt[:, :n] = q2[item, :n].T
        for head in range(HEADS):
            rows = head_rows(head)
            s = dot(k2_o[0, :, pair_lanes(head)], head_rhs(qt[rows, :n], head)) * scale + shift
            at2[item, rows, :n], lse2_o[0, head : head + 1, :n] = attend(s, vt2[rows, :])
        box.send("at2", item)
        h2[item, :n] += dot(at2[item, :, :n].T, w2[3 * D :]) + vec2_o[2:3, :]
        box.send("h2", item)

    by_rows(horizon, item, chunks, rows_of)

    @pl.when(item == pl.num_programs(0) - 1)
    def _():
        box.close(2)
        for copy in w_copies:
            copy.wait()


def attention_forward(horizon, me, tau, x, memory, shift, params):
    items, steps, _ = x.shape
    mem = memory.shape[1]
    half, rows, _ = params[0].shape
    row, col = (items, steps, D), (items, D, steps)
    shards, memo, lses = whole_spec(half, rows, LANES), item_spec(mem, D), item_spec(HEADS, steps)
    saved = lambda *shape: (kept(*shape), any_spec())
    return call(
        functools.partial(attention_forward_kernel, chunks=steps // CH), "attention_forward", items, (horizon, me),
        [
            (tau, pl.BlockSpec(memory_space=pltpu.SMEM)), (x, item_spec(steps, D)), (memory, memo), (shift, item_spec(1, mem)),
            (params[0], shards), (params[1], shards),
        ],
        [
            saved(*row), saved(*row), saved(*row), saved(*col), (kept(*row, dtype=f32), any_spec()), saved(4 * D, D),
            saved(*row), saved(*col), (shape_of(row, f32), any_spec()), saved(4 * D, D),
            (shape_of((items, mem, D), bf16), memo), (shape_of((items, mem, D), bf16), memo),
            (shape_of((items, HEADS, steps), f32), lses), (shape_of((items, HEADS, steps), f32), lses),
            (shape_of((8, D), f32), whole_spec(8, D)), (shape_of((8, D), f32), whole_spec(8, D)),
        ],
        [
            vmem(PIECES * SHARD_ROWS + 16, LANES), vmem(4 * D, D, dtype=bf16), vmem(4 * D, D, dtype=bf16),
            vmem(D, steps, dtype=bf16), vmem(D, steps, dtype=bf16), vmem(D, mem, dtype=bf16),
            vmem(*row, dtype=bf16), vmem(*row, dtype=bf16), vmem(*row, dtype=bf16), vmem(*col, dtype=bf16), vmem(*row),
            vmem(*row, dtype=bf16), vmem(*col, dtype=bf16), vmem(*row),
            pltpu.SemaphoreType.DMA((2, 8)), pltpu.SemaphoreType.DMA((2,)),
        ],
        LIMITS[0], 1.2e10,
    )


def dense_kernel(
    horizon, me, horizon_at, h_ref, ct_ref, vec2_ref, pn_ref, pf_ref, y_o, dh_o, gn_o, gf_o, small_o,
    w_in, w_out, vecb, vec_sc, bias, acc_in, acc_out, acc_bias, f_sc, gp_sc, y, dh, out, sems, p_sems, vec_sem, *, chunks,
):
    item = pl.program_id(0)
    box = Outbox({"y": (y, y_o), "dh": (dh, dh_o)}, sems)
    out_row, gain_row = 8 + TILES, 8 + TILES + 1
    vec = lambda i: vec_sc[i : i + 1, :]

    def fetch(who, ref, slot):
        if who >= HALF:
            pieces = [(0, FR, w_out.at[pl.ds((who - HALF) * FR, FR), :])]
        else:
            pieces = [
                (part * IN, IN, w_in.at[pl.ds(who * IN, IN), pl.ds(part * D, D)]) for part in range(TILES)
            ]
        for start, size, place in pieces:
            pltpu.make_async_copy(ref.at[slot, pl.ds(start, size), :], place, p_sems.at[who]).start()

    @pl.when(item == 0)
    def _():
        for who in range(PIECES):
            slot, is_far = slot_of(me, who)
            pl.when(jnp.logical_not(is_far))(functools.partial(fetch, who, pn_ref, slot))
            pl.when(is_far)(functools.partial(fetch, who, pf_ref, slot))
        vec_copies = [
            pltpu.make_async_copy(ref.at[slot, pl.ds(FR, VEC), :], vecb, vec_sem) for ref in (pn_ref, pf_ref)
        ]
        either(is_far, *vec_copies)
        acc_in[...] = jnp.zeros_like(acc_in)
        acc_out[...] = jnp.zeros_like(acc_out)
        acc_bias[...] = jnp.zeros_like(acc_bias)
        small_o[...] = jnp.zeros_like(small_o)
        vec_copies[0].wait()
        vec_sc[...] = vecb[:8].astype(f32)
        for part in range(TILES):
            bias[:, part * D : (part + 1) * D] = vec(part)
        for who in range(PIECES):
            pltpu.make_async_copy(pf_ref.at[0, pl.ds(0, FR), :], w_out.at[pl.ds(0, FR), :], p_sems.at[who]).wait()

    def add(row, value):
        small_o[row : row + 1, :] += value

    y[item] = jnp.zeros(y.shape[1:], bf16)

    @pl.loop(0, chunk_count(horizon, item, chunks))
    def _(chunk):
        here = pl.ds(pl.multiple_of(chunk * CH, CH), CH)
        n2, r2 = norm_stats(h_ref[0, here])
        x2 = n2 * vec2_ref[3:4, :] + vec2_ref[4:5, :]
        x2b = x2.astype(bf16)
        u = dot(x2b, w_in[...]) + bias[...]
        cdf = 0.5 * (1.0 + lax.erf(u * 0.7071067811865476))
        f_sc[...] = (u * cdf).astype(bf16)
        gp_sc[...] = cdf + u * jnp.exp(u * u * -0.5) * (1.0 / math.sqrt(2.0 * math.pi))
        n3, r3 = norm_stats(x2 + dot(f_sc[...], w_out[...]) + vec(TILES))
        at = lax.broadcasted_iota(jnp.int32, (CH, 1), 0) + chunk * CH
        valid = (at < LABEL + horizon_at[item]).astype(f32)
        y[item, here] = ((n3 * vec(TILES + 1) + vec(TILES + 2)) * valid).astype(bf16)
        dy = ct_ref[0, here].astype(f32) * valid
        add(gain_row, col_sum(dy * n3))
        add(gain_row + 1, col_sum(dy))
        dh3 = norm_back(dy, n3, r3, vec(TILES + 1))
        add(out_row, col_sum(dh3))
        e3 = dh3.astype(bf16)
        acc_out[...] += dot(e3.T, f_sc[...])
        du = dot_nt(e3, w_out[...]) * gp_sc[...]
        acc_bias[...] += col_sum(du)
        eu = du.astype(bf16)
        acc_in[...] += dot(x2b.T, eu)
        dx2 = dh3 + dot_nt(eu, w_in[...])
        add(3, col_sum(dx2 * n2))
        add(4, col_sum(dx2))
        dh2 = norm_back(dx2, n2, r2, vec2_ref[3:4, :])
        add(2, col_sum(dh2))
        dh[item, here] = dh2

    box.send("y", item)
    box.send("dh", item)

    @pl.when(item == pl.num_programs(0) - 1)
    def _():
        for part in range(TILES):
            add(8 + part, acc_bias[:, part * D : (part + 1) * D])
        for who in range(PIECES):
            if who < HALF:
                for part in range(TILES):
                    out[who, part * IN : (part + 1) * IN, :] = acc_in[
                        who * IN : (who + 1) * IN, part * D : (part + 1) * D
                    ].astype(bf16)
            else:
                out[who] = acc_out[:, (who - HALF) * FR : (who - HALF + 1) * FR].astype(bf16).T
            slot, is_far = slot_of(me, who)
            either(
                is_far,
                pltpu.make_async_copy(out.at[who], gn_o.at[slot], p_sems.at[who]),
                pltpu.make_async_copy(out.at[who], gf_o.at[slot], p_sems.at[who]),
            )
        box.close(2)
        for who in range(PIECES):
            pltpu.make_async_copy(out.at[who], gf_o.at[0], p_sems.at[who]).wait()


def dense_both(horizon, me, h2, ct, vec2, params):
    items, steps, _ = h2.shape
    row, grads = (items, steps, D), shape_of((HALF, FR, D), bf16)
    return call(
        functools.partial(dense_kernel, chunks=steps // CH), "dense_both", items, (horizon, me),
        [
            (horizon, pl.BlockSpec(memory_space=pltpu.SMEM)), (h2, item_spec(steps, D)), (ct, item_spec(steps, D)),
            (vec2, whole_spec(8, D)), (params[0], any_spec()), (params[1], any_spec()),
        ],
        [
            (kept(*row), any_spec()), (shape_of(row, f32), any_spec()), (grads, any_spec()), (grads, any_spec()),
            (shape_of((VEC, D), f32), whole_spec(VEC, D)),
        ],
        [
            vmem(D, FF, dtype=bf16), vmem(FF, D, dtype=bf16), vmem(VEC, D, dtype=bf16), vmem(8, D), vmem(1, FF), vmem(D, FF), vmem(D, FF), vmem(1, FF),
            vmem(CH, FF, dtype=bf16), vmem(CH, FF),
            vmem(*row, dtype=bf16), vmem(*row), vmem(PIECES, FR, D, dtype=bf16), pltpu.SemaphoreType.DMA((2, 2)), pltpu.SemaphoreType.DMA((PIECES,)),
            pltpu.SemaphoreType.DMA,
        ],
        LIMITS[2], 2e10,
    )


def head_back(keys, values, keys_t, qt, q_rows, dat, da_rows, lse, inner, scale, shift, head, causal):
    s = dot(keys, head_rhs(qt, head)) * scale - lse
    if shift is not None:
        s = s + shift
    weights = jnp.exp2(s)
    if causal:
        weights = causal_cut(weights, 0.0)
    g = (weights * (dot(values, head_rhs(dat, head)) - inner)).astype(bf16)
    return dot(keys_t, g), dot(g, one_head(q_rows, head)), dot(weights.astype(bf16), one_head(da_rows, head))


def cross_backward_kernel(
    horizon, me, tau, dh_ref, h1_ref, m_ref, shift_ref, q_ref, k_ref, v_ref, at_ref, lse_ref, w, vec1_ref, small2_ref,
    dh_o, gn_o, gf_o, gm_o, small_o,
    acc, tail, da, dat, qt, kt, dqt, dk, dv, dh, out, sems, p_sems, *, chunks,
):
    item = pl.program_id(0)
    last = item == pl.num_programs(0) - 1
    box = Outbox({"dh": (dh, dh_o)}, sems)
    matrix = lambda m: w[m * D : (m + 1) * D]

    @pl.when(item == 0)
    def _():
        acc[...] = jnp.zeros_like(acc)
        tail[...] = small2_ref[...]
        small_o[...] = jnp.zeros_like(small_o)

    factor = tau[item] * ROOT
    kt[...] = k_ref[0].T

    def rows_of(n):
        scale = tau[item] * (LOG2E * ROOT)
        shift = shift_column(shift_ref)
        e2 = dh_ref[0, :n].astype(bf16)
        acc[3] += dot(at_ref[0, :, :n], e2)
        da[:n] = dot_nt(e2, matrix(3)).astype(bf16)
        dat[:, :n] = da[:n].T
        qt[:, :n] = q_ref[0, :n].T
        for pair in range(HEADS // 2):
            lanes = pair_lanes(2 * pair)
            dk_pair, dv_pair = 0.0, 0.0
            for head in (2 * pair, 2 * pair + 1):
                rows = head_rows(head)
                part, dk_head, dv_head = head_back(
                    k_ref[0, :, lanes], v_ref[0, :, lanes], kt[rows, :], qt[rows, :n], q_ref[0, :n, lanes],
                    dat[rows, :n], da[:n, lanes], lse_ref[0, head : head + 1, :n],
                    head_inner(dat[rows, :n], at_ref[0, rows, :n]), scale, shift, head, False,
                )
                dqt[rows, :n] = (part * factor).astype(bf16)
                dk_pair, dv_pair = dk_pair + dk_head, dv_pair + dv_head
            dk[:, lanes] = (dk_pair * factor).astype(bf16)
            dv[:, lanes] = dv_pair
        dq = dqt[:, :n].T
        tail[0:1, :] += col_sum(dq.astype(f32))
        n1, r1 = norm_stats(h1_ref[0, :n])
        x1b = (n1 * vec1_ref[3:4, :] + vec1_ref[4:5, :]).astype(bf16)
        acc[0] += dot(x1b.T, dq)
        dx1 = dh_ref[0, :n] + dot_nt(dq, matrix(0))
        small_o[3:4, :] += col_sum(dx1 * n1)
        small_o[4:5, :] += col_sum(dx1)
        dh1 = norm_back(dx1, n1, r1, vec1_ref[3:4, :])
        small_o[2:3, :] += col_sum(dh1)
        dh[item, :n] = dh1
        box.send("dh", item)

    by_rows(horizon, item, chunks, rows_of)

    tail[1:2, :] += col_sum(dv[...])
    dvb = dv[...].astype(bf16)
    mt = m_ref[0].T
    acc[1] += dot(mt, dk[...])
    acc[2] += dot(mt, dvb)
    gm_o[0] = dot_nt(dk[...], matrix(1)) + dot_nt(dvb, matrix(2))

    @pl.when(last)
    def _():
        for m in range(4):
            out[m * 8 : (m + 1) * 8, :SQ, :] = acc[m].astype(bf16).reshape(8, SQ, D)
        out[:, SQ:, :] = jnp.broadcast_to(tail[...].astype(bf16)[None], (PIECES, VEC, D))
        sent = []
        for index, who, ref, slot in each_piece(me, gn_o, gf_o):
            sent.append(pltpu.make_async_copy(out.at[who], ref.at[slot], p_sems.at[index]))
            sent[-1].start()
        box.close(2)
        for copy in sent:
            copy.wait()


def cross_backward(horizon, me, tau, dh2, h1, memory, shift, saved, w, vec1, small2):
    q, k, v, at, lse = saved
    items, steps, _ = h1.shape
    mem = memory.shape[1]
    row, grads = (items, steps, D), shape_of((HALF, SQ + VEC, D), bf16)
    memo, rows, cols = item_spec(mem, D), item_spec(steps, D), item_spec(D, steps)
    return call(
        functools.partial(cross_backward_kernel, chunks=steps // CH), "cross_backward", items, (horizon, me),
        [
            (tau, pl.BlockSpec(memory_space=pltpu.SMEM)), (dh2, rows), (h1, rows), (memory, memo), (shift, item_spec(1, mem)),
            (q, rows), (k, memo), (v, memo), (at, cols), (lse, item_spec(HEADS, steps)),
            (w, whole_spec(4 * D, D)), (vec1, whole_spec(8, D)), (small2, whole_spec(VEC, D)),
        ],
        [
            (shape_of(row, f32), any_spec()), (grads, any_spec()), (grads, any_spec()),
            (shape_of((items, mem, D), f32), memo), (shape_of((8, D), f32), whole_spec(8, D)),
        ],
        [
            vmem(4, D, D), vmem(VEC, D),
            vmem(steps, D, dtype=bf16), vmem(D, steps, dtype=bf16), vmem(D, steps, dtype=bf16), vmem(D, mem, dtype=bf16),
            vmem(D, steps, dtype=bf16), vmem(mem, D, dtype=bf16), vmem(mem, D), vmem(*row), vmem(PIECES, SQ + VEC, D, dtype=bf16),
            pltpu.SemaphoreType.DMA((2, 1)), pltpu.SemaphoreType.DMA((PIECES,)),
        ],
        LIMITS[3], 8e9,
    )


def self_backward_kernel(
    horizon, me, tau, dh_ref, x_ref, q_ref, k_ref, v_ref, at_ref, lse_ref, w, small1_ref,
    gx_o, gn_o, gf_o,
    flat, acc, tail, da, dat, qt, kt, xt, dqt, dqsc, dksc, dvsc, gx, sems, *, chunks,
):
    item = pl.program_id(0)
    box = Outbox({"gx": (gx, gx_o)}, sems)

    @pl.when(item == 0)
    def _():
        acc[...] = jnp.zeros_like(acc)
        tail[...] = small1_ref[...]

    factor = tau[item] * ROOT
    scale = tau[item] * (LOG2E * ROOT)

    count = chunk_count(horizon, item, chunks)

    def rows_at(chunk):
        return pl.ds(pl.multiple_of(chunk * CH, CH), CH)

    def before(here):
        e1 = dh_ref[0, here].astype(bf16)
        acc[3] += dot(at_ref[0, :, here], e1)
        da[here] = dot_nt(e1, w[3 * D :]).astype(bf16)
        dat[:, here] = da[here].T
        qt[:, here] = q_ref[0, here].T
        kt[:, here] = k_ref[0, here].T
        xt[:, here] = x_ref[0, here].T

    def behind(here):
        dq = dqsc[here]
        dk = (dksc[here] * factor).astype(bf16)
        dv = dvsc[here]
        tail[0:1, :] += col_sum(dq.astype(f32))
        tail[1:2, :] += col_sum(dv)
        dv = dv.astype(bf16)
        gx[item, here] = dh_ref[0, here] + dot_nt(dq, w[:D]) + dot_nt(dk, w[D : 2 * D]) + dot_nt(dv, w[2 * D : 3 * D])
        acc[0] += dot(xt[:, here], dq)
        acc[1] += dot(xt[:, here], dk)
        acc[2] += dot(xt[:, here], dv)

    def on_rows(step):
        pl.when(count == chunks)(lambda: step(slice(0, chunks * CH)))

        @pl.when(count < chunks)
        def _():
            pl.loop(0, count)(lambda chunk: step(rows_at(chunk)))

    on_rows(before)

    @pl.loop(0, count)
    def _(turn):
        chunk = count - 1 - turn
        here = rows_at(chunk)
        for at_chunk in range(chunks):

            @pl.when(chunk == at_chunk)
            def _(keys=(at_chunk + 1) * CH):
                @pl.loop(0, 2)
                def _(group):
                    for pair in range(HEADS // 4):
                        start = group * (D // 2) + pair * LANES
                        lanes = pl.ds(pl.multiple_of(start, LANES), LANES)
                        dk_pair, dv_pair = 0.0, 0.0
                        for head in range(2):
                            rows = pl.ds(pl.multiple_of(start + head * HW, HW), HW)
                            index = pl.ds(group * (HEADS // 2) + 2 * pair + head, 1)
                            part, dk_head, dv_head = head_back(
                                k_ref[0, :keys, lanes], v_ref[0, :keys, lanes], kt[rows, :keys], qt[rows, here],
                                q_ref[0, here, lanes], dat[rows, here], da[here, lanes], lse_ref[0, index, here],
                                head_inner(dat[rows, here], at_ref[0, rows, here]), scale, None, head, True,
                            )
                            dqt[rows, :] = (part * factor).astype(bf16)
                            dk_pair, dv_pair = dk_pair + dk_head, dv_pair + dv_head
                        dksc[:keys, lanes] = jnp.where(turn == 0, 0.0, dksc[:keys, lanes]) + dk_pair
                        dvsc[:keys, lanes] = jnp.where(turn == 0, 0.0, dvsc[:keys, lanes]) + dv_pair

        dqsc[here, :] = dqt[...].T

    gx[item] = jnp.zeros(gx.shape[1:], f32)
    on_rows(behind)
    box.send("gx", item)

    @pl.when(item == pl.num_programs(0) - 1)
    def _():
        store_shards(me, gn_o, gf_o, flat, acc, tail)
        box.close(2)


def self_backward(horizon, me, tau, dh1, x, saved, w, small1):
    q, k, v, at, lse = saved
    items, steps, _ = x.shape
    half, shard = HALF, SHARD_PAD
    row, grads = (items, steps, D), shape_of((half, shard, LANES), bf16)
    rows, cols = item_spec(steps, D), item_spec(D, steps)
    return call(
        functools.partial(self_backward_kernel, chunks=steps // CH), "self_backward", items, (horizon, me),
        [
            (tau, pl.BlockSpec(memory_space=pltpu.SMEM)), (dh1, rows), (x, rows), (q, rows), (k, rows), (v, rows), (at, cols),
            (lse, item_spec(HEADS, steps)), (w, whole_spec(4 * D, D)), (small1, whole_spec(8, D)),
        ],
        [(kept(*row, dtype=f32), any_spec()), (grads, whole_spec(half, shard, LANES)), (grads, whole_spec(half, shard, LANES))],
        [
            vmem(PIECES * SHARD_ROWS + 16, LANES), vmem(4, D, D), vmem(8, D),
            vmem(steps, D, dtype=bf16), vmem(D, steps, dtype=bf16), vmem(D, steps, dtype=bf16), vmem(D, steps, dtype=bf16),
            vmem(D, steps, dtype=bf16), vmem(D, CH, dtype=bf16), vmem(steps, D, dtype=bf16),
            vmem(steps, D), vmem(steps, D), vmem(*row), pltpu.SemaphoreType.DMA((2, 1)),
        ],
        LIMITS[4], 1.5e10,
    )


AXES = ("wide", "narrow")
ALONG_Z = (8, 16, 24)
WITHIN = (1, 4, 5)
DEPTH = 4
TAIL = 32


def after(value, event):
    return lax.optimization_barrier((value, event))[0]


def swap(rows, offset):
    return lax.ppermute(rows, AXES, [(i, i ^ offset) for i in range(PIECES)])


def from_device(rows, step):
    return lax.ppermute(rows, AXES, [((i + step) % PIECES, i) for i in range(PIECES)])


def line_round(piece):
    return [piece[None]] + [swap(piece[None], o) for o in ALONG_Z]


def plane_round(line):
    return [line] + [swap(line, o) for o in WITHIN]


def plane_scatter(mine):
    return [mine[:DEPTH]] + [swap(mine[DEPTH * i : DEPTH * (i + 1)], o) for i, o in enumerate(WITHIN, 1)]


def line_scatter(line):
    return [line[:1]] + [swap(line[i : i + 1], o) for i, o in enumerate(ALONG_Z, 1)]


def add_up(parts):
    return sum(part.astype(f32) for part in parts)


def turned(rows, away):
    if away:
        return rows.reshape(IN, TILES, D).transpose(1, 0, 2).reshape(FR, D)
    return rows.reshape(TILES, IN, D).transpose(1, 0, 2).reshape(FR, D)


def raw_piece(shard):
    return jnp.pad(shard.reshape(-1, LANES), ((0, SHARD_PAD - SHARD_ROWS), (0, 0)))


def dense_piece(shard, who):
    rows = shard.reshape(-1, LANES)
    tail = rows[-TAIL:]
    joined = jnp.concatenate([from_device(tail, -1), rows])
    main = lax.dynamic_slice_in_dim(joined, TAIL - who, rows.shape[0] - 1).reshape(FR, D)
    main = jnp.where(who < HALF, turned(main, True), main)
    return jnp.pad(jnp.concatenate([main, tail.reshape(VEC // 2, D)]), ((0, VEC // 2), (0, 0)))


def rest_shards(rest, who):
    cross, vectors, dense = rest[:SQ], rest[SQ : SQ + VEC], rest[SQ + VEC :]
    dense = jnp.where(who < HALF, turned(dense, False), dense)
    ahead = from_device(jnp.concatenate([cross[: VEC // 2], dense[: VEC // 2]]), 1)
    ahead = jnp.where(who == PIECES - 1, vectors, ahead)
    out = []
    for i, main in enumerate((cross, dense)):
        rows = jnp.concatenate([main, ahead[i * VEC // 2 : (i + 1) * VEC // 2]]).reshape(-1, LANES)
        out.append(lax.dynamic_slice_in_dim(rows, who, main.shape[0] * D // LANES + 1).reshape(-1))
    return out


def body(inputs, memory, tau_scale, delta_shift, horizon, self_params, cross_params, dense_params, cotangent):
    who = lax.axis_index(AXES).astype(jnp.int32)
    me = who[None]
    x, m, ct = inputs[:, 0], memory[:, 0], cotangent[:, 0]
    tau, shift, horizon = tau_scale[:, 0], delta_shift, horizon[:, 0]

    line_both = jnp.concatenate(line_round(jnp.concatenate([raw_piece(self_params), raw_piece(cross_params)])))
    line_dense = line_round(dense_piece(dense_params, who))
    near_both = jnp.concatenate(after(plane_round(line_both), line_dense))
    p_both = near_both, swap(near_both, CORE)
    plane_dense = plane_round(jnp.concatenate(after(line_dense, near_both)))
    q, k, v, at, h1, w1, q2, at2, h2, w2, k2, v2, lse, lse2, vec1, vec2 = attention_forward(
        horizon, me, tau, x, m, shift, p_both
    )
    near_dense = jnp.concatenate(after(plane_dense, vec2))
    p_dense = near_dense, swap(near_dense, CORE)
    y, dh2, gn_dense, gf_dense, small2 = dense_both(horizon, me, h2, ct, vec2, p_dense)
    other_dense = swap(gf_dense, CORE)
    dh1, gn_cross, gf_cross, gm, small1 = cross_backward(
        horizon, me, tau, after(dh2, gf_dense), h1, m, shift, (q2, k2, v2, at2, lse2), w2, vec1, small2
    )
    other_cross = swap(gf_cross, CORE)
    mine_rest = jnp.concatenate(
        [add_up([gn_cross, other_cross]).astype(bf16), add_up([gn_dense, after(other_dense, small1)]).astype(bf16)], 1
    )
    plane_rest = plane_scatter(mine_rest)
    gx, gn_self, gf_self = self_backward(
        horizon, me, tau, after(dh1, mine_rest), x, (q, k, v, at, lse), w1, small1
    )
    plane_rest, gf_self = after((plane_rest, gf_self), gn_self)
    other_self = swap(gf_self, CORE)
    line_rest = line_scatter(add_up(plane_rest).astype(bf16))
    plane_self = plane_scatter(add_up([gn_self, other_self]).astype(bf16))
    line_self = line_scatter(add_up(plane_self).astype(bf16))
    g_cross, g_dense = rest_shards(add_up(after(line_rest, plane_self))[0], who)
    g_self = add_up(line_self)[0, :SHARD_ROWS].reshape(-1)
    return y[:, None], gx[:, None], gm[:, None], g_self, g_cross, g_dense


def general_body(inputs, memory, tau_scale, delta_shift, horizon, self_params, cross_params, dense_params, cotangent):
    x, m, ct = inputs[:, 0], memory[:, 0], cotangent[:, 0]
    tau, shift, horizon = tau_scale[:, 0], delta_shift, horizon[:, 0]
    me = jnp.zeros((1,), jnp.int32)
    near = jnp.array([slot_offset(slot) for slot in range(HALF)], jnp.int32)
    owners = jnp.concatenate([near, near ^ CORE])
    square, tall = 4 * D, 2 * FF
    flat = [lax.all_gather(v, AXES, axis=0, tiled=True) for v in (self_params, cross_params, dense_params)]
    raw = [v[: PIECES * SHARD_ROWS * LANES].reshape(PIECES, SHARD_ROWS, LANES) for v in flat[:2]]
    raw = jnp.concatenate([jnp.pad(v, ((0, 0), (0, SHARD_PAD - SHARD_ROWS), (0, 0))) for v in raw], 1)[owners]
    dense = flat[2][: (tall + VEC) * D].reshape(-1, D)
    parts = dense[:tall].reshape(PIECES, FR, D)
    parts = jnp.concatenate([jax.vmap(lambda rows: turned(rows, True))(parts[:HALF]), parts[HALF:]])
    parts = jnp.concatenate([parts, jnp.broadcast_to(dense[None, tall:], (PIECES, VEC, D))], 1)[owners]
    q, k, v, at, h1, w1, q2, at2, h2, w2, k2, v2, lse, lse2, vec1, vec2 = attention_forward(
        horizon, me, tau, x, m, shift, (raw[:HALF], raw[HALF:])
    )
    y, dh2, gn_dense, gf_dense, small2 = dense_both(horizon, me, h2, ct, vec2, (parts[:HALF], parts[HALF:]))
    dh1, gn_cross, gf_cross, gm, small1 = cross_backward(
        horizon, me, tau, dh2, h1, m, shift, (q2, k2, v2, at2, lse2), w2, vec1, small2
    )
    gx, gn_self, gf_self = self_backward(horizon, me, tau, dh1, x, (q, k, v, at, lse), w1, small1)

    def in_order(near_part, far_part):
        both = jnp.concatenate([near_part, far_part]).astype(f32)
        return jnp.zeros_like(both).at[owners].set(both)

    cross = in_order(gn_cross, gf_cross)
    vectors = cross[PIECES - 1, SQ:]
    dense = in_order(gn_dense, gf_dense)
    dense = jnp.concatenate([jax.vmap(lambda rows: turned(rows, False))(dense[:HALF]), dense[HALF:]])
    wholes = (
        in_order(gn_self, gf_self)[:, :SHARD_ROWS].reshape(-1),
        jnp.concatenate([cross[:, :SQ].reshape(-1), vectors[: VEC // 2].reshape(-1)]),
        jnp.concatenate([dense.reshape(-1), vectors[VEC // 2 :].reshape(-1)]),
    )
    sums = [
        lax.psum_scatter(jnp.pad(v, (0, f.shape[0] - v.shape[0])), AXES, scatter_dimension=0, tiled=True)
        for v, f in zip(wholes, flat)
    ]
    return y[:, None], gx[:, None], gm[:, None], *sums


def solution(mesh):
    items = P(None, AXES, None, None)
    placed = (items, items, P(None, AXES), P(None, AXES, None), P(None, AXES), P(AXES), P(AXES), P(AXES), items)
    fits = dict(mesh.shape) == {"wide": HALF, "narrow": 2}
    return jax.shard_map(
        body if fits else general_body,
        mesh=mesh, in_specs=placed, out_specs=(items, items, items, P(AXES), P(AXES), P(AXES)), check_vma=False,
    )
```

```python
import functools
import math

import jax
import jax.numpy as jnp
from jax import lax
from jax.experimental import pallas as pl
from jax.experimental.pallas import tpu as pltpu
from jax.sharding import PartitionSpec as P

D = 512
FF = 2048
HEADS = 8
HW = D // HEADS
LABEL = 48
LANES = 128
CH_BITS = 8
CH = 1 << CH_BITS
PIECES = 32
HALF = PIECES // 2
CORE = 2
SQ = 4 * D // PIECES
FR = 2 * FF // PIECES
IN = D // (PIECES // 2)
TILES = FF // D
VEC = 16
AHEAD = 8
SQ_OUT = SQ + 16
FR_OUT = FR + 16
SHARD_ROWS = 257
SHARD_PAD = (SHARD_ROWS + 15) // 16 * 16
EPS = 1e-05
NEG = -1e30
LOG2E = 1.4426950408889634
LIMITS = (40, 0, 48, 44, 46)
ROOT = 1.0 / math.sqrt(HW)
f32, bf16 = jnp.float32, jnp.bfloat16
MIB = 2**20


def dot(a, b):
    return jnp.dot(a, b, preferred_element_type=f32)


def dot_nt(a, b):
    return lax.dot_general(a, b, (((1,), (1,)), ((), ())), preferred_element_type=f32)


def norm_stats(h):
    center = h - jnp.mean(h, -1, keepdims=True)
    rstd = lax.rsqrt(jnp.mean(center * center, -1, keepdims=True) + EPS)
    return center * rstd, rstd


def norm_back(dz, n, rstd, gain):
    dn = dz * gain
    return rstd * (dn - jnp.mean(dn, -1, keepdims=True) - n * jnp.mean(dn * n, -1, keepdims=True))


def col_sum(v):
    return jnp.sum(v, 0, keepdims=True)


def slot_offset(slot):
    return ((slot & 3) << 3) | (((slot >> 3) & 1) << 2) | ((slot >> 2) & 1)


def each_piece(me, near, far):
    for slot in range(HALF):
        who = me[0] ^ slot_offset(slot)
        yield slot, who, near, slot
        yield HALF + slot, who ^ CORE, far, slot


def slot_of(me, who):
    away = me[0] ^ who
    return (((away >> 2) & 1) * 2 + (away & 1)) * 4 + (away >> 3), (away & CORE) != 0


def either(is_far, near_copy, far_copy):
    pl.when(jnp.logical_not(is_far))(near_copy.start)
    pl.when(is_far)(far_copy.start)


def load_shards(me, near, far, first, flat, w, vec):
    @pl.loop(0, HALF // 4)
    def _(turn):
        for slot in [turn * 4 + i for i in range(4)]:
            who = me[0] ^ slot_offset(slot)
            for ref, owner in ((near, who), (far, who ^ CORE)):
                flat[pl.ds(owner * SHARD_ROWS, SHARD_ROWS), :] = ref[slot, first : first + SHARD_ROWS, :].astype(f32)

    per = D // LANES
    for j in range(per):
        w[:, j * LANES : (j + 1) * LANES] = flat[pl.ds(j, 4 * D, stride=per), :].astype(bf16)
    vec[...] = jnp.zeros_like(vec)
    for i in range(5):
        for j in range(per):
            at = 4 * D * per + i * per + j
            vec[i : i + 1, j * LANES : (j + 1) * LANES] = flat[at : at + 1, :]


def store_shards(me, near, far, flat, acc, vec):
    per = D // LANES
    for m in range(4):
        for j in range(per):
            flat[pl.ds(m * D * per + j, D, stride=per), :] = acc[m, :, j * LANES : (j + 1) * LANES]
    start = 4 * D * per
    flat[start:, :] = jnp.zeros((flat.shape[0] - start, LANES), f32)
    for i in range(5):
        for j in range(per):
            flat[start + i * per + j : start + i * per + j + 1, :] = vec[i : i + 1, j * LANES : (j + 1) * LANES]
    rows = near.shape[1]

    @pl.loop(0, HALF)
    def _(slot):
        who = me[0] ^ slot_offset(slot)
        near[slot] = flat[pl.ds(who * SHARD_ROWS, rows), :].astype(bf16)
        far[slot] = flat[pl.ds((who ^ CORE) * SHARD_ROWS, rows), :].astype(bf16)


def head_rows(head):
    return slice(head * HW, (head + 1) * HW)


def pair_lanes(head):
    return slice(head // 2 * LANES, (head // 2 + 1) * LANES)


def head_rhs(block, head):
    zero = jnp.zeros_like(block)
    return jnp.concatenate([block, zero] if head % 2 == 0 else [zero, block], 0)


def one_head(rows, head):
    lane = lax.broadcasted_iota(jnp.int32, rows.shape, 1)
    return jnp.where((lane < HW) == (head % 2 == 0), rows, jnp.zeros_like(rows))


def causal_cut(scores, fill):
    keys = scores.shape[0]
    tail = scores[keys - CH :, :]
    key_at = lax.broadcasted_iota(jnp.int32, tail.shape, 0)
    query_at = lax.broadcasted_iota(jnp.int32, tail.shape, 1)
    tail = jnp.where(key_at <= query_at, tail, fill)
    return tail if keys == CH else jnp.concatenate([scores[: keys - CH, :], tail], 0)


def shift_column(shift_ref):
    row = shift_ref[0] * (LOG2E * ROOT)
    return jnp.broadcast_to(row, (8, row.shape[1])).T[:, :1]


def attend_heads(score, shape, values_t):
    following, waiting, out = score(0), None, []

    def finish(head, e, top, total):
        mixed = dot(values_t(head), e)
        out.append(((mixed * (1.0 / total)).astype(bf16), top + jnp.log2(total)))

    for head in range(HEADS):
        raw, following = following, score(head + 1) if head + 1 < HEADS else None
        if waiting is not None:
            finish(head - 1, *waiting)
        s = shape(raw)
        top = jnp.max(s, 0, keepdims=True)
        e = jnp.exp2(s - top)
        waiting = e.astype(bf16), top, jnp.sum(e, 0, keepdims=True)
    finish(HEADS - 1, *waiting)
    return out


def head_inner(da_t, a_t):
    return jnp.sum(da_t.astype(f32) * a_t.astype(f32), 0, keepdims=True)


def chunk_count(horizon, item, chunks):
    return jnp.minimum(lax.shift_right_logical(horizon[item] + (LABEL + CH - 1), CH_BITS), chunks)


class Outbox:
    def __init__(self, pairs, sems):
        self.pairs, self.sems = pairs, sems

    def copy(self, name, item):
        index = list(self.pairs).index(name)
        src, dst = self.pairs[name]
        return pltpu.make_async_copy(src.at[item], dst.at[item], self.sems.at[item, index])

    def send(self, name, item):
        self.copy(name, item).start()

    def close(self, items):
        for item in range(items):
            for name in self.pairs:
                self.copy(name, item).wait()


def vmem(*shape, dtype=f32):
    return pltpu.VMEM(shape, dtype)


def call(kernel, name, items, prefetch, ins, outs, scratch, limit, flops):
    return pl.pallas_call(
        kernel,
        grid_spec=pltpu.PrefetchScalarGridSpec(
            num_scalar_prefetch=len(prefetch),
            grid=(items,),
            in_specs=[spec for _, spec in ins],
            out_specs=[spec for _, spec in outs],
            scratch_shapes=scratch,
        ),
        out_shape=[shape for shape, _ in outs],
        compiler_params=pltpu.CompilerParams(vmem_limit_bytes=limit * MIB),
        cost_estimate=pl.CostEstimate(flops=int(flops), bytes_accessed=int(2e7), transcendentals=0),
        name=name,
    )(*prefetch, *[array for array, _ in ins])


def any_spec():
    return pl.BlockSpec(memory_space=pl.ANY)


def item_spec(*shape):
    return pl.BlockSpec((1, *shape), lambda i, *_: (i, *[0] * len(shape)))


def whole_spec(*shape):
    return pl.BlockSpec(shape, lambda i, *_: (0,) * len(shape), pipeline_mode=pl.Buffered(1))


def kept(*shape, dtype=bf16):
    return pltpu.HBM(shape, dtype)


shape_of = jax.ShapeDtypeStruct


def attention_forward_kernel(
    horizon, me, tau, x_ref, m_ref, shift_ref, pn_ref, pf_ref,
    q_o, k_o, v_o, at_o, h1_o, w1_o, q2_o, at2_o, h2_o, w2_o, k2_o, v2_o, lse_o, lse2_o, vec1_o, vec2_o,
    flat, w, w2, vt, qt, vt2, q, k, v, at, h1, q2, at2, h2, sems, w_sems, *, chunks,
):
    item = pl.program_id(0)
    box = Outbox(
        {
            "q": (q, q_o), "k": (k, k_o), "v": (v, v_o), "at": (at, at_o), "h1": (h1, h1_o),
            "q2": (q2, q2_o), "at2": (at2, at2_o), "h2": (h2, h2_o),
        },
        sems,
    )
    w_copies = [pltpu.make_async_copy(a, b, w_sems.at[i]) for i, (a, b) in enumerate(((w, w1_o), (w2, w2_o)))]

    @pl.when(item == 0)
    def _():
        load_shards(me, pn_ref, pf_ref, 0, flat, w, vec1_o)
        w_copies[0].start()
        load_shards(me, pn_ref, pf_ref, SHARD_PAD, flat, w2, vec2_o)
        w_copies[1].start()

    k2_o[0] = dot(m_ref[0], w2[D : 2 * D]).astype(bf16)
    v2_o[0] = (dot(m_ref[0], w2[2 * D : 3 * D]) + vec2_o[1:2, :]).astype(bf16)
    vt2[...] = v2_o[0].T

    def rows_of(n):
        scale = tau[item] * (LOG2E * ROOT)
        x = x_ref[0, :n]
        q[item, :n] = (dot(x, w[:D]) + vec1_o[0:1, :]).astype(bf16)
        box.send("q", item)
        k[item, :n] = dot(x, w[D : 2 * D]).astype(bf16)
        box.send("k", item)
        v[item, :n] = (dot(x, w[2 * D : 3 * D]) + vec1_o[1:2, :]).astype(bf16)
        box.send("v", item)
        qt[:, :n] = q[item, :n].T
        vt[:, :n] = v[item, :n].T
        for start in range(0, n, CH):
            keys, here = start + CH, slice(start, start + CH)
            score = lambda head: dot(k[item, :keys, pair_lanes(head)], head_rhs(qt[head_rows(head), here], head))
            outs = attend_heads(
                score, lambda raw: causal_cut(raw * scale, NEG), lambda head: vt[head_rows(head), :keys]
            )
            for head, (mixed, total) in enumerate(outs):
                at[item, head_rows(head), here], lse_o[0, head : head + 1, here] = mixed, total
        box.send("at", item)
        hidden = x.astype(f32) + dot(at[item, :, :n].T, w[3 * D :]) + vec1_o[2:3, :]
        h1[item, :n] = hidden
        box.send("h1", item)

        shift = shift_column(shift_ref)
        n1, _ = norm_stats(hidden)
        x1 = n1 * vec1_o[3:4, :] + vec1_o[4:5, :]
        h2[item, :n] = x1
        q2[item, :n] = (dot(x1.astype(bf16), w2[:D]) + vec2_o[0:1, :]).astype(bf16)
        box.send("q2", item)
        qt[:, :n] = q2[item, :n].T
        score = lambda head: dot(k2_o[0, :, pair_lanes(head)], head_rhs(qt[head_rows(head), :n], head))
        outs = attend_heads(score, lambda raw: raw * scale + shift, lambda head: vt2[head_rows(head), :])
        for head, (mixed, total) in enumerate(outs):
            at2[item, head_rows(head), :n], lse2_o[0, head : head + 1, :n] = mixed, total
        box.send("at2", item)
        h2[item, :n] += dot(at2[item, :, :n].T, w2[3 * D :]) + vec2_o[2:3, :]
        box.send("h2", item)

    rows_of(chunks * CH)

    @pl.when(item == pl.num_programs(0) - 1)
    def _():
        box.close(2)
        for copy in w_copies:
            copy.wait()


def attention_forward(horizon, me, tau, x, memory, shift, params):
    items, steps, _ = x.shape
    mem = memory.shape[1]
    half, rows, _ = params[0].shape
    row, col = (items, steps, D), (items, D, steps)
    shards, memo, lses = whole_spec(half, rows, LANES), item_spec(mem, D), item_spec(HEADS, steps)
    saved = lambda *shape: (kept(*shape), any_spec())
    return call(
        functools.partial(attention_forward_kernel, chunks=steps // CH), "attention_forward", items, (horizon, me),
        [
            (tau, pl.BlockSpec(memory_space=pltpu.SMEM)), (x, item_spec(steps, D)), (memory, memo), (shift, item_spec(1, mem)),
            (params[0], shards), (params[1], shards),
        ],
        [
            saved(*row), saved(*row), saved(*row), saved(*col), (kept(*row, dtype=f32), any_spec()), saved(4 * D, D),
            saved(*row), saved(*col), (kept(*row, dtype=f32), any_spec()), saved(4 * D, D),
            (shape_of((items, mem, D), bf16), memo), (shape_of((items, mem, D), bf16), memo),
            (shape_of((items, HEADS, steps), f32), lses), (shape_of((items, HEADS, steps), f32), lses),
            (shape_of((8, D), f32), whole_spec(8, D)), (shape_of((8, D), f32), whole_spec(8, D)),
        ],
        [
            vmem(PIECES * SHARD_ROWS + 16, LANES), vmem(4 * D, D, dtype=bf16), vmem(4 * D, D, dtype=bf16),
            vmem(D, steps, dtype=bf16), vmem(D, steps, dtype=bf16), vmem(D, mem, dtype=bf16),
            vmem(*row, dtype=bf16), vmem(*row, dtype=bf16), vmem(*row, dtype=bf16), vmem(*col, dtype=bf16), vmem(*row),
            vmem(*row, dtype=bf16), vmem(*col, dtype=bf16), vmem(*row),
            pltpu.SemaphoreType.DMA((2, 8)), pltpu.SemaphoreType.DMA((2,)),
        ],
        LIMITS[0], 1.2e10,
    )


def dense_kernel(
    horizon, me, horizon_at, h_ref, ct_ref, vec2_ref, pn_ref, pf_ref, y_o, dh_o, gn_o, gf_o, small_o,
    w_in, w, vecb, vec_sc, bias, acc_in, acc_out, acc_bias, f_sc, gp_sc, y, dh, out, sems, p_sems, vec_sem, *, chunks,
):
    item = pl.program_id(0)
    box = Outbox({"y": (y, y_o), "dh": (dh, dh_o)}, sems)
    out_row, gain_row = 8 + TILES, 8 + TILES + 1
    vec = lambda i: vec_sc[i : i + 1, :]

    @pl.when(item == 0)
    def _():
        copies = [
            pltpu.make_async_copy(ref.at[slot, pl.ds(0, FR), :], w.at[who], p_sems.at[index])
            for index, who, ref, slot in each_piece(me, pn_ref, pf_ref)
        ]
        for copy in copies:
            copy.start()
        slot, is_far = slot_of(me, PIECES - 1)
        vec_copies = [
            pltpu.make_async_copy(ref.at[slot, pl.ds(FR, VEC), :], vecb, vec_sem) for ref in (pn_ref, pf_ref)
        ]
        either(is_far, *vec_copies)
        acc_in[...] = jnp.zeros_like(acc_in)
        acc_out[...] = jnp.zeros_like(acc_out)
        acc_bias[...] = jnp.zeros_like(acc_bias)
        small_o[...] = jnp.zeros_like(small_o)
        vec_copies[0].wait()
        vec_sc[...] = vecb[:8].astype(f32)
        for part in range(TILES):
            bias[:, part * D : (part + 1) * D] = vec(part)
        for copy in copies:
            copy.wait()
        for who in range(HALF):
            for part in range(TILES):
                w_in[who * IN : (who + 1) * IN, part * D : (part + 1) * D] = w[who, part * IN : (part + 1) * IN, :]

    w_out = lambda: w[HALF:].reshape(FF, D)

    def add(row, value):
        small_o[row : row + 1, :] += value

    y[item] = jnp.zeros(y.shape[1:], bf16)
    dh[item] = jnp.zeros(dh.shape[1:], f32)

    @pl.loop(0, chunk_count(horizon, item, chunks))
    def _(chunk):
        here = pl.ds(pl.multiple_of(chunk * CH, CH), CH)
        n2, r2 = norm_stats(h_ref[0, here])
        x2 = n2 * vec2_ref[3:4, :] + vec2_ref[4:5, :]
        x2b = x2.astype(bf16)
        u = dot(x2b, w_in[...]) + bias[...]
        cdf = 0.5 * (1.0 + lax.erf(u * 0.7071067811865476))
        f_sc[...] = (u * cdf).astype(bf16)
        gp_sc[...] = cdf + u * jnp.exp(u * u * -0.5) * (1.0 / math.sqrt(2.0 * math.pi))
        n3, r3 = norm_stats(x2 + dot(f_sc[...], w_out()) + vec(TILES))
        at = lax.broadcasted_iota(jnp.int32, (CH, 1), 0) + chunk * CH
        valid = (at < LABEL + horizon_at[item]).astype(f32)
        y[item, here] = ((n3 * vec(TILES + 1) + vec(TILES + 2)) * valid).astype(bf16)
        dy = ct_ref[0, here].astype(f32) * valid
        add(gain_row, col_sum(dy * n3))
        add(gain_row + 1, col_sum(dy))
        dh3 = norm_back(dy, n3, r3, vec(TILES + 1))
        add(out_row, col_sum(dh3))
        e3 = dh3.astype(bf16)
        acc_out[...] += dot(e3.T, f_sc[...])
        du = dot_nt(e3, w_out()) * gp_sc[...]
        acc_bias[...] += col_sum(du)
        eu = du.astype(bf16)
        acc_in[...] += dot(x2b.T, eu)
        dx2 = dh3 + dot_nt(eu, w_in[...])
        add(3, col_sum(dx2 * n2))
        add(4, col_sum(dx2))
        dh2 = norm_back(dx2, n2, r2, vec2_ref[3:4, :])
        add(2, col_sum(dh2))
        dh[item, here] = dh2

    box.send("y", item)
    box.send("dh", item)

    @pl.when(item == pl.num_programs(0) - 1)
    def _():
        for part in range(TILES):
            add(8 + part, acc_bias[:, part * D : (part + 1) * D])
        pad = jnp.zeros((FR_OUT - FR - AHEAD, D), bf16)
        ahead = small_o[8:, :].astype(bf16)
        for who in reversed(range(PIECES)):
            out[who, FR:, :] = jnp.concatenate([ahead, pad], 0)
            if who < HALF:
                for part in range(TILES):
                    out[who, part * IN : (part + 1) * IN, :] = acc_in[
                        who * IN : (who + 1) * IN, part * D : (part + 1) * D
                    ].astype(bf16)
                ahead = jnp.concatenate(
                    [acc_in[who * IN + i : who * IN + i + 1, part * D : (part + 1) * D] for i in range(2) for part in range(TILES)], 0
                ).astype(bf16)
            else:
                turn = acc_out[:, (who - HALF) * FR : (who - HALF + 1) * FR].astype(bf16).T
                out[who, :FR, :] = turn
                ahead = turn[:AHEAD]
            slot, is_far = slot_of(me, who)
            either(
                is_far,
                pltpu.make_async_copy(out.at[who], gn_o.at[slot], p_sems.at[who]),
                pltpu.make_async_copy(out.at[who], gf_o.at[slot], p_sems.at[who]),
            )
        box.close(2)
        for who in range(PIECES):
            pltpu.make_async_copy(out.at[who], gf_o.at[0], p_sems.at[who]).wait()


def dense_both(horizon, me, h2, ct, vec2, params):
    items, steps, _ = h2.shape
    row, grads = (items, steps, D), shape_of((HALF, FR_OUT, D), bf16)
    return call(
        functools.partial(dense_kernel, chunks=steps // CH), "dense_both", items, (horizon, me),
        [
            (horizon, pl.BlockSpec(memory_space=pltpu.SMEM)), (h2, item_spec(steps, D)), (ct, item_spec(steps, D)),
            (vec2, whole_spec(8, D)), (params[0], any_spec()), (params[1], any_spec()),
        ],
        [
            (kept(*row), any_spec()), (shape_of(row, f32), any_spec()), (grads, any_spec()), (grads, any_spec()),
            (shape_of((VEC, D), f32), whole_spec(VEC, D)),
        ],
        [
            vmem(D, FF, dtype=bf16), vmem(PIECES, FR, D, dtype=bf16), vmem(VEC, D, dtype=bf16), vmem(8, D), vmem(1, FF), vmem(D, FF), vmem(D, FF), vmem(1, FF),
            vmem(CH, FF, dtype=bf16), vmem(CH, FF),
            vmem(*row, dtype=bf16), vmem(*row), vmem(PIECES, FR_OUT, D, dtype=bf16), pltpu.SemaphoreType.DMA((2, 2)), pltpu.SemaphoreType.DMA((PIECES,)),
            pltpu.SemaphoreType.DMA,
        ],
        LIMITS[2], 2e10,
    )


def heads_back(count, products, weigh, inner, finish):
    following, waiting, out = products(0), None, []
    for i in range(count):
        (raw, dp), following = following, products(i + 1) if i + 1 < count else None
        if waiting is not None:
            out.append(finish(i - 1, *waiting))
        weights = weigh(i, raw)
        waiting = weights.astype(bf16), (weights * (dp - inner(i))).astype(bf16)
    out.append(finish(count - 1, *waiting))
    return out


def cross_backward_kernel(
    horizon, me, tau, dh_ref, h1_ref, m_ref, shift_ref, q_ref, k_ref, v_ref, at_ref, lse_ref, w, vec1_ref, small2_ref,
    dh_o, gn_o, gf_o, gm_o, small_o,
    acc, tail, da, dat, qt, kt, dqt, dk, dv, dh, out, sems, p_sems, *, chunks,
):
    item = pl.program_id(0)
    last = item == pl.num_programs(0) - 1
    box = Outbox({"dh": (dh, dh_o)}, sems)
    matrix = lambda m: w[m * D : (m + 1) * D]

    @pl.when(item == 0)
    def _():
        acc[...] = jnp.zeros_like(acc)
        tail[...] = small2_ref[...]
        small_o[...] = jnp.zeros_like(small_o)

    factor = tau[item] * ROOT
    kt[...] = k_ref[0].T

    def rows_of(n):
        scale = tau[item] * (LOG2E * ROOT)
        shift = shift_column(shift_ref)
        e2 = dh_ref[0, :n].astype(bf16)
        acc[3] += dot(at_ref[0, :, :n], e2)
        da[:n] = dot_nt(e2, matrix(3)).astype(bf16)
        dat[:, :n] = da[:n].T
        qt[:, :n] = q_ref[0, :n].T

        def products(head):
            lanes, rows = pair_lanes(head), head_rows(head)
            return (
                dot(k_ref[0, :, lanes], head_rhs(qt[rows, :n], head)),
                dot(v_ref[0, :, lanes], head_rhs(dat[rows, :n], head)),
            )

        def finish(head, weights, g):
            lanes, rows = pair_lanes(head), head_rows(head)
            dqt[rows, :n] = (dot(kt[rows, :], g) * factor).astype(bf16)
            return dot(g, one_head(q_ref[0, :n, lanes], head)), dot(weights, one_head(da[:n, lanes], head))

        parts = heads_back(
            HEADS, products,
            lambda head, raw: jnp.exp2(raw * scale + shift - lse_ref[0, head : head + 1, :n]),
            lambda head: head_inner(dat[head_rows(head), :n], at_ref[0, head_rows(head), :n]),
            finish,
        )
        for head in range(0, HEADS, 2):
            dk[:, pair_lanes(head)] = ((parts[head][0] + parts[head + 1][0]) * factor).astype(bf16)
            dv[:, pair_lanes(head)] = parts[head][1] + parts[head + 1][1]
        dq = dqt[:, :n].T
        tail[0:1, :] += col_sum(dq.astype(f32))
        n1, r1 = norm_stats(h1_ref[0, :n])
        x1b = (n1 * vec1_ref[3:4, :] + vec1_ref[4:5, :]).astype(bf16)
        acc[0] += dot(x1b.T, dq)
        dx1 = dh_ref[0, :n] + dot_nt(dq, matrix(0))
        small_o[3:4, :] += col_sum(dx1 * n1)
        small_o[4:5, :] += col_sum(dx1)
        dh1 = norm_back(dx1, n1, r1, vec1_ref[3:4, :])
        small_o[2:3, :] += col_sum(dh1)
        dh[item, :n] = dh1
        box.send("dh", item)

    rows_of(chunks * CH)

    tail[1:2, :] += col_sum(dv[...])
    dvb = dv[...].astype(bf16)
    mt = m_ref[0].T
    acc[1] += dot(mt, dk[...])
    acc[2] += dot(mt, dvb)
    gm_o[0] = dot_nt(dk[...], matrix(1)) + dot_nt(dvb, matrix(2))

    @pl.when(last)
    def _():
        for m in range(4):
            out[m * 8 : (m + 1) * 8, :SQ, :] = acc[m].astype(bf16).reshape(8, SQ, D)
        ahead = jnp.concatenate([out[1:, :AHEAD, :], tail[:AHEAD, :].astype(bf16)[None]], 0)
        out[:, SQ:, :] = jnp.concatenate([ahead, jnp.zeros((PIECES, SQ_OUT - SQ - AHEAD, D), bf16)], 1)
        sent = []
        for index, who, ref, slot in each_piece(me, gn_o, gf_o):
            sent.append(pltpu.make_async_copy(out.at[who], ref.at[slot], p_sems.at[index]))
            sent[-1].start()
        box.close(2)
        for copy in sent:
            copy.wait()


def cross_backward(horizon, me, tau, dh2, h1, memory, shift, saved, w, vec1, small2):
    q, k, v, at, lse = saved
    items, steps, _ = h1.shape
    mem = memory.shape[1]
    row, grads = (items, steps, D), shape_of((HALF, SQ_OUT, D), bf16)
    memo, rows, cols = item_spec(mem, D), item_spec(steps, D), item_spec(D, steps)
    return call(
        functools.partial(cross_backward_kernel, chunks=steps // CH), "cross_backward", items, (horizon, me),
        [
            (tau, pl.BlockSpec(memory_space=pltpu.SMEM)), (dh2, rows), (h1, rows), (memory, memo), (shift, item_spec(1, mem)),
            (q, rows), (k, memo), (v, memo), (at, cols), (lse, item_spec(HEADS, steps)),
            (w, whole_spec(4 * D, D)), (vec1, whole_spec(8, D)), (small2, whole_spec(VEC, D)),
        ],
        [
            (shape_of(row, f32), any_spec()), (grads, any_spec()), (grads, any_spec()),
            (shape_of((items, mem, D), f32), memo), (shape_of((8, D), f32), whole_spec(8, D)),
        ],
        [
            vmem(4, D, D), vmem(VEC, D),
            vmem(steps, D, dtype=bf16), vmem(D, steps, dtype=bf16), vmem(D, steps, dtype=bf16), vmem(D, mem, dtype=bf16),
            vmem(D, steps, dtype=bf16), vmem(mem, D, dtype=bf16), vmem(mem, D), vmem(*row), vmem(PIECES, SQ_OUT, D, dtype=bf16),
            pltpu.SemaphoreType.DMA((2, 1)), pltpu.SemaphoreType.DMA((PIECES,)),
        ],
        LIMITS[3], 8e9,
    )


def self_backward_kernel(
    horizon, me, tau, dh_ref, x_ref, q_ref, k_ref, v_ref, at_ref, lse_ref, w, small1_ref,
    gx_o, gn_o, gf_o,
    flat, acc, tail, da, dat, qt, kt, xt, dqt, dqsc, dksc, dvsc, gx, sems, *, chunks,
):
    item = pl.program_id(0)
    box = Outbox({"gx": (gx, gx_o)}, sems)

    @pl.when(item == 0)
    def _():
        acc[...] = jnp.zeros_like(acc)
        tail[...] = small1_ref[...]

    factor = tau[item] * ROOT
    scale = tau[item] * (LOG2E * ROOT)

    count = chunk_count(horizon, item, chunks)

    def rows_at(chunk):
        return pl.ds(pl.multiple_of(chunk * CH, CH), CH)

    def before(here):
        e1 = dh_ref[0, here].astype(bf16)
        acc[3] += dot(at_ref[0, :, here], e1)
        da[here] = dot_nt(e1, w[3 * D :]).astype(bf16)
        dat[:, here] = da[here].T
        qt[:, here] = q_ref[0, here].T
        kt[:, here] = k_ref[0, here].T
        xt[:, here] = x_ref[0, here].T

    def behind(here):
        dq = dqsc[here]
        dk = (dksc[here] * factor).astype(bf16)
        dv = dvsc[here]
        tail[0:1, :] += col_sum(dq.astype(f32))
        tail[1:2, :] += col_sum(dv)
        dv = dv.astype(bf16)
        gx[item, here] = dh_ref[0, here] + dot_nt(dq, w[:D]) + dot_nt(dk, w[D : 2 * D]) + dot_nt(dv, w[2 * D : 3 * D])
        acc[0] += dot(xt[:, here], dq)
        acc[1] += dot(xt[:, here], dk)
        acc[2] += dot(xt[:, here], dv)

    everything = slice(0, chunks * CH)
    for held in (dksc, dvsc, dqsc):
        held[...] = jnp.zeros_like(held)
    before(everything)

    @pl.loop(0, count)
    def _(chunk):
        here = rows_at(chunk)
        for at_chunk in range(chunks):

            @pl.when(chunk == at_chunk)
            def _(keys=(at_chunk + 1) * CH):
                @pl.loop(0, 2)
                def _(group):
                    places = []
                    for index in range(HEADS // 2):
                        start = group * (D // 2) + index // 2 * LANES
                        rows = pl.ds(pl.multiple_of(start + index % 2 * HW, HW), HW)
                        places.append((pl.ds(pl.multiple_of(start, LANES), LANES), rows))

                    def products(i):
                        lanes, rows = places[i]
                        return (
                            dot(k_ref[0, :keys, lanes], head_rhs(qt[rows, here], i)),
                            dot(v_ref[0, :keys, lanes], head_rhs(dat[rows, here], i)),
                        )

                    def weigh(i, raw):
                        lse = lse_ref[0, pl.ds(group * (HEADS // 2) + i, 1), here]
                        return causal_cut(jnp.exp2(raw * scale - lse), 0.0)

                    def finish(i, weights, g):
                        lanes, rows = places[i]
                        dqt[rows, :] = (dot(kt[rows, :keys], g) * factor).astype(bf16)
                        return dot(g, one_head(q_ref[0, here, lanes], i)), dot(weights, one_head(da[here, lanes], i))

                    def inner(i):
                        return head_inner(dat[places[i][1], here], at_ref[0, places[i][1], here])

                    parts = heads_back(HEADS // 2, products, weigh, inner, finish)
                    for i in range(0, HEADS // 2, 2):
                        lanes = places[i][0]
                        dksc[:keys, lanes] += parts[i][0] + parts[i + 1][0]
                        dvsc[:keys, lanes] += parts[i][1] + parts[i + 1][1]

        dqsc[here, :] = dqt[...].T

    behind(everything)
    box.send("gx", item)

    @pl.when(item == pl.num_programs(0) - 1)
    def _():
        store_shards(me, gn_o, gf_o, flat, acc, tail)
        box.close(2)


def self_backward(horizon, me, tau, dh1, x, saved, w, small1):
    q, k, v, at, lse = saved
    items, steps, _ = x.shape
    half, shard = HALF, SHARD_PAD
    row, grads = (items, steps, D), shape_of((half, shard, LANES), bf16)
    rows, cols = item_spec(steps, D), item_spec(D, steps)
    return call(
        functools.partial(self_backward_kernel, chunks=steps // CH), "self_backward", items, (horizon, me),
        [
            (tau, pl.BlockSpec(memory_space=pltpu.SMEM)), (dh1, rows), (x, rows), (q, rows), (k, rows), (v, rows), (at, cols),
            (lse, item_spec(HEADS, steps)), (w, whole_spec(4 * D, D)), (small1, whole_spec(8, D)),
        ],
        [(kept(*row, dtype=f32), any_spec()), (grads, whole_spec(half, shard, LANES)), (grads, whole_spec(half, shard, LANES))],
        [
            vmem(PIECES * SHARD_ROWS + 16, LANES), vmem(4, D, D), vmem(8, D),
            vmem(steps, D, dtype=bf16), vmem(D, steps, dtype=bf16), vmem(D, steps, dtype=bf16), vmem(D, steps, dtype=bf16),
            vmem(D, steps, dtype=bf16), vmem(D, CH, dtype=bf16), vmem(steps, D, dtype=bf16),
            vmem(steps, D), vmem(steps, D), vmem(*row), pltpu.SemaphoreType.DMA((2, 1)),
        ],
        LIMITS[4], 1.5e10,
    )


AXES = ("wide", "narrow")
ALONG_Z = (8, 16, 24)
WITHIN = (1, 4, 5)
DEPTH = 4
TAIL = 32


def after(value, event):
    return lax.optimization_barrier((value, event))[0]


def swap(rows, offset):
    return lax.ppermute(rows, AXES, [(i, i ^ offset) for i in range(PIECES)])


def from_device(rows, step):
    return lax.ppermute(rows, AXES, [((i + step) % PIECES, i) for i in range(PIECES)])


def line_round(piece):
    return [piece[None]] + [swap(piece[None], o) for o in ALONG_Z]


def plane_round(line):
    return [line] + [swap(line, o) for o in WITHIN]


def plane_scatter(mine):
    return mine[:1] + [swap(part, o) for part, o in zip(mine[1:], WITHIN)]


def line_scatter(line):
    return [line[:1]] + [swap(line[i : i + 1], o) for i, o in enumerate(ALONG_Z, 1)]


def add_up(parts):
    return sum(part.astype(f32) for part in parts)


def turned(rows, away):
    if away:
        return rows.reshape(IN, TILES, D).transpose(1, 0, 2).reshape(FR, D)
    return rows.reshape(TILES, IN, D).transpose(1, 0, 2).reshape(FR, D)


def raw_piece(shard):
    return jnp.pad(shard.reshape(-1, LANES), ((0, SHARD_PAD - SHARD_ROWS), (0, 0)))


def dense_piece(shard, who):
    rows = shard.reshape(-1, LANES)
    tail = rows[-TAIL:]
    joined = jnp.concatenate([from_device(tail, -1), rows])
    main = lax.dynamic_slice_in_dim(joined, TAIL - who, rows.shape[0] - 1).reshape(FR, D)
    main = jnp.where(who < HALF, turned(main, True), main)
    return jnp.pad(jnp.concatenate([main, tail.reshape(VEC // 2, D)]), ((0, VEC // 2), (0, 0)))


def rest_shards(rest, who):
    cross, dense = rest[: SQ + AHEAD], rest[SQ_OUT : SQ_OUT + FR]
    dense = jnp.where(who < HALF, turned(dense, False), dense)
    dense = jnp.concatenate([dense, rest[SQ_OUT + FR : SQ_OUT + FR + AHEAD]])
    return [
        lax.dynamic_slice_in_dim(rows.reshape(-1, LANES), who, (rows.shape[0] - AHEAD) * D // LANES + 1).reshape(-1)
        for rows in (cross, dense)
    ]


def quarters(near, far):
    return [add_up([near[i : i + DEPTH], far[i : i + DEPTH]]).astype(bf16) for i in range(0, HALF, DEPTH)]


def body(inputs, memory, tau_scale, delta_shift, horizon, self_params, cross_params, dense_params, cotangent):
    who = lax.axis_index(AXES).astype(jnp.int32)
    me = who[None]
    x, m, ct = inputs[:, 0], memory[:, 0], cotangent[:, 0]
    tau, shift, horizon = tau_scale[:, 0], delta_shift, horizon[:, 0]

    line_both = jnp.concatenate(line_round(jnp.concatenate([raw_piece(self_params), raw_piece(cross_params)])))
    line_dense = line_round(dense_piece(dense_params, who))
    near_both = jnp.concatenate(after(plane_round(line_both), line_dense))
    p_both = near_both, swap(near_both, CORE)
    plane_dense = plane_round(jnp.concatenate(after(line_dense, near_both)))
    q, k, v, at, h1, w1, q2, at2, h2, w2, k2, v2, lse, lse2, vec1, vec2 = attention_forward(
        horizon, me, tau, x, m, shift, p_both
    )
    near_dense = jnp.concatenate(after(plane_dense, vec2))
    p_dense = near_dense, swap(near_dense, CORE)
    y, dh2, gn_dense, gf_dense, small2 = dense_both(horizon, me, h2, ct, vec2, p_dense)
    other_dense = swap(gf_dense, CORE)
    dh1, gn_cross, gf_cross, gm, small1 = cross_backward(
        horizon, me, tau, after(dh2, gf_dense), h1, m, shift, (q2, k2, v2, at2, lse2), w2, vec1, small2
    )
    other_cross = swap(gf_cross, CORE)
    other_dense = after(other_dense, small1)
    mine_rest = [
        jnp.concatenate(pair, 1) for pair in zip(quarters(gn_cross, other_cross), quarters(gn_dense, other_dense))
    ]
    plane_rest = plane_scatter(mine_rest)
    gx, gn_self, gf_self = self_backward(
        horizon, me, tau, after(dh1, mine_rest), x, (q, k, v, at, lse), w1, small1
    )
    plane_rest, gf_self = after((plane_rest, gf_self), gn_self)
    other_self = swap(gf_self, CORE)
    sum_rest = add_up(plane_rest).astype(bf16)
    line_rest = line_scatter(sum_rest)
    plane_self = plane_scatter(quarters(gn_self, after(other_self, sum_rest)))
    sum_self = add_up(plane_self).astype(bf16)
    line_self = line_scatter(sum_self)
    g_cross, g_dense = rest_shards(add_up(after(line_rest, line_self))[0], who)
    g_self = add_up(line_self)[0, :SHARD_ROWS].reshape(-1)
    return y[:, None], gx[:, None], gm[:, None], g_self, g_cross, g_dense


def general_body(inputs, memory, tau_scale, delta_shift, horizon, self_params, cross_params, dense_params, cotangent):
    x, m, ct = inputs[:, 0], memory[:, 0], cotangent[:, 0]
    tau, shift, horizon = tau_scale[:, 0], delta_shift, horizon[:, 0]
    me = jnp.zeros((1,), jnp.int32)
    near = jnp.array([slot_offset(slot) for slot in range(HALF)], jnp.int32)
    owners = jnp.concatenate([near, near ^ CORE])
    square, tall = 4 * D, 2 * FF
    flat = [lax.all_gather(v, AXES, axis=0, tiled=True) for v in (self_params, cross_params, dense_params)]
    raw = [v[: PIECES * SHARD_ROWS * LANES].reshape(PIECES, SHARD_ROWS, LANES) for v in flat[:2]]
    raw = jnp.concatenate([jnp.pad(v, ((0, 0), (0, SHARD_PAD - SHARD_ROWS), (0, 0))) for v in raw], 1)[owners]
    dense = flat[2][: (tall + VEC) * D].reshape(-1, D)
    parts = dense[:tall].reshape(PIECES, FR, D)
    parts = jnp.concatenate([jax.vmap(lambda rows: turned(rows, True))(parts[:HALF]), parts[HALF:]])
    parts = jnp.concatenate([parts, jnp.broadcast_to(dense[None, tall:], (PIECES, VEC, D))], 1)[owners]
    q, k, v, at, h1, w1, q2, at2, h2, w2, k2, v2, lse, lse2, vec1, vec2 = attention_forward(
        horizon, me, tau, x, m, shift, (raw[:HALF], raw[HALF:])
    )
    y, dh2, gn_dense, gf_dense, small2 = dense_both(horizon, me, h2, ct, vec2, (parts[:HALF], parts[HALF:]))
    dh1, gn_cross, gf_cross, gm, small1 = cross_backward(
        horizon, me, tau, dh2, h1, m, shift, (q2, k2, v2, at2, lse2), w2, vec1, small2
    )
    gx, gn_self, gf_self = self_backward(horizon, me, tau, dh1, x, (q, k, v, at, lse), w1, small1)

    def in_order(near_part, far_part):
        both = jnp.concatenate([near_part, far_part]).astype(f32)
        return jnp.zeros_like(both).at[owners].set(both)

    cross = in_order(gn_cross, gf_cross)
    dense = in_order(gn_dense, gf_dense)
    tall_part = jnp.concatenate([jax.vmap(lambda rows: turned(rows, False))(dense[:HALF, :FR]), dense[HALF:, :FR]])
    wholes = (
        in_order(gn_self, gf_self)[:, :SHARD_ROWS].reshape(-1),
        jnp.concatenate([cross[:, :SQ].reshape(-1), cross[PIECES - 1, SQ : SQ + AHEAD].reshape(-1)]),
        jnp.concatenate([tall_part.reshape(-1), dense[PIECES - 1, FR : FR + AHEAD].reshape(-1)]),
    )
    sums = [
        lax.psum_scatter(jnp.pad(v, (0, f.shape[0] - v.shape[0])), AXES, scatter_dimension=0, tiled=True)
        for v, f in zip(wholes, flat)
    ]
    return y[:, None], gx[:, None], gm[:, None], *sums


def solution(mesh):
    items = P(None, AXES, None, None)
    placed = (items, items, P(None, AXES), P(None, AXES, None), P(None, AXES), P(AXES), P(AXES), P(AXES), items)
    fits = dict(mesh.shape) == {"wide": HALF, "narrow": 2}
    return jax.shard_map(
        body if fits else general_body,
        mesh=mesh, in_specs=placed, out_specs=(items, items, items, P(AXES), P(AXES), P(AXES)), check_vma=False,
    )
```

```python
import functools
import math

import jax
import jax.numpy as jnp
from jax import lax
from jax.experimental import pallas as pl
from jax.experimental.pallas import tpu as pltpu
from jax.sharding import PartitionSpec as P

D = 512
FF = 2048
HEADS = 8
HW = D // HEADS
LABEL = 48
LANES = 128
CH_BITS = 8
CH = 1 << CH_BITS
PIECES = 32
HALF = PIECES // 2
CORE = 2
SQ = 4 * D // PIECES
FR = 2 * FF // PIECES
IN = D // (PIECES // 2)
TILES = FF // D
VEC = 16
AHEAD = 8
SQ_OUT = SQ + 16
FR_OUT = FR + 16
SHARD_ROWS = 257
SHARD_PAD = (SHARD_ROWS + 15) // 16 * 16
EPS = 1e-05
NEG = -1e30
LOG2E = 1.4426950408889634
LIMITS = (40, 0, 48, 44, 46)
ROOT = 1.0 / math.sqrt(HW)
f32, bf16 = jnp.float32, jnp.bfloat16
MIB = 2**20


def dot(a, b):
    return jnp.dot(a, b, preferred_element_type=f32)


def dot_nt(a, b):
    return lax.dot_general(a, b, (((1,), (1,)), ((), ())), preferred_element_type=f32)


def norm_stats(h):
    center = h - jnp.mean(h, -1, keepdims=True)
    rstd = lax.rsqrt(jnp.mean(center * center, -1, keepdims=True) + EPS)
    return center * rstd, rstd


def norm_back(dz, n, rstd, gain):
    dn = dz * gain
    return rstd * (dn - jnp.mean(dn, -1, keepdims=True) - n * jnp.mean(dn * n, -1, keepdims=True))


def col_sum(v):
    return jnp.sum(v, 0, keepdims=True)


def slot_offset(slot):
    return ((slot & 3) << 3) | (((slot >> 3) & 1) << 2) | ((slot >> 2) & 1)


def each_piece(me, near, far):
    for slot in range(HALF):
        who = me[0] ^ slot_offset(slot)
        yield slot, who, near, slot
        yield HALF + slot, who ^ CORE, far, slot


def slot_of(me, who):
    away = me[0] ^ who
    return (((away >> 2) & 1) * 2 + (away & 1)) * 4 + (away >> 3), (away & CORE) != 0


def either(is_far, near_copy, far_copy):
    pl.when(jnp.logical_not(is_far))(near_copy.start)
    pl.when(is_far)(far_copy.start)


def load_shards(me, near, far, first, flat, w, vec):
    @pl.loop(0, HALF // 4)
    def _(turn):
        for slot in [turn * 4 + i for i in range(4)]:
            who = me[0] ^ slot_offset(slot)
            for ref, owner in ((near, who), (far, who ^ CORE)):
                flat[pl.ds(owner * SHARD_ROWS, SHARD_ROWS), :] = ref[slot, first : first + SHARD_ROWS, :].astype(f32)

    per = D // LANES
    for j in range(per):
        w[:, j * LANES : (j + 1) * LANES] = flat[pl.ds(j, 4 * D, stride=per), :].astype(bf16)
    vec[...] = jnp.zeros_like(vec)
    for i in range(5):
        for j in range(per):
            at = 4 * D * per + i * per + j
            vec[i : i + 1, j * LANES : (j + 1) * LANES] = flat[at : at + 1, :]


def store_shards(me, near, far, flat, acc, vec):
    per = D // LANES
    for m in range(4):
        for j in range(per):
            flat[pl.ds(m * D * per + j, D, stride=per), :] = acc[m, :, j * LANES : (j + 1) * LANES]
    start = 4 * D * per
    flat[start:, :] = jnp.zeros((flat.shape[0] - start, LANES), f32)
    for i in range(5):
        for j in range(per):
            flat[start + i * per + j : start + i * per + j + 1, :] = vec[i : i + 1, j * LANES : (j + 1) * LANES]
    rows = near.shape[1]

    @pl.loop(0, HALF)
    def _(slot):
        who = me[0] ^ slot_offset(slot)
        near[slot] = flat[pl.ds(who * SHARD_ROWS, rows), :].astype(bf16)
        far[slot] = flat[pl.ds((who ^ CORE) * SHARD_ROWS, rows), :].astype(bf16)


def head_rows(head):
    return slice(head * HW, (head + 1) * HW)


def pair_lanes(head):
    return slice(head // 2 * LANES, (head // 2 + 1) * LANES)


def head_rhs(block, head):
    zero = jnp.zeros_like(block)
    return jnp.concatenate([block, zero] if head % 2 == 0 else [zero, block], 0)


def one_head(rows, head):
    lane = lax.broadcasted_iota(jnp.int32, rows.shape, 1)
    return jnp.where((lane < HW) == (head % 2 == 0), rows, jnp.zeros_like(rows))


def causal_cut(scores, fill):
    keys = scores.shape[0]
    tail = scores[keys - CH :, :]
    key_at = lax.broadcasted_iota(jnp.int32, tail.shape, 0)
    query_at = lax.broadcasted_iota(jnp.int32, tail.shape, 1)
    tail = jnp.where(key_at <= query_at, tail, fill)
    return tail if keys == CH else jnp.concatenate([scores[: keys - CH, :], tail], 0)


def shift_column(shift_ref):
    row = shift_ref[0] * (LOG2E * ROOT)
    return jnp.broadcast_to(row, (8, row.shape[1])).T[:, :1]


def attend_heads(score, shape, values_t):
    following, waiting, out = score(0), None, []

    def finish(head, e, top, total):
        mixed = dot(values_t(head), e)
        out.append(((mixed * (1.0 / total)).astype(bf16), top + jnp.log2(total)))

    for head in range(HEADS):
        raw, following = following, score(head + 1) if head + 1 < HEADS else None
        if waiting is not None:
            finish(head - 1, *waiting)
        s = shape(raw)
        top = jnp.max(s, 0, keepdims=True)
        e = jnp.exp2(s - top)
        waiting = e.astype(bf16), top, jnp.sum(e, 0, keepdims=True)
    finish(HEADS - 1, *waiting)
    return out


def head_inner(da_t, a_t):
    return jnp.sum(da_t.astype(f32) * a_t.astype(f32), 0, keepdims=True)


def chunk_count(horizon, item, chunks):
    return jnp.minimum(lax.shift_right_logical(horizon[item] + (LABEL + CH - 1), CH_BITS), chunks)


class Outbox:
    def __init__(self, pairs, sems):
        self.pairs, self.sems = pairs, sems

    def copy(self, name, item):
        index = list(self.pairs).index(name)
        src, dst = self.pairs[name]
        return pltpu.make_async_copy(src.at[item], dst.at[item], self.sems.at[item, index])

    def send(self, name, item):
        self.copy(name, item).start()

    def close(self, items):
        for item in range(items):
            for name in self.pairs:
                self.copy(name, item).wait()


def vmem(*shape, dtype=f32):
    return pltpu.VMEM(shape, dtype)


def call(kernel, name, items, prefetch, ins, outs, scratch, limit, flops):
    return pl.pallas_call(
        kernel,
        grid_spec=pltpu.PrefetchScalarGridSpec(
            num_scalar_prefetch=len(prefetch),
            grid=(items,),
            in_specs=[spec for _, spec in ins],
            out_specs=[spec for _, spec in outs],
            scratch_shapes=scratch,
        ),
        out_shape=[shape for shape, _ in outs],
        compiler_params=pltpu.CompilerParams(vmem_limit_bytes=limit * MIB),
        cost_estimate=pl.CostEstimate(flops=int(flops), bytes_accessed=int(2e7), transcendentals=0),
        name=name,
    )(*prefetch, *[array for array, _ in ins])


def any_spec():
    return pl.BlockSpec(memory_space=pl.ANY)


def item_spec(*shape):
    return pl.BlockSpec((1, *shape), lambda i, *_: (i, *[0] * len(shape)))


def whole_spec(*shape):
    return pl.BlockSpec(shape, lambda i, *_: (0,) * len(shape), pipeline_mode=pl.Buffered(1))


def kept(*shape, dtype=bf16):
    return pltpu.HBM(shape, dtype)


shape_of = jax.ShapeDtypeStruct


def attention_forward_kernel(
    horizon, me, tau, x_ref, m_ref, shift_ref, pn_ref, pf_ref,
    q_o, k_o, v_o, at_o, h1_o, w1_o, q2_o, at2_o, h2_o, w2_o, k2_o, v2_o, lse_o, lse2_o, vec1_o, vec2_o,
    flat, w, w2, vt, qt, vt2, q, k, v, at, h1, q2, at2, h2, sems, w_sems, *, chunks,
):
    item = pl.program_id(0)
    box = Outbox(
        {
            "q": (q, q_o), "k": (k, k_o), "v": (v, v_o), "at": (at, at_o), "h1": (h1, h1_o),
            "q2": (q2, q2_o), "at2": (at2, at2_o), "h2": (h2, h2_o),
        },
        sems,
    )
    w_copies = [pltpu.make_async_copy(a, b, w_sems.at[i]) for i, (a, b) in enumerate(((w, w1_o), (w2, w2_o)))]

    @pl.when(item == 0)
    def _():
        load_shards(me, pn_ref, pf_ref, 0, flat, w, vec1_o)
        w_copies[0].start()
        load_shards(me, pn_ref, pf_ref, SHARD_PAD, flat, w2, vec2_o)
        w_copies[1].start()

    k2_o[0] = dot(m_ref[0], w2[D : 2 * D]).astype(bf16)
    v2_o[0] = (dot(m_ref[0], w2[2 * D : 3 * D]) + vec2_o[1:2, :]).astype(bf16)
    vt2[...] = v2_o[0].T

    def rows_of(n):
        scale = tau[item] * (LOG2E * ROOT)
        x = x_ref[0, :n]
        q[item, :n] = (dot(x, w[:D]) + vec1_o[0:1, :]).astype(bf16)
        box.send("q", item)
        k[item, :n] = dot(x, w[D : 2 * D]).astype(bf16)
        box.send("k", item)
        v[item, :n] = (dot(x, w[2 * D : 3 * D]) + vec1_o[1:2, :]).astype(bf16)
        box.send("v", item)
        qt[:, :n] = q[item, :n].T
        vt[:, :n] = v[item, :n].T
        for start in range(0, n, CH):
            keys, here = start + CH, slice(start, start + CH)
            score = lambda head: dot(k[item, :keys, pair_lanes(head)], head_rhs(qt[head_rows(head), here], head))
            outs = attend_heads(
                score, lambda raw: causal_cut(raw * scale, NEG), lambda head: vt[head_rows(head), :keys]
            )
            for head, (mixed, total) in enumerate(outs):
                at[item, head_rows(head), here], lse_o[0, head : head + 1, here] = mixed, total
        box.send("at", item)
        hidden = x.astype(f32) + dot(at[item, :, :n].T, w[3 * D :]) + vec1_o[2:3, :]
        h1[item, :n] = hidden
        box.send("h1", item)

        shift = shift_column(shift_ref)
        n1, _ = norm_stats(hidden)
        x1 = n1 * vec1_o[3:4, :] + vec1_o[4:5, :]
        h2[item, :n] = x1
        q2[item, :n] = (dot(x1.astype(bf16), w2[:D]) + vec2_o[0:1, :]).astype(bf16)
        box.send("q2", item)
        qt[:, :n] = q2[item, :n].T
        score = lambda head: dot(k2_o[0, :, pair_lanes(head)], head_rhs(qt[head_rows(head), :n], head))
        outs = attend_heads(score, lambda raw: raw * scale + shift, lambda head: vt2[head_rows(head), :])
        for head, (mixed, total) in enumerate(outs):
            at2[item, head_rows(head), :n], lse2_o[0, head : head + 1, :n] = mixed, total
        box.send("at2", item)
        h2[item, :n] += dot(at2[item, :, :n].T, w2[3 * D :]) + vec2_o[2:3, :]
        box.send("h2", item)

    rows_of(chunks * CH)

    @pl.when(item == pl.num_programs(0) - 1)
    def _():
        box.close(2)
        for copy in w_copies:
            copy.wait()


def attention_forward(horizon, me, tau, x, memory, shift, params):
    items, steps, _ = x.shape
    mem = memory.shape[1]
    half, rows, _ = params[0].shape
    row, col = (items, steps, D), (items, D, steps)
    shards, memo, lses = whole_spec(half, rows, LANES), item_spec(mem, D), item_spec(HEADS, steps)
    saved = lambda *shape: (kept(*shape), any_spec())
    return call(
        functools.partial(attention_forward_kernel, chunks=steps // CH), "attention_forward", items, (horizon, me),
        [
            (tau, pl.BlockSpec(memory_space=pltpu.SMEM)), (x, item_spec(steps, D)), (memory, memo), (shift, item_spec(1, mem)),
            (params[0], shards), (params[1], shards),
        ],
        [
            saved(*row), saved(*row), saved(*row), saved(*col), (kept(*row, dtype=f32), any_spec()), saved(4 * D, D),
            saved(*row), saved(*col), (kept(*row, dtype=f32), any_spec()), saved(4 * D, D),
            (shape_of((items, mem, D), bf16), memo), (shape_of((items, mem, D), bf16), memo),
            (shape_of((items, HEADS, steps), f32), lses), (shape_of((items, HEADS, steps), f32), lses),
            (shape_of((8, D), f32), whole_spec(8, D)), (shape_of((8, D), f32), whole_spec(8, D)),
        ],
        [
            vmem(PIECES * SHARD_ROWS + 16, LANES), vmem(4 * D, D, dtype=bf16), vmem(4 * D, D, dtype=bf16),
            vmem(D, steps, dtype=bf16), vmem(D, steps, dtype=bf16), vmem(D, mem, dtype=bf16),
            vmem(*row, dtype=bf16), vmem(*row, dtype=bf16), vmem(*row, dtype=bf16), vmem(*col, dtype=bf16), vmem(*row),
            vmem(*row, dtype=bf16), vmem(*col, dtype=bf16), vmem(*row),
            pltpu.SemaphoreType.DMA((2, 8)), pltpu.SemaphoreType.DMA((2,)),
        ],
        LIMITS[0], 1.2e10,
    )


def dense_kernel(
    horizon, me, horizon_at, h_ref, ct_ref, vec2_ref, pn_ref, pf_ref, y_o, dh_o, gn_o, gf_o, small_o,
    w_in, w, vecb, vec_sc, bias, acc_in, acc_out, acc_bias, f_sc, gp_sc, y, dh, out, sems, p_sems, vec_sem, *, chunks,
):
    item = pl.program_id(0)
    box = Outbox({"y": (y, y_o), "dh": (dh, dh_o)}, sems)
    out_row, gain_row = 8 + TILES, 8 + TILES + 1
    vec = lambda i: vec_sc[i : i + 1, :]

    @pl.when(item == 0)
    def _():
        copies = [
            pltpu.make_async_copy(ref.at[slot, pl.ds(0, FR), :], w.at[who], p_sems.at[index])
            for index, who, ref, slot in each_piece(me, pn_ref, pf_ref)
        ]
        for copy in copies:
            copy.start()
        slot, is_far = slot_of(me, PIECES - 1)
        vec_copies = [
            pltpu.make_async_copy(ref.at[slot, pl.ds(FR, VEC), :], vecb, vec_sem) for ref in (pn_ref, pf_ref)
        ]
        either(is_far, *vec_copies)
        acc_in[...] = jnp.zeros_like(acc_in)
        acc_out[...] = jnp.zeros_like(acc_out)
        acc_bias[...] = jnp.zeros_like(acc_bias)
        small_o[...] = jnp.zeros_like(small_o)
        vec_copies[0].wait()
        vec_sc[...] = vecb[:8].astype(f32)
        for part in range(TILES):
            bias[:, part * D : (part + 1) * D] = vec(part)
        for copy in copies:
            copy.wait()
        for who in range(HALF):
            for part in range(TILES):
                w_in[who * IN : (who + 1) * IN, part * D : (part + 1) * D] = w[who, part * IN : (part + 1) * IN, :]

    w_out = lambda: w[HALF:].reshape(FF, D)

    def add(row, value):
        small_o[row : row + 1, :] += value

    y[item] = jnp.zeros(y.shape[1:], bf16)
    dh[item] = jnp.zeros(dh.shape[1:], f32)

    @pl.loop(0, chunk_count(horizon, item, chunks))
    def _(chunk):
        here = pl.ds(pl.multiple_of(chunk * CH, CH), CH)
        n2, r2 = norm_stats(h_ref[0, here])
        x2 = n2 * vec2_ref[3:4, :] + vec2_ref[4:5, :]
        x2b = x2.astype(bf16)
        u = dot(x2b, w_in[...]) + bias[...]
        cdf = 0.5 * (1.0 + lax.erf(u * 0.7071067811865476))
        f_sc[...] = (u * cdf).astype(bf16)
        gp_sc[...] = cdf + u * jnp.exp(u * u * -0.5) * (1.0 / math.sqrt(2.0 * math.pi))
        n3, r3 = norm_stats(x2 + dot(f_sc[...], w_out()) + vec(TILES))
        at = lax.broadcasted_iota(jnp.int32, (CH, 1), 0) + chunk * CH
        valid = (at < LABEL + horizon_at[item]).astype(f32)
        y[item, here] = ((n3 * vec(TILES + 1) + vec(TILES + 2)) * valid).astype(bf16)
        dy = ct_ref[0, here].astype(f32) * valid
        add(gain_row, col_sum(dy * n3))
        add(gain_row + 1, col_sum(dy))
        dh3 = norm_back(dy, n3, r3, vec(TILES + 1))
        add(out_row, col_sum(dh3))
        e3 = dh3.astype(bf16)
        acc_out[...] += dot(e3.T, f_sc[...])
        du = dot_nt(e3, w_out()) * gp_sc[...]
        acc_bias[...] += col_sum(du)
        eu = du.astype(bf16)
        acc_in[...] += dot(x2b.T, eu)
        dx2 = dh3 + dot_nt(eu, w_in[...])
        add(3, col_sum(dx2 * n2))
        add(4, col_sum(dx2))
        dh2 = norm_back(dx2, n2, r2, vec2_ref[3:4, :])
        add(2, col_sum(dh2))
        dh[item, here] = dh2

    box.send("y", item)
    box.send("dh", item)

    @pl.when(item == pl.num_programs(0) - 1)
    def _():
        for part in range(TILES):
            add(8 + part, acc_bias[:, part * D : (part + 1) * D])
        pad = jnp.zeros((FR_OUT - FR - AHEAD, D), bf16)
        ahead = small_o[8:, :].astype(bf16)
        for who in reversed(range(PIECES)):
            out[who, FR:, :] = jnp.concatenate([ahead, pad], 0)
            if who < HALF:
                for part in range(TILES):
                    out[who, part * IN : (part + 1) * IN, :] = acc_in[
                        who * IN : (who + 1) * IN, part * D : (part + 1) * D
                    ].astype(bf16)
                ahead = jnp.concatenate(
                    [acc_in[who * IN + i : who * IN + i + 1, part * D : (part + 1) * D] for i in range(2) for part in range(TILES)], 0
                ).astype(bf16)
            else:
                turn = acc_out[:, (who - HALF) * FR : (who - HALF + 1) * FR].astype(bf16).T
                out[who, :FR, :] = turn
                ahead = turn[:AHEAD]
            slot, is_far = slot_of(me, who)
            either(
                is_far,
                pltpu.make_async_copy(out.at[who], gn_o.at[slot], p_sems.at[who]),
                pltpu.make_async_copy(out.at[who], gf_o.at[slot], p_sems.at[who]),
            )
        box.close(2)
        for who in range(PIECES):
            pltpu.make_async_copy(out.at[who], gf_o.at[0], p_sems.at[who]).wait()


def dense_both(horizon, me, h2, ct, vec2, params):
    items, steps, _ = h2.shape
    row, grads = (items, steps, D), shape_of((HALF, FR_OUT, D), bf16)
    return call(
        functools.partial(dense_kernel, chunks=steps // CH), "dense_both", items, (horizon, me),
        [
            (horizon, pl.BlockSpec(memory_space=pltpu.SMEM)), (h2, item_spec(steps, D)), (ct, item_spec(steps, D)),
            (vec2, whole_spec(8, D)), (params[0], any_spec()), (params[1], any_spec()),
        ],
        [
            (kept(*row), any_spec()), (shape_of(row, f32), any_spec()), (grads, any_spec()), (grads, any_spec()),
            (shape_of((VEC, D), f32), whole_spec(VEC, D)),
        ],
        [
            vmem(D, FF, dtype=bf16), vmem(PIECES, FR, D, dtype=bf16), vmem(VEC, D, dtype=bf16), vmem(8, D), vmem(1, FF), vmem(D, FF), vmem(D, FF), vmem(1, FF),
            vmem(CH, FF, dtype=bf16), vmem(CH, FF),
            vmem(*row, dtype=bf16), vmem(*row), vmem(PIECES, FR_OUT, D, dtype=bf16), pltpu.SemaphoreType.DMA((2, 2)), pltpu.SemaphoreType.DMA((PIECES,)),
            pltpu.SemaphoreType.DMA,
        ],
        LIMITS[2], 2e10,
    )


def heads_back(count, products, weigh, inner, finish):
    following, waiting, out = products(0), None, []
    for i in range(count):
        (raw, dp), following = following, products(i + 1) if i + 1 < count else None
        if waiting is not None:
            out.append(finish(i - 1, *waiting))
        weights = weigh(i, raw)
        waiting = weights.astype(bf16), (weights * (dp - inner(i))).astype(bf16)
    out.append(finish(count - 1, *waiting))
    return out


def cross_backward_kernel(
    horizon, me, tau, dh_ref, h1_ref, m_ref, shift_ref, q_ref, k_ref, v_ref, at_ref, lse_ref, w, vec1_ref, small2_ref,
    dh_o, gn_o, gf_o, gm_o, small_o,
    acc, tail, da, dat, qt, kt, dqt, dk, dv, dh, out, sems, p_sems, *, chunks,
):
    item = pl.program_id(0)
    last = item == pl.num_programs(0) - 1
    box = Outbox({"dh": (dh, dh_o)}, sems)
    matrix = lambda m: w[m * D : (m + 1) * D]

    @pl.when(item == 0)
    def _():
        acc[...] = jnp.zeros_like(acc)
        tail[...] = small2_ref[...]
        small_o[...] = jnp.zeros_like(small_o)

    factor = tau[item] * ROOT
    kt[...] = k_ref[0].T

    def rows_of(n):
        scale = tau[item] * (LOG2E * ROOT)
        shift = shift_column(shift_ref)
        e2 = dh_ref[0, :n].astype(bf16)
        acc[3] += dot(at_ref[0, :, :n], e2)
        da[:n] = dot_nt(e2, matrix(3)).astype(bf16)
        dat[:, :n] = da[:n].T
        qt[:, :n] = q_ref[0, :n].T

        def products(head):
            lanes, rows = pair_lanes(head), head_rows(head)
            return (
                dot(k_ref[0, :, lanes], head_rhs(qt[rows, :n], head)),
                dot(v_ref[0, :, lanes], head_rhs(dat[rows, :n], head)),
            )

        def finish(head, weights, g):
            lanes, rows = pair_lanes(head), head_rows(head)
            dqt[rows, :n] = (dot(kt[rows, :], g) * factor).astype(bf16)
            return dot(g, one_head(q_ref[0, :n, lanes], head)), dot(weights, one_head(da[:n, lanes], head))

        parts = heads_back(
            HEADS, products,
            lambda head, raw: jnp.exp2(raw * scale + shift - lse_ref[0, head : head + 1, :n]),
            lambda head: head_inner(dat[head_rows(head), :n], at_ref[0, head_rows(head), :n]),
            finish,
        )
        for head in range(0, HEADS, 2):
            dk[:, pair_lanes(head)] = ((parts[head][0] + parts[head + 1][0]) * factor).astype(bf16)
            dv[:, pair_lanes(head)] = parts[head][1] + parts[head + 1][1]
        dq = dqt[:, :n].T
        tail[0:1, :] += col_sum(dq.astype(f32))
        n1, r1 = norm_stats(h1_ref[0, :n])
        x1b = (n1 * vec1_ref[3:4, :] + vec1_ref[4:5, :]).astype(bf16)
        acc[0] += dot(x1b.T, dq)
        dx1 = dh_ref[0, :n] + dot_nt(dq, matrix(0))
        small_o[3:4, :] += col_sum(dx1 * n1)
        small_o[4:5, :] += col_sum(dx1)
        dh1 = norm_back(dx1, n1, r1, vec1_ref[3:4, :])
        small_o[2:3, :] += col_sum(dh1)
        dh[item, :n] = dh1
        box.send("dh", item)

    rows_of(chunks * CH)

    tail[1:2, :] += col_sum(dv[...])
    dvb = dv[...].astype(bf16)
    mt = m_ref[0].T
    acc[1] += dot(mt, dk[...])
    acc[2] += dot(mt, dvb)
    gm_o[0] = dot_nt(dk[...], matrix(1)) + dot_nt(dvb, matrix(2))

    @pl.when(last)
    def _():
        for m in range(4):
            out[m * 8 : (m + 1) * 8, :SQ, :] = acc[m].astype(bf16).reshape(8, SQ, D)
        ahead = jnp.concatenate([out[1:, :AHEAD, :], tail[:AHEAD, :].astype(bf16)[None]], 0)
        out[:, SQ:, :] = jnp.concatenate([ahead, jnp.zeros((PIECES, SQ_OUT - SQ - AHEAD, D), bf16)], 1)
        sent = []
        for index, who, ref, slot in each_piece(me, gn_o, gf_o):
            sent.append(pltpu.make_async_copy(out.at[who], ref.at[slot], p_sems.at[index]))
            sent[-1].start()
        box.close(2)
        for copy in sent:
            copy.wait()


def cross_backward(horizon, me, tau, dh2, h1, memory, shift, saved, w, vec1, small2):
    q, k, v, at, lse = saved
    items, steps, _ = h1.shape
    mem = memory.shape[1]
    row, grads = (items, steps, D), shape_of((HALF, SQ_OUT, D), bf16)
    memo, rows, cols = item_spec(mem, D), item_spec(steps, D), item_spec(D, steps)
    return call(
        functools.partial(cross_backward_kernel, chunks=steps // CH), "cross_backward", items, (horizon, me),
        [
            (tau, pl.BlockSpec(memory_space=pltpu.SMEM)), (dh2, rows), (h1, rows), (memory, memo), (shift, item_spec(1, mem)),
            (q, rows), (k, memo), (v, memo), (at, cols), (lse, item_spec(HEADS, steps)),
            (w, whole_spec(4 * D, D)), (vec1, whole_spec(8, D)), (small2, whole_spec(VEC, D)),
        ],
        [
            (shape_of(row, f32), any_spec()), (grads, any_spec()), (grads, any_spec()),
            (shape_of((items, mem, D), f32), memo), (shape_of((8, D), f32), whole_spec(8, D)),
        ],
        [
            vmem(4, D, D), vmem(VEC, D),
            vmem(steps, D, dtype=bf16), vmem(D, steps, dtype=bf16), vmem(D, steps, dtype=bf16), vmem(D, mem, dtype=bf16),
            vmem(D, steps, dtype=bf16), vmem(mem, D, dtype=bf16), vmem(mem, D), vmem(*row), vmem(PIECES, SQ_OUT, D, dtype=bf16),
            pltpu.SemaphoreType.DMA((2, 1)), pltpu.SemaphoreType.DMA((PIECES,)),
        ],
        LIMITS[3], 8e9,
    )


def self_backward_kernel(
    horizon, me, tau, dh_ref, x_ref, q_ref, k_ref, v_ref, at_ref, lse_ref, w, small1_ref,
    gx_o, gn_o, gf_o,
    flat, acc, tail, da, dat, qt, kt, xt, dqt, dqsc, dksc, dvsc, gx, sems, *, chunks,
):
    item = pl.program_id(0)
    box = Outbox({"gx": (gx, gx_o)}, sems)

    @pl.when(item == 0)
    def _():
        acc[...] = jnp.zeros_like(acc)
        tail[...] = small1_ref[...]

    factor = tau[item] * ROOT
    scale = tau[item] * (LOG2E * ROOT)

    count = chunk_count(horizon, item, chunks)

    def rows_at(chunk):
        return pl.ds(pl.multiple_of(chunk * CH, CH), CH)

    def before(here):
        e1 = dh_ref[0, here].astype(bf16)
        acc[3] += dot(at_ref[0, :, here], e1)
        da[here] = dot_nt(e1, w[3 * D :]).astype(bf16)
        dat[:, here] = da[here].T
        qt[:, here] = q_ref[0, here].T
        kt[:, here] = k_ref[0, here].T
        xt[:, here] = x_ref[0, here].T

    def behind(here):
        dq = dqsc[here]
        dk = (dksc[here] * factor).astype(bf16)
        dv = dvsc[here]
        tail[0:1, :] += col_sum(dq.astype(f32))
        tail[1:2, :] += col_sum(dv)
        dv = dv.astype(bf16)
        gx[item, here] = dh_ref[0, here] + dot_nt(dq, w[:D]) + dot_nt(dk, w[D : 2 * D]) + dot_nt(dv, w[2 * D : 3 * D])
        acc[0] += dot(xt[:, here], dq)
        acc[1] += dot(xt[:, here], dk)
        acc[2] += dot(xt[:, here], dv)

    everything = slice(0, chunks * CH)
    for held in (dksc, dvsc, dqsc):
        held[...] = jnp.zeros_like(held)
    before(everything)

    @pl.loop(0, count)
    def _(chunk):
        here = rows_at(chunk)
        for at_chunk in range(chunks):

            @pl.when(chunk == at_chunk)
            def _(keys=(at_chunk + 1) * CH):
                @pl.loop(0, 2)
                def _(group):
                    places = []
                    for index in range(HEADS // 2):
                        start = group * (D // 2) + index // 2 * LANES
                        rows = pl.ds(pl.multiple_of(start + index % 2 * HW, HW), HW)
                        places.append((pl.ds(pl.multiple_of(start, LANES), LANES), rows))

                    def products(i):
                        lanes, rows = places[i]
                        return (
                            dot(k_ref[0, :keys, lanes], head_rhs(qt[rows, here], i)),
                            dot(v_ref[0, :keys, lanes], head_rhs(dat[rows, here], i)),
                        )

                    def weigh(i, raw):
                        lse = lse_ref[0, pl.ds(group * (HEADS // 2) + i, 1), here]
                        return causal_cut(jnp.exp2(raw * scale - lse), 0.0)

                    def finish(i, weights, g):
                        lanes, rows = places[i]
                        dqt[rows, :] = (dot(kt[rows, :keys], g) * factor).astype(bf16)
                        return dot(g, one_head(q_ref[0, here, lanes], i)), dot(weights, one_head(da[here, lanes], i))

                    def inner(i):
                        return head_inner(dat[places[i][1], here], at_ref[0, places[i][1], here])

                    parts = heads_back(HEADS // 2, products, weigh, inner, finish)
                    for i in range(0, HEADS // 2, 2):
                        lanes = places[i][0]
                        dksc[:keys, lanes] += parts[i][0] + parts[i + 1][0]
                        dvsc[:keys, lanes] += parts[i][1] + parts[i + 1][1]

        dqsc[here, :] = dqt[...].T

    behind(everything)
    box.send("gx", item)

    @pl.when(item == pl.num_programs(0) - 1)
    def _():
        store_shards(me, gn_o, gf_o, flat, acc, tail)
        box.close(2)


def self_backward(horizon, me, tau, dh1, x, saved, w, small1):
    q, k, v, at, lse = saved
    items, steps, _ = x.shape
    half, shard = HALF, SHARD_PAD
    row, grads = (items, steps, D), shape_of((half, shard, LANES), bf16)
    rows, cols = item_spec(steps, D), item_spec(D, steps)
    return call(
        functools.partial(self_backward_kernel, chunks=steps // CH), "self_backward", items, (horizon, me),
        [
            (tau, pl.BlockSpec(memory_space=pltpu.SMEM)), (dh1, rows), (x, rows), (q, rows), (k, rows), (v, rows), (at, cols),
            (lse, item_spec(HEADS, steps)), (w, whole_spec(4 * D, D)), (small1, whole_spec(8, D)),
        ],
        [(kept(*row, dtype=f32), any_spec()), (grads, whole_spec(half, shard, LANES)), (grads, whole_spec(half, shard, LANES))],
        [
            vmem(PIECES * SHARD_ROWS + 16, LANES), vmem(4, D, D), vmem(8, D),
            vmem(steps, D, dtype=bf16), vmem(D, steps, dtype=bf16), vmem(D, steps, dtype=bf16), vmem(D, steps, dtype=bf16),
            vmem(D, steps, dtype=bf16), vmem(D, CH, dtype=bf16), vmem(steps, D, dtype=bf16),
            vmem(steps, D), vmem(steps, D), vmem(*row), pltpu.SemaphoreType.DMA((2, 1)),
        ],
        LIMITS[4], 1.5e10,
    )


AXES = ("wide", "narrow")
ALONG_Z = (8, 16, 24)
WITHIN = (1, 4, 5)
DEPTH = 4
TAIL = 32


def after(value, event):
    return lax.optimization_barrier((value, event))[0]


def swap(rows, offset):
    return lax.ppermute(rows, AXES, [(i, i ^ offset) for i in range(PIECES)])


def from_device(rows, step):
    return lax.ppermute(rows, AXES, [((i + step) % PIECES, i) for i in range(PIECES)])


def line_round(piece):
    return [piece[None]] + [swap(piece[None], o) for o in ALONG_Z]


def plane_round(line):
    return [line] + [swap(line, o) for o in WITHIN]


def plane_scatter(mine):
    return mine[:1] + [swap(part, o) for part, o in zip(mine[1:], WITHIN)]


def line_scatter(line):
    return [line[:1]] + [swap(line[i : i + 1], o) for i, o in enumerate(ALONG_Z, 1)]


def add_up(parts):
    return sum(part.astype(f32) for part in parts)


def turned(rows, away):
    if away:
        return rows.reshape(IN, TILES, D).transpose(1, 0, 2).reshape(FR, D)
    return rows.reshape(TILES, IN, D).transpose(1, 0, 2).reshape(FR, D)


def raw_piece(shard):
    return jnp.pad(shard.reshape(-1, LANES), ((0, SHARD_PAD - SHARD_ROWS), (0, 0)))


def dense_piece(shard, who):
    rows = shard.reshape(-1, LANES)
    tail = rows[-TAIL:]
    joined = jnp.concatenate([from_device(tail, -1), rows])
    main = lax.dynamic_slice_in_dim(joined, TAIL - who, rows.shape[0] - 1).reshape(FR, D)
    main = jnp.where(who < HALF, turned(main, True), main)
    return jnp.pad(jnp.concatenate([main, tail.reshape(VEC // 2, D)]), ((0, VEC // 2), (0, 0)))


def rest_shards(rest, who):
    cross, dense = rest[: SQ + AHEAD], rest[SQ + AHEAD :]
    main = jnp.where(who < HALF, turned(dense[:FR], False), dense[:FR])
    dense = jnp.concatenate([main, dense[FR:]])
    return [
        lax.dynamic_slice_in_dim(rows.reshape(-1, LANES), who, (rows.shape[0] - AHEAD) * D // LANES + 1).reshape(-1)
        for rows in (cross, dense)
    ]


def quarters(near, far, rows):
    return [
        add_up([near[i : i + DEPTH, :rows], far[i : i + DEPTH, :rows]]).astype(bf16) for i in range(0, HALF, DEPTH)
    ]


def body(inputs, memory, tau_scale, delta_shift, horizon, self_params, cross_params, dense_params, cotangent):
    who = lax.axis_index(AXES).astype(jnp.int32)
    me = who[None]
    x, m, ct = inputs[:, 0], memory[:, 0], cotangent[:, 0]
    tau, shift, horizon = tau_scale[:, 0], delta_shift, horizon[:, 0]

    line_both = jnp.concatenate(line_round(jnp.concatenate([raw_piece(self_params), raw_piece(cross_params)])))
    line_dense = line_round(dense_piece(dense_params, who))
    near_both = jnp.concatenate(after(plane_round(line_both), line_dense))
    p_both = near_both, swap(near_both, CORE)
    plane_dense = plane_round(jnp.concatenate(after(line_dense, near_both)))
    q, k, v, at, h1, w1, q2, at2, h2, w2, k2, v2, lse, lse2, vec1, vec2 = attention_forward(
        horizon, me, tau, x, m, shift, p_both
    )
    near_dense = jnp.concatenate(after(plane_dense, vec2))
    p_dense = near_dense, swap(near_dense, CORE)
    y, dh2, gn_dense, gf_dense, small2 = dense_both(horizon, me, h2, ct, vec2, p_dense)
    other_dense = swap(gf_dense, CORE)
    dh1, gn_cross, gf_cross, gm, small1 = cross_backward(
        horizon, me, tau, after(dh2, gf_dense), h1, m, shift, (q2, k2, v2, at2, lse2), w2, vec1, small2
    )
    other_cross = swap(gf_cross, CORE)
    other_dense = after(other_dense, small1)
    mine_rest = [
        jnp.concatenate(pair, 1) for pair in zip(quarters(gn_cross, other_cross, SQ + AHEAD), quarters(gn_dense, other_dense, FR + AHEAD))
    ]
    plane_rest = plane_scatter(mine_rest)
    gx, gn_self, gf_self = self_backward(
        horizon, me, tau, after(dh1, mine_rest), x, (q, k, v, at, lse), w1, small1
    )
    plane_rest, gf_self = after((plane_rest, gf_self), gn_self)
    other_self = swap(gf_self, CORE)
    sum_rest = add_up(plane_rest).astype(bf16)
    line_rest = line_scatter(sum_rest)
    plane_self = plane_scatter(quarters(gn_self, after(other_self, sum_rest), SHARD_PAD))
    sum_self = add_up(plane_self).astype(bf16)
    line_self = line_scatter(sum_self)
    g_cross, g_dense = rest_shards(add_up(after(line_rest, line_self))[0], who)
    g_self = add_up(line_self)[0, :SHARD_ROWS].reshape(-1)
    return y[:, None], gx[:, None], gm[:, None], g_self, g_cross, g_dense


def general_body(inputs, memory, tau_scale, delta_shift, horizon, self_params, cross_params, dense_params, cotangent):
    x, m, ct = inputs[:, 0], memory[:, 0], cotangent[:, 0]
    tau, shift, horizon = tau_scale[:, 0], delta_shift, horizon[:, 0]
    me = jnp.zeros((1,), jnp.int32)
    near = jnp.array([slot_offset(slot) for slot in range(HALF)], jnp.int32)
    owners = jnp.concatenate([near, near ^ CORE])
    square, tall = 4 * D, 2 * FF
    flat = [lax.all_gather(v, AXES, axis=0, tiled=True) for v in (self_params, cross_params, dense_params)]
    raw = [v[: PIECES * SHARD_ROWS * LANES].reshape(PIECES, SHARD_ROWS, LANES) for v in flat[:2]]
    raw = jnp.concatenate([jnp.pad(v, ((0, 0), (0, SHARD_PAD - SHARD_ROWS), (0, 0))) for v in raw], 1)[owners]
    dense = flat[2][: (tall + VEC) * D].reshape(-1, D)
    parts = dense[:tall].reshape(PIECES, FR, D)
    parts = jnp.concatenate([jax.vmap(lambda rows: turned(rows, True))(parts[:HALF]), parts[HALF:]])
    parts = jnp.concatenate([parts, jnp.broadcast_to(dense[None, tall:], (PIECES, VEC, D))], 1)[owners]
    q, k, v, at, h1, w1, q2, at2, h2, w2, k2, v2, lse, lse2, vec1, vec2 = attention_forward(
        horizon, me, tau, x, m, shift, (raw[:HALF], raw[HALF:])
    )
    y, dh2, gn_dense, gf_dense, small2 = dense_both(horizon, me, h2, ct, vec2, (parts[:HALF], parts[HALF:]))
    dh1, gn_cross, gf_cross, gm, small1 = cross_backward(
        horizon, me, tau, dh2, h1, m, shift, (q2, k2, v2, at2, lse2), w2, vec1, small2
    )
    gx, gn_self, gf_self = self_backward(horizon, me, tau, dh1, x, (q, k, v, at, lse), w1, small1)

    def in_order(near_part, far_part):
        both = jnp.concatenate([near_part, far_part]).astype(f32)
        return jnp.zeros_like(both).at[owners].set(both)

    cross = in_order(gn_cross, gf_cross)
    dense = in_order(gn_dense, gf_dense)
    tall_part = jnp.concatenate([jax.vmap(lambda rows: turned(rows, False))(dense[:HALF, :FR]), dense[HALF:, :FR]])
    wholes = (
        in_order(gn_self, gf_self)[:, :SHARD_ROWS].reshape(-1),
        jnp.concatenate([cross[:, :SQ].reshape(-1), cross[PIECES - 1, SQ : SQ + AHEAD].reshape(-1)]),
        jnp.concatenate([tall_part.reshape(-1), dense[PIECES - 1, FR : FR + AHEAD].reshape(-1)]),
    )
    sums = [
        lax.psum_scatter(jnp.pad(v, (0, f.shape[0] - v.shape[0])), AXES, scatter_dimension=0, tiled=True)
        for v, f in zip(wholes, flat)
    ]
    return y[:, None], gx[:, None], gm[:, None], *sums


def solution(mesh):
    items = P(None, AXES, None, None)
    placed = (items, items, P(None, AXES), P(None, AXES, None), P(None, AXES), P(AXES), P(AXES), P(AXES), items)
    fits = dict(mesh.shape) == {"wide": HALF, "narrow": 2}
    return jax.shard_map(
        body if fits else general_body,
        mesh=mesh, in_specs=placed, out_specs=(items, items, items, P(AXES), P(AXES), P(AXES)), check_vma=False,
    )
```

```python
import functools
import math

import jax
import jax.numpy as jnp
from jax import lax
from jax.experimental import pallas as pl
from jax.experimental.pallas import tpu as pltpu
from jax.sharding import PartitionSpec as P

D = 512
FF = 2048
HEADS = 8
HW = D // HEADS
LABEL = 48
LANES = 128
CH_BITS = 8
CH = 1 << CH_BITS
PIECES = 32
HALF = PIECES // 2
CORE = 2
SQ = 4 * D // PIECES
FR = 2 * FF // PIECES
IN = D // (PIECES // 2)
TILES = FF // D
VEC = 16
AHEAD = 8
SQ_OUT = SQ + 16
FR_OUT = FR + 16
SHARD_ROWS = 257
SHARD_PAD = (SHARD_ROWS + 15) // 16 * 16
SHARD_SENT = (SHARD_ROWS + 7) // 8 * 8
BOTH_ROWS = (2 * SHARD_ROWS + 15) // 16 * 16
EPS = 1e-05
NEG = -1e30
LOG2E = 1.4426950408889634
LIMITS = (40, 0, 48, 44, 46)
ROOT = 1.0 / math.sqrt(HW)
f32, bf16 = jnp.float32, jnp.bfloat16
MIB = 2**20


def dot(a, b):
    return jnp.dot(a, b, preferred_element_type=f32)


def dot_nt(a, b):
    return lax.dot_general(a, b, (((1,), (1,)), ((), ())), preferred_element_type=f32)


def norm_stats(h):
    center = h - jnp.mean(h, -1, keepdims=True)
    rstd = lax.rsqrt(jnp.mean(center * center, -1, keepdims=True) + EPS)
    return center * rstd, rstd


def norm_back(dz, n, rstd, gain):
    dn = dz * gain
    return rstd * (dn - jnp.mean(dn, -1, keepdims=True) - n * jnp.mean(dn * n, -1, keepdims=True))


def col_sum(v):
    return jnp.sum(v, 0, keepdims=True)


def slot_offset(slot):
    return ((slot & 3) << 3) | (((slot >> 3) & 1) << 2) | ((slot >> 2) & 1)


def each_piece(me, near, far):
    for slot in range(HALF):
        who = me[0] ^ slot_offset(slot)
        yield slot, who, near, slot
        yield HALF + slot, who ^ CORE, far, slot


def slot_of(me, who):
    away = me[0] ^ who
    return (((away >> 2) & 1) * 2 + (away & 1)) * 4 + (away >> 3), (away & CORE) != 0


def either(is_far, near_copy, far_copy):
    pl.when(jnp.logical_not(is_far))(near_copy.start)
    pl.when(is_far)(far_copy.start)


def load_shards(me, near, far, first, flat, w, vec):
    @pl.loop(0, HALF // 4)
    def _(turn):
        for slot in [turn * 4 + i for i in range(4)]:
            who = me[0] ^ slot_offset(slot)
            for ref, owner in ((near, who), (far, who ^ CORE)):
                flat[pl.ds(owner * SHARD_ROWS, SHARD_ROWS), :] = ref[slot, first : first + SHARD_ROWS, :].astype(f32)

    per = D // LANES
    for j in range(per):
        w[:, j * LANES : (j + 1) * LANES] = flat[pl.ds(j, 4 * D, stride=per), :].astype(bf16)
    vec[...] = jnp.zeros_like(vec)
    for i in range(5):
        for j in range(per):
            at = 4 * D * per + i * per + j
            vec[i : i + 1, j * LANES : (j + 1) * LANES] = flat[at : at + 1, :]


def store_shards(me, near, far, flat, acc, vec):
    per = D // LANES
    for m in range(4):
        for j in range(per):
            flat[pl.ds(m * D * per + j, D, stride=per), :] = acc[m, :, j * LANES : (j + 1) * LANES]
    start = 4 * D * per
    flat[start:, :] = jnp.zeros((flat.shape[0] - start, LANES), f32)
    for i in range(5):
        for j in range(per):
            flat[start + i * per + j : start + i * per + j + 1, :] = vec[i : i + 1, j * LANES : (j + 1) * LANES]
    rows = near.shape[1]

    @pl.loop(0, HALF)
    def _(slot):
        who = me[0] ^ slot_offset(slot)
        near[slot] = flat[pl.ds(who * SHARD_ROWS, rows), :].astype(bf16)
        far[slot] = flat[pl.ds((who ^ CORE) * SHARD_ROWS, rows), :].astype(bf16)


def head_rows(head):
    return slice(head * HW, (head + 1) * HW)


def pair_lanes(head):
    return slice(head // 2 * LANES, (head // 2 + 1) * LANES)


def head_rhs(block, head):
    zero = jnp.zeros_like(block)
    return jnp.concatenate([block, zero] if head % 2 == 0 else [zero, block], 0)


def one_head(rows, head):
    lane = lax.broadcasted_iota(jnp.int32, rows.shape, 1)
    return jnp.where((lane < HW) == (head % 2 == 0), rows, jnp.zeros_like(rows))


def causal_cut(scores, fill):
    keys = scores.shape[0]
    tail = scores[keys - CH :, :]
    key_at = lax.broadcasted_iota(jnp.int32, tail.shape, 0)
    query_at = lax.broadcasted_iota(jnp.int32, tail.shape, 1)
    tail = jnp.where(key_at <= query_at, tail, fill)
    return tail if keys == CH else jnp.concatenate([scores[: keys - CH, :], tail], 0)


def shift_column(shift_ref):
    row = shift_ref[0] * (LOG2E * ROOT)
    return jnp.broadcast_to(row, (8, row.shape[1])).T[:, :1]


def attend_heads(score, shape, values_t):
    following, waiting, out = score(0), None, []

    def finish(head, e, top, total):
        mixed = dot(values_t(head), e)
        out.append(((mixed * (1.0 / total)).astype(bf16), top + jnp.log2(total)))

    for head in range(HEADS):
        raw, following = following, score(head + 1) if head + 1 < HEADS else None
        if waiting is not None:
            finish(head - 1, *waiting)
        s = shape(raw)
        top = jnp.max(s, 0, keepdims=True)
        e = jnp.exp2(s - top)
        waiting = e.astype(bf16), top, jnp.sum(e, 0, keepdims=True)
    finish(HEADS - 1, *waiting)
    return out


def head_inner(da_t, a_t):
    return jnp.sum(da_t.astype(f32) * a_t.astype(f32), 0, keepdims=True)


def chunk_count(horizon, item, chunks):
    return jnp.minimum(lax.shift_right_logical(horizon[item] + (LABEL + CH - 1), CH_BITS), chunks)


class Outbox:
    def __init__(self, pairs, sems):
        self.pairs, self.sems = pairs, sems

    def copy(self, name, item):
        index = list(self.pairs).index(name)
        src, dst = self.pairs[name]
        return pltpu.make_async_copy(src.at[item], dst.at[item], self.sems.at[item, index])

    def send(self, name, item):
        self.copy(name, item).start()

    def close(self, items):
        for item in range(items):
            for name in self.pairs:
                self.copy(name, item).wait()


def vmem(*shape, dtype=f32):
    return pltpu.VMEM(shape, dtype)


def call(kernel, name, items, prefetch, ins, outs, scratch, limit, flops):
    return pl.pallas_call(
        kernel,
        grid_spec=pltpu.PrefetchScalarGridSpec(
            num_scalar_prefetch=len(prefetch),
            grid=(items,),
            in_specs=[spec for _, spec in ins],
            out_specs=[spec for _, spec in outs],
            scratch_shapes=scratch,
        ),
        out_shape=[shape for shape, _ in outs],
        compiler_params=pltpu.CompilerParams(vmem_limit_bytes=limit * MIB),
        cost_estimate=pl.CostEstimate(flops=int(flops), bytes_accessed=int(2e7), transcendentals=0),
        name=name,
    )(*prefetch, *[array for array, _ in ins])


def any_spec():
    return pl.BlockSpec(memory_space=pl.ANY)


def item_spec(*shape):
    return pl.BlockSpec((1, *shape), lambda i, *_: (i, *[0] * len(shape)))


def whole_spec(*shape):
    return pl.BlockSpec(shape, lambda i, *_: (0,) * len(shape), pipeline_mode=pl.Buffered(1))


def kept(*shape, dtype=bf16):
    return pltpu.HBM(shape, dtype)


shape_of = jax.ShapeDtypeStruct


def attention_forward_kernel(
    horizon, me, tau, x_ref, m_ref, shift_ref, pn_ref, pf_ref,
    q_o, k_o, v_o, at_o, h1_o, w1_o, q2_o, at2_o, h2_o, w2_o, k2_o, v2_o, lse_o, lse2_o, vec1_o, vec2_o,
    flat, w, w2, vt, qt, vt2, q, k, v, at, h1, q2, at2, h2, sems, w_sems, *, chunks,
):
    item = pl.program_id(0)
    box = Outbox(
        {
            "q": (q, q_o), "k": (k, k_o), "v": (v, v_o), "at": (at, at_o), "h1": (h1, h1_o),
            "q2": (q2, q2_o), "at2": (at2, at2_o), "h2": (h2, h2_o),
        },
        sems,
    )
    w_copies = [pltpu.make_async_copy(a, b, w_sems.at[i]) for i, (a, b) in enumerate(((w, w1_o), (w2, w2_o)))]

    @pl.when(item == 0)
    def _():
        load_shards(me, pn_ref, pf_ref, 0, flat, w, vec1_o)
        w_copies[0].start()
        load_shards(me, pn_ref, pf_ref, SHARD_ROWS, flat, w2, vec2_o)
        w_copies[1].start()

    k2_o[0] = dot(m_ref[0], w2[D : 2 * D]).astype(bf16)
    v2_o[0] = (dot(m_ref[0], w2[2 * D : 3 * D]) + vec2_o[1:2, :]).astype(bf16)
    vt2[...] = v2_o[0].T

    def rows_of(n):
        scale = tau[item] * (LOG2E * ROOT)
        x = x_ref[0, :n]
        q[item, :n] = (dot(x, w[:D]) + vec1_o[0:1, :]).astype(bf16)
        box.send("q", item)
        k[item, :n] = dot(x, w[D : 2 * D]).astype(bf16)
        box.send("k", item)
        v[item, :n] = (dot(x, w[2 * D : 3 * D]) + vec1_o[1:2, :]).astype(bf16)
        box.send("v", item)
        qt[:, :n] = q[item, :n].T
        vt[:, :n] = v[item, :n].T
        for start in range(0, n, CH):
            keys, here = start + CH, slice(start, start + CH)
            score = lambda head: dot(k[item, :keys, pair_lanes(head)], head_rhs(qt[head_rows(head), here], head))
            outs = attend_heads(
                score, lambda raw: causal_cut(raw * scale, NEG), lambda head: vt[head_rows(head), :keys]
            )
            for head, (mixed, total) in enumerate(outs):
                at[item, head_rows(head), here], lse_o[0, head : head + 1, here] = mixed, total
        box.send("at", item)
        hidden = x.astype(f32) + dot(at[item, :, :n].T, w[3 * D :]) + vec1_o[2:3, :]
        h1[item, :n] = hidden
        box.send("h1", item)

        shift = shift_column(shift_ref)
        n1, _ = norm_stats(hidden)
        x1 = n1 * vec1_o[3:4, :] + vec1_o[4:5, :]
        h2[item, :n] = x1
        q2[item, :n] = (dot(x1.astype(bf16), w2[:D]) + vec2_o[0:1, :]).astype(bf16)
        box.send("q2", item)
        qt[:, :n] = q2[item, :n].T
        score = lambda head: dot(k2_o[0, :, pair_lanes(head)], head_rhs(qt[head_rows(head), :n], head))
        outs = attend_heads(score, lambda raw: raw * scale + shift, lambda head: vt2[head_rows(head), :])
        for head, (mixed, total) in enumerate(outs):
            at2[item, head_rows(head), :n], lse2_o[0, head : head + 1, :n] = mixed, total
        box.send("at2", item)
        h2[item, :n] += dot(at2[item, :, :n].T, w2[3 * D :]) + vec2_o[2:3, :]
        box.send("h2", item)

    rows_of(chunks * CH)

    @pl.when(item == pl.num_programs(0) - 1)
    def _():
        box.close(2)
        for copy in w_copies:
            copy.wait()


def attention_forward(horizon, me, tau, x, memory, shift, params):
    items, steps, _ = x.shape
    mem = memory.shape[1]
    half, rows, _ = params[0].shape
    row, col = (items, steps, D), (items, D, steps)
    shards, memo, lses = whole_spec(half, rows, LANES), item_spec(mem, D), item_spec(HEADS, steps)
    saved = lambda *shape: (kept(*shape), any_spec())
    return call(
        functools.partial(attention_forward_kernel, chunks=steps // CH), "attention_forward", items, (horizon, me),
        [
            (tau, pl.BlockSpec(memory_space=pltpu.SMEM)), (x, item_spec(steps, D)), (memory, memo), (shift, item_spec(1, mem)),
            (params[0], shards), (params[1], shards),
        ],
        [
            saved(*row), saved(*row), saved(*row), saved(*col), (kept(*row, dtype=f32), any_spec()), saved(4 * D, D),
            saved(*row), saved(*col), (kept(*row, dtype=f32), any_spec()), saved(4 * D, D),
            (shape_of((items, mem, D), bf16), memo), (shape_of((items, mem, D), bf16), memo),
            (shape_of((items, HEADS, steps), f32), lses), (shape_of((items, HEADS, steps), f32), lses),
            (shape_of((8, D), f32), whole_spec(8, D)), (shape_of((8, D), f32), whole_spec(8, D)),
        ],
        [
            vmem(PIECES * SHARD_ROWS + 16, LANES), vmem(4 * D, D, dtype=bf16), vmem(4 * D, D, dtype=bf16),
            vmem(D, steps, dtype=bf16), vmem(D, steps, dtype=bf16), vmem(D, mem, dtype=bf16),
            vmem(*row, dtype=bf16), vmem(*row, dtype=bf16), vmem(*row, dtype=bf16), vmem(*col, dtype=bf16), vmem(*row),
            vmem(*row, dtype=bf16), vmem(*col, dtype=bf16), vmem(*row),
            pltpu.SemaphoreType.DMA((2, 8)), pltpu.SemaphoreType.DMA((2,)),
        ],
        LIMITS[0], 1.2e10,
    )


def dense_kernel(
    horizon, me, horizon_at, h_ref, ct_ref, vec2_ref, pn_ref, pf_ref, y_o, dh_o, gn_o, gf_o, small_o,
    w_in, w, vecb, vec_sc, bias, acc_in, acc_out, acc_bias, f_sc, gp_sc, y, dh, out, sems, p_sems, vec_sem, *, chunks,
):
    item = pl.program_id(0)
    box = Outbox({"y": (y, y_o), "dh": (dh, dh_o)}, sems)
    out_row, gain_row = 8 + TILES, 8 + TILES + 1
    vec = lambda i: vec_sc[i : i + 1, :]

    @pl.when(item == 0)
    def _():
        copies = [
            pltpu.make_async_copy(ref.at[slot, pl.ds(0, FR), :], w.at[who], p_sems.at[index])
            for index, who, ref, slot in each_piece(me, pn_ref, pf_ref)
        ]
        for copy in copies:
            copy.start()
        slot, is_far = slot_of(me, PIECES - 1)
        vec_copies = [
            pltpu.make_async_copy(ref.at[slot, pl.ds(FR, VEC), :], vecb, vec_sem) for ref in (pn_ref, pf_ref)
        ]
        either(is_far, *vec_copies)
        acc_in[...] = jnp.zeros_like(acc_in)
        acc_out[...] = jnp.zeros_like(acc_out)
        acc_bias[...] = jnp.zeros_like(acc_bias)
        small_o[...] = jnp.zeros_like(small_o)
        vec_copies[0].wait()
        vec_sc[...] = vecb[:8].astype(f32)
        for part in range(TILES):
            bias[:, part * D : (part + 1) * D] = vec(part)
        for copy in copies:
            copy.wait()
        for who in range(HALF):
            for part in range(TILES):
                w_in[who * IN : (who + 1) * IN, part * D : (part + 1) * D] = w[who, part * IN : (part + 1) * IN, :]

    w_out = lambda: w[HALF:].reshape(FF, D)

    def add(row, value):
        small_o[row : row + 1, :] += value

    y[item] = jnp.zeros(y.shape[1:], bf16)
    dh[item] = jnp.zeros(dh.shape[1:], f32)

    @pl.loop(0, chunk_count(horizon, item, chunks))
    def _(chunk):
        here = pl.ds(pl.multiple_of(chunk * CH, CH), CH)
        n2, r2 = norm_stats(h_ref[0, here])
        x2 = n2 * vec2_ref[3:4, :] + vec2_ref[4:5, :]
        x2b = x2.astype(bf16)
        u = dot(x2b, w_in[...]) + bias[...]
        cdf = 0.5 * (1.0 + lax.erf(u * 0.7071067811865476))
        f_sc[...] = (u * cdf).astype(bf16)
        gp_sc[...] = cdf + u * jnp.exp(u * u * -0.5) * (1.0 / math.sqrt(2.0 * math.pi))
        n3, r3 = norm_stats(x2 + dot(f_sc[...], w_out()) + vec(TILES))
        at = lax.broadcasted_iota(jnp.int32, (CH, 1), 0) + chunk * CH
        valid = (at < LABEL + horizon_at[item]).astype(f32)
        y[item, here] = ((n3 * vec(TILES + 1) + vec(TILES + 2)) * valid).astype(bf16)
        dy = ct_ref[0, here].astype(f32) * valid
        add(gain_row, col_sum(dy * n3))
        add(gain_row + 1, col_sum(dy))
        dh3 = norm_back(dy, n3, r3, vec(TILES + 1))
        add(out_row, col_sum(dh3))
        e3 = dh3.astype(bf16)
        acc_out[...] += dot(e3.T, f_sc[...])
        du = dot_nt(e3, w_out()) * gp_sc[...]
        acc_bias[...] += col_sum(du)
        eu = du.astype(bf16)
        acc_in[...] += dot(x2b.T, eu)
        dx2 = dh3 + dot_nt(eu, w_in[...])
        add(3, col_sum(dx2 * n2))
        add(4, col_sum(dx2))
        dh2 = norm_back(dx2, n2, r2, vec2_ref[3:4, :])
        add(2, col_sum(dh2))
        dh[item, here] = dh2

    box.send("y", item)
    box.send("dh", item)

    @pl.when(item == pl.num_programs(0) - 1)
    def _():
        for part in range(TILES):
            add(8 + part, acc_bias[:, part * D : (part + 1) * D])
        pad = jnp.zeros((FR_OUT - FR - AHEAD, D), bf16)
        ahead = small_o[8:, :].astype(bf16)
        for who in reversed(range(PIECES)):
            out[who, FR:, :] = jnp.concatenate([ahead, pad], 0)
            if who < HALF:
                for part in range(TILES):
                    out[who, part * IN : (part + 1) * IN, :] = acc_in[
                        who * IN : (who + 1) * IN, part * D : (part + 1) * D
                    ].astype(bf16)
                ahead = jnp.concatenate(
                    [acc_in[who * IN + i : who * IN + i + 1, part * D : (part + 1) * D] for i in range(2) for part in range(TILES)], 0
                ).astype(bf16)
            else:
                turn = acc_out[:, (who - HALF) * FR : (who - HALF + 1) * FR].astype(bf16).T
                out[who, :FR, :] = turn
                ahead = turn[:AHEAD]
            slot, is_far = slot_of(me, who)
            either(
                is_far,
                pltpu.make_async_copy(out.at[who], gn_o.at[slot], p_sems.at[who]),
                pltpu.make_async_copy(out.at[who], gf_o.at[slot], p_sems.at[who]),
            )
        box.close(2)
        for who in range(PIECES):
            pltpu.make_async_copy(out.at[who], gf_o.at[0], p_sems.at[who]).wait()


def dense_both(horizon, me, h2, ct, vec2, params):
    items, steps, _ = h2.shape
    row, grads = (items, steps, D), shape_of((HALF, FR_OUT, D), bf16)
    return call(
        functools.partial(dense_kernel, chunks=steps // CH), "dense_both", items, (horizon, me),
        [
            (horizon, pl.BlockSpec(memory_space=pltpu.SMEM)), (h2, item_spec(steps, D)), (ct, item_spec(steps, D)),
            (vec2, whole_spec(8, D)), (params[0], any_spec()), (params[1], any_spec()),
        ],
        [
            (kept(*row), any_spec()), (shape_of(row, f32), any_spec()), (grads, any_spec()), (grads, any_spec()),
            (shape_of((VEC, D), f32), whole_spec(VEC, D)),
        ],
        [
            vmem(D, FF, dtype=bf16), vmem(PIECES, FR, D, dtype=bf16), vmem(VEC, D, dtype=bf16), vmem(8, D), vmem(1, FF), vmem(D, FF), vmem(D, FF), vmem(1, FF),
            vmem(CH, FF, dtype=bf16), vmem(CH, FF),
            vmem(*row, dtype=bf16), vmem(*row), vmem(PIECES, FR_OUT, D, dtype=bf16), pltpu.SemaphoreType.DMA((2, 2)), pltpu.SemaphoreType.DMA((PIECES,)),
            pltpu.SemaphoreType.DMA,
        ],
        LIMITS[2], 2e10,
    )


def heads_back(count, products, weigh, inner, finish):
    following, waiting, out = products(0), None, []
    for i in range(count):
        (raw, dp), following = following, products(i + 1) if i + 1 < count else None
        if waiting is not None:
            out.append(finish(i - 1, *waiting))
        weights = weigh(i, raw)
        waiting = weights.astype(bf16), (weights * (dp - inner(i))).astype(bf16)
    out.append(finish(count - 1, *waiting))
    return out


def cross_backward_kernel(
    horizon, me, tau, dh_ref, h1_ref, m_ref, shift_ref, q_ref, k_ref, v_ref, at_ref, lse_ref, w, vec1_ref, small2_ref,
    dh_o, gn_o, gf_o, gm_o, small_o,
    acc, tail, da, dat, qt, kt, dqt, dk, dv, dh, out, sems, p_sems, *, chunks,
):
    item = pl.program_id(0)
    last = item == pl.num_programs(0) - 1
    box = Outbox({"dh": (dh, dh_o)}, sems)
    matrix = lambda m: w[m * D : (m + 1) * D]

    @pl.when(item == 0)
    def _():
        acc[...] = jnp.zeros_like(acc)
        tail[...] = small2_ref[...]
        small_o[...] = jnp.zeros_like(small_o)

    factor = tau[item] * ROOT
    kt[...] = k_ref[0].T

    def rows_of(n):
        scale = tau[item] * (LOG2E * ROOT)
        shift = shift_column(shift_ref)
        e2 = dh_ref[0, :n].astype(bf16)
        acc[3] += dot(at_ref[0, :, :n], e2)
        da[:n] = dot_nt(e2, matrix(3)).astype(bf16)
        dat[:, :n] = da[:n].T
        qt[:, :n] = q_ref[0, :n].T

        def products(head):
            lanes, rows = pair_lanes(head), head_rows(head)
            return (
                dot(k_ref[0, :, lanes], head_rhs(qt[rows, :n], head)),
                dot(v_ref[0, :, lanes], head_rhs(dat[rows, :n], head)),
            )

        def finish(head, weights, g):
            lanes, rows = pair_lanes(head), head_rows(head)
            dqt[rows, :n] = (dot(kt[rows, :], g) * factor).astype(bf16)
            return dot(g, one_head(q_ref[0, :n, lanes], head)), dot(weights, one_head(da[:n, lanes], head))

        parts = heads_back(
            HEADS, products,
            lambda head, raw: jnp.exp2(raw * scale + shift - lse_ref[0, head : head + 1, :n]),
            lambda head: head_inner(dat[head_rows(head), :n], at_ref[0, head_rows(head), :n]),
            finish,
        )
        for head in range(0, HEADS, 2):
            dk[:, pair_lanes(head)] = ((parts[head][0] + parts[head + 1][0]) * factor).astype(bf16)
            dv[:, pair_lanes(head)] = parts[head][1] + parts[head + 1][1]
        dq = dqt[:, :n].T
        tail[0:1, :] += col_sum(dq.astype(f32))
        n1, r1 = norm_stats(h1_ref[0, :n])
        x1b = (n1 * vec1_ref[3:4, :] + vec1_ref[4:5, :]).astype(bf16)
        acc[0] += dot(x1b.T, dq)
        dx1 = dh_ref[0, :n] + dot_nt(dq, matrix(0))
        small_o[3:4, :] += col_sum(dx1 * n1)
        small_o[4:5, :] += col_sum(dx1)
        dh1 = norm_back(dx1, n1, r1, vec1_ref[3:4, :])
        small_o[2:3, :] += col_sum(dh1)
        dh[item, :n] = dh1
        box.send("dh", item)

    rows_of(chunks * CH)

    tail[1:2, :] += col_sum(dv[...])
    dvb = dv[...].astype(bf16)
    mt = m_ref[0].T
    acc[1] += dot(mt, dk[...])
    acc[2] += dot(mt, dvb)
    gm_o[0] = dot_nt(dk[...], matrix(1)) + dot_nt(dvb, matrix(2))

    @pl.when(last)
    def _():
        for m in range(4):
            out[m * 8 : (m + 1) * 8, :SQ, :] = acc[m].astype(bf16).reshape(8, SQ, D)
        ahead = jnp.concatenate([out[1:, :AHEAD, :], tail[:AHEAD, :].astype(bf16)[None]], 0)
        out[:, SQ:, :] = jnp.concatenate([ahead, jnp.zeros((PIECES, SQ_OUT - SQ - AHEAD, D), bf16)], 1)
        sent = []
        for index, who, ref, slot in each_piece(me, gn_o, gf_o):
            sent.append(pltpu.make_async_copy(out.at[who], ref.at[slot], p_sems.at[index]))
            sent[-1].start()
        box.close(2)
        for copy in sent:
            copy.wait()


def cross_backward(horizon, me, tau, dh2, h1, memory, shift, saved, w, vec1, small2):
    q, k, v, at, lse = saved
    items, steps, _ = h1.shape
    mem = memory.shape[1]
    row, grads = (items, steps, D), shape_of((HALF, SQ_OUT, D), bf16)
    memo, rows, cols = item_spec(mem, D), item_spec(steps, D), item_spec(D, steps)
    return call(
        functools.partial(cross_backward_kernel, chunks=steps // CH), "cross_backward", items, (horizon, me),
        [
            (tau, pl.BlockSpec(memory_space=pltpu.SMEM)), (dh2, rows), (h1, rows), (memory, memo), (shift, item_spec(1, mem)),
            (q, rows), (k, memo), (v, memo), (at, cols), (lse, item_spec(HEADS, steps)),
            (w, whole_spec(4 * D, D)), (vec1, whole_spec(8, D)), (small2, whole_spec(VEC, D)),
        ],
        [
            (shape_of(row, f32), any_spec()), (grads, any_spec()), (grads, any_spec()),
            (shape_of((items, mem, D), f32), memo), (shape_of((8, D), f32), whole_spec(8, D)),
        ],
        [
            vmem(4, D, D), vmem(VEC, D),
            vmem(steps, D, dtype=bf16), vmem(D, steps, dtype=bf16), vmem(D, steps, dtype=bf16), vmem(D, mem, dtype=bf16),
            vmem(D, steps, dtype=bf16), vmem(mem, D, dtype=bf16), vmem(mem, D), vmem(*row), vmem(PIECES, SQ_OUT, D, dtype=bf16),
            pltpu.SemaphoreType.DMA((2, 1)), pltpu.SemaphoreType.DMA((PIECES,)),
        ],
        LIMITS[3], 8e9,
    )


def self_backward_kernel(
    horizon, me, tau, dh_ref, x_ref, q_ref, k_ref, v_ref, at_ref, lse_ref, w, small1_ref,
    gx_o, gn_o, gf_o,
    flat, acc, tail, da, dat, qt, kt, xt, dqt, dqsc, dksc, dvsc, gx, sems, *, chunks,
):
    item = pl.program_id(0)
    box = Outbox({"gx": (gx, gx_o)}, sems)

    @pl.when(item == 0)
    def _():
        acc[...] = jnp.zeros_like(acc)
        tail[...] = small1_ref[...]

    factor = tau[item] * ROOT
    scale = tau[item] * (LOG2E * ROOT)

    count = chunk_count(horizon, item, chunks)

    def rows_at(chunk):
        return pl.ds(pl.multiple_of(chunk * CH, CH), CH)

    def before(here):
        e1 = dh_ref[0, here].astype(bf16)
        acc[3] += dot(at_ref[0, :, here], e1)
        da[here] = dot_nt(e1, w[3 * D :]).astype(bf16)
        dat[:, here] = da[here].T
        qt[:, here] = q_ref[0, here].T
        kt[:, here] = k_ref[0, here].T
        xt[:, here] = x_ref[0, here].T

    def behind(here):
        dq = dqsc[here]
        dk = (dksc[here] * factor).astype(bf16)
        dv = dvsc[here]
        tail[0:1, :] += col_sum(dq.astype(f32))
        tail[1:2, :] += col_sum(dv)
        dv = dv.astype(bf16)
        gx[item, here] = dh_ref[0, here] + dot_nt(dq, w[:D]) + dot_nt(dk, w[D : 2 * D]) + dot_nt(dv, w[2 * D : 3 * D])
        acc[0] += dot(xt[:, here], dq)
        acc[1] += dot(xt[:, here], dk)
        acc[2] += dot(xt[:, here], dv)

    everything = slice(0, chunks * CH)
    for held in (dksc, dvsc, dqsc):
        held[...] = jnp.zeros_like(held)
    before(everything)

    @pl.loop(0, count)
    def _(chunk):
        here = rows_at(chunk)
        for at_chunk in range(chunks):

            @pl.when(chunk == at_chunk)
            def _(keys=(at_chunk + 1) * CH):
                @pl.loop(0, 2)
                def _(group):
                    places = []
                    for index in range(HEADS // 2):
                        start = group * (D // 2) + index // 2 * LANES
                        rows = pl.ds(pl.multiple_of(start + index % 2 * HW, HW), HW)
                        places.append((pl.ds(pl.multiple_of(start, LANES), LANES), rows))

                    def products(i):
                        lanes, rows = places[i]
                        return (
                            dot(k_ref[0, :keys, lanes], head_rhs(qt[rows, here], i)),
                            dot(v_ref[0, :keys, lanes], head_rhs(dat[rows, here], i)),
                        )

                    def weigh(i, raw):
                        lse = lse_ref[0, pl.ds(group * (HEADS // 2) + i, 1), here]
                        return causal_cut(jnp.exp2(raw * scale - lse), 0.0)

                    def finish(i, weights, g):
                        lanes, rows = places[i]
                        dqt[rows, :] = (dot(kt[rows, :keys], g) * factor).astype(bf16)
                        return dot(g, one_head(q_ref[0, here, lanes], i)), dot(weights, one_head(da[here, lanes], i))

                    def inner(i):
                        return head_inner(dat[places[i][1], here], at_ref[0, places[i][1], here])

                    parts = heads_back(HEADS // 2, products, weigh, inner, finish)
                    for i in range(0, HEADS // 2, 2):
                        lanes = places[i][0]
                        dksc[:keys, lanes] += parts[i][0] + parts[i + 1][0]
                        dvsc[:keys, lanes] += parts[i][1] + parts[i + 1][1]

        dqsc[here, :] = dqt[...].T

    behind(everything)
    box.send("gx", item)

    @pl.when(item == pl.num_programs(0) - 1)
    def _():
        store_shards(me, gn_o, gf_o, flat, acc, tail)
        box.close(2)


def self_backward(horizon, me, tau, dh1, x, saved, w, small1):
    q, k, v, at, lse = saved
    items, steps, _ = x.shape
    half, shard = HALF, SHARD_PAD
    row, grads = (items, steps, D), shape_of((half, shard, LANES), bf16)
    rows, cols = item_spec(steps, D), item_spec(D, steps)
    return call(
        functools.partial(self_backward_kernel, chunks=steps // CH), "self_backward", items, (horizon, me),
        [
            (tau, pl.BlockSpec(memory_space=pltpu.SMEM)), (dh1, rows), (x, rows), (q, rows), (k, rows), (v, rows), (at, cols),
            (lse, item_spec(HEADS, steps)), (w, whole_spec(4 * D, D)), (small1, whole_spec(8, D)),
        ],
        [(kept(*row, dtype=f32), any_spec()), (grads, whole_spec(half, shard, LANES)), (grads, whole_spec(half, shard, LANES))],
        [
            vmem(PIECES * SHARD_ROWS + 16, LANES), vmem(4, D, D), vmem(8, D),
            vmem(steps, D, dtype=bf16), vmem(D, steps, dtype=bf16), vmem(D, steps, dtype=bf16), vmem(D, steps, dtype=bf16),
            vmem(D, steps, dtype=bf16), vmem(D, CH, dtype=bf16), vmem(steps, D, dtype=bf16),
            vmem(steps, D), vmem(steps, D), vmem(*row), pltpu.SemaphoreType.DMA((2, 1)),
        ],
        LIMITS[4], 1.5e10,
    )


AXES = ("wide", "narrow")
ALONG_Z = (8, 16, 24)
WITHIN = (1, 4, 5)
DEPTH = 4
TAIL = 32


def after(value, event):
    return lax.optimization_barrier((value, event))[0]


def swap(rows, offset):
    return lax.ppermute(rows, AXES, [(i, i ^ offset) for i in range(PIECES)])


def from_device(rows, step):
    return lax.ppermute(rows, AXES, [((i + step) % PIECES, i) for i in range(PIECES)])


def line_round(piece):
    return [piece[None]] + [swap(piece[None], o) for o in ALONG_Z]


def plane_round(line):
    return [line] + [swap(line, o) for o in WITHIN]


def plane_scatter(mine):
    return mine[:1] + [swap(part, o) for part, o in zip(mine[1:], WITHIN)]


def line_scatter(line):
    return [line[:1]] + [swap(line[i : i + 1], o) for i, o in enumerate(ALONG_Z, 1)]


def add_up(parts):
    return sum(part.astype(f32) for part in parts)


def turned(rows, away):
    if away:
        return rows.reshape(IN, TILES, D).transpose(1, 0, 2).reshape(FR, D)
    return rows.reshape(TILES, IN, D).transpose(1, 0, 2).reshape(FR, D)


def raw_piece(first, second):
    rows = jnp.concatenate([first.reshape(-1, LANES), second.reshape(-1, LANES)])
    return jnp.pad(rows, ((0, BOTH_ROWS - 2 * SHARD_ROWS), (0, 0)))


def dense_piece(shard, who):
    rows = shard.reshape(-1, LANES)
    tail = rows[-TAIL:]
    joined = jnp.concatenate([from_device(tail, -1), rows])
    main = lax.dynamic_slice_in_dim(joined, TAIL - who, rows.shape[0] - 1).reshape(FR, D)
    main = jnp.where(who < HALF, turned(main, True), main)
    return jnp.pad(jnp.concatenate([main, tail.reshape(VEC // 2, D)]), ((0, VEC // 2), (0, 0)))


def rest_shards(rest, who):
    cross, dense = rest[: SQ + AHEAD], rest[SQ + AHEAD :]
    main = jnp.where(who < HALF, turned(dense[:FR], False), dense[:FR])
    dense = jnp.concatenate([main, dense[FR:]])
    return [
        lax.dynamic_slice_in_dim(rows.reshape(-1, LANES), who, (rows.shape[0] - AHEAD) * D // LANES + 1).reshape(-1)
        for rows in (cross, dense)
    ]


def quarters(near, far, rows):
    return [
        add_up([near[i : i + DEPTH, :rows], far[i : i + DEPTH, :rows]]).astype(bf16) for i in range(0, HALF, DEPTH)
    ]


def body(inputs, memory, tau_scale, delta_shift, horizon, self_params, cross_params, dense_params, cotangent):
    who = lax.axis_index(AXES).astype(jnp.int32)
    me = who[None]
    x, m, ct = inputs[:, 0], memory[:, 0], cotangent[:, 0]
    tau, shift, horizon = tau_scale[:, 0], delta_shift, horizon[:, 0]

    line_both = jnp.concatenate(line_round(raw_piece(self_params, cross_params)))
    line_dense = line_round(dense_piece(dense_params, who))
    near_both = jnp.concatenate(after(plane_round(line_both), line_dense))
    p_both = near_both, swap(near_both, CORE)
    plane_dense = plane_round(jnp.concatenate(after(line_dense, near_both)))
    q, k, v, at, h1, w1, q2, at2, h2, w2, k2, v2, lse, lse2, vec1, vec2 = attention_forward(
        horizon, me, tau, x, m, shift, p_both
    )
    near_dense = jnp.concatenate(after(plane_dense, vec2))
    p_dense = near_dense, swap(near_dense, CORE)
    y, dh2, gn_dense, gf_dense, small2 = dense_both(horizon, me, h2, ct, vec2, p_dense)
    other_dense = swap(gf_dense, CORE)
    dh1, gn_cross, gf_cross, gm, small1 = cross_backward(
        horizon, me, tau, after(dh2, gf_dense), h1, m, shift, (q2, k2, v2, at2, lse2), w2, vec1, small2
    )
    other_cross = swap(gf_cross, CORE)
    other_dense = after(other_dense, small1)
    mine_rest = [
        jnp.concatenate(pair, 1) for pair in zip(quarters(gn_cross, other_cross, SQ + AHEAD), quarters(gn_dense, other_dense, FR + AHEAD))
    ]
    plane_rest = plane_scatter(mine_rest)
    gx, gn_self, gf_self = self_backward(
        horizon, me, tau, after(dh1, mine_rest), x, (q, k, v, at, lse), w1, small1
    )
    plane_rest, gf_self = after((plane_rest, gf_self), gn_self)
    other_self = swap(gf_self, CORE)
    sum_rest = add_up(plane_rest).astype(bf16)
    line_rest = line_scatter(sum_rest)
    plane_self = plane_scatter(quarters(gn_self, after(other_self, sum_rest), SHARD_SENT))
    sum_self = add_up(plane_self).astype(bf16)
    line_self = line_scatter(sum_self)
    g_cross, g_dense = rest_shards(add_up(after(line_rest, line_self))[0], who)
    g_self = add_up(line_self)[0, :SHARD_ROWS].reshape(-1)
    return y[:, None], gx[:, None], gm[:, None], g_self, g_cross, g_dense


def general_body(inputs, memory, tau_scale, delta_shift, horizon, self_params, cross_params, dense_params, cotangent):
    x, m, ct = inputs[:, 0], memory[:, 0], cotangent[:, 0]
    tau, shift, horizon = tau_scale[:, 0], delta_shift, horizon[:, 0]
    me = jnp.zeros((1,), jnp.int32)
    near = jnp.array([slot_offset(slot) for slot in range(HALF)], jnp.int32)
    owners = jnp.concatenate([near, near ^ CORE])
    square, tall = 4 * D, 2 * FF
    flat = [lax.all_gather(v, AXES, axis=0, tiled=True) for v in (self_params, cross_params, dense_params)]
    raw = [v[: PIECES * SHARD_ROWS * LANES].reshape(PIECES, SHARD_ROWS, LANES) for v in flat[:2]]
    raw = jnp.pad(jnp.concatenate(raw, 1), ((0, 0), (0, BOTH_ROWS - 2 * SHARD_ROWS), (0, 0)))[owners]
    dense = flat[2][: (tall + VEC) * D].reshape(-1, D)
    parts = dense[:tall].reshape(PIECES, FR, D)
    parts = jnp.concatenate([jax.vmap(lambda rows: turned(rows, True))(parts[:HALF]), parts[HALF:]])
    parts = jnp.concatenate([parts, jnp.broadcast_to(dense[None, tall:], (PIECES, VEC, D))], 1)[owners]
    q, k, v, at, h1, w1, q2, at2, h2, w2, k2, v2, lse, lse2, vec1, vec2 = attention_forward(
        horizon, me, tau, x, m, shift, (raw[:HALF], raw[HALF:])
    )
    y, dh2, gn_dense, gf_dense, small2 = dense_both(horizon, me, h2, ct, vec2, (parts[:HALF], parts[HALF:]))
    dh1, gn_cross, gf_cross, gm, small1 = cross_backward(
        horizon, me, tau, dh2, h1, m, shift, (q2, k2, v2, at2, lse2), w2, vec1, small2
    )
    gx, gn_self, gf_self = self_backward(horizon, me, tau, dh1, x, (q, k, v, at, lse), w1, small1)

    def in_order(near_part, far_part):
        both = jnp.concatenate([near_part, far_part]).astype(f32)
        return jnp.zeros_like(both).at[owners].set(both)

    cross = in_order(gn_cross, gf_cross)
    dense = in_order(gn_dense, gf_dense)
    tall_part = jnp.concatenate([jax.vmap(lambda rows: turned(rows, False))(dense[:HALF, :FR]), dense[HALF:, :FR]])
    wholes = (
        in_order(gn_self, gf_self)[:, :SHARD_ROWS].reshape(-1),
        jnp.concatenate([cross[:, :SQ].reshape(-1), cross[PIECES - 1, SQ : SQ + AHEAD].reshape(-1)]),
        jnp.concatenate([tall_part.reshape(-1), dense[PIECES - 1, FR : FR + AHEAD].reshape(-1)]),
    )
    sums = [
        lax.psum_scatter(jnp.pad(v, (0, f.shape[0] - v.shape[0])), AXES, scatter_dimension=0, tiled=True)
        for v, f in zip(wholes, flat)
    ]
    return y[:, None], gx[:, None], gm[:, None], *sums


def solution(mesh):
    items = P(None, AXES, None, None)
    placed = (items, items, P(None, AXES), P(None, AXES, None), P(None, AXES), P(AXES), P(AXES), P(AXES), items)
    fits = dict(mesh.shape) == {"wide": HALF, "narrow": 2}
    return jax.shard_map(
        body if fits else general_body,
        mesh=mesh, in_specs=placed, out_specs=(items, items, items, P(AXES), P(AXES), P(AXES)), check_vma=False,
    )
```
